32 devices in a mesh: dp: 16 (over z, y, core), tensor: 2 (over x).
Axes of the slice: x: 2, y: 2, z: 4, core: 2. Of those that a mesh axis runs over, the one named last changes fastest.
Arguments:
- cot_student: bfloat16 [16384, 2432], P(('dp', 'tensor')), may hold values from -32 to 32
- cot_fake: bfloat16 [16384, 2432], P(('dp', 'tensor')), may hold values from -32 to 32
- act_student: bfloat16 [1216, 16384], P('tensor', 'dp'), may hold values from -5 to 5
- act_fake: bfloat16 [1216, 16384], P('tensor', 'dp'), may hold values from -5 to 5
- weight_student: bfloat16 [1216, 2432], P('tensor'), may hold values from -0.125 to 0.125
- weight_fake: bfloat16 [1216, 2432], P('tensor'), may hold values from -0.125 to 0.125
- master_student: float32 [1216, 2432], P('tensor', 'dp'), may hold values from -0.15625 to 0.15625
- first_student: float32 [1216, 2432], P('tensor', 'dp'), may hold values from -6 to 6
- second_student: float32 [1216, 2432], P('tensor', 'dp'), may hold values from 0.25 to 4
- master_fake: float32 [1216, 2432], P('tensor', 'dp'), may hold values from -0.15625 to 0.15625
- first_fake: float32 [1216, 2432], P('tensor', 'dp'), may hold values from -6 to 6
- second_fake: float32 [1216, 2432], P('tensor', 'dp'), may hold values from 0.25 to 4
- timesteps: int32 [16, 2, 1], P('dp'), may hold values from 0 to 999
Outputs:
- back_student: bfloat16 [1216, 16384], P('tensor', 'dp')
- back_fake: bfloat16 [1216, 16384], P('tensor', 'dp')
- new_master_student: float32 [1216, 2432], P('tensor', 'dp')
- new_first_student: float32 [1216, 2432], P('tensor', 'dp')
- new_second_student: float32 [1216, 2432], P('tensor', 'dp')
- new_master_fake: float32 [1216, 2432], P('tensor', 'dp')
- new_first_fake: float32 [1216, 2432], P('tensor', 'dp')
- new_second_fake: float32 [1216, 2432], P('tensor', 'dp')
- params_student: bfloat16 [1216, 2432], P('tensor')
- params_fake: bfloat16 [1216, 2432], P('tensor')
The draws below stay inside these ranges and needn't reach their ends.
All inputs are finite; a program needn't handle non-finite values.
Results may differ from the reference program's by a relative error of at most 0.0011.
Values may be sent and summed in bfloat16 or wider, within the bound.
No kernel may reach another device: no remote copies, remote signals or barrier semaphores. Data moves between devices by JAX's collectives and lax.ppermute only.
A program may use at most 128 MiB of HBM per device.

```python
import math
import jax
import jax.numpy as jnp

D = 2432
F = 1216
ROWS = 1024
SAMPLES = 1
TOK = 1024
ALL_ROWS = 16384
N_DP = 16


def shared_signs(key, salt):
    return jax.random.rademacher(jax.random.fold_in(key, salt), (ALL_ROWS,), dtype=jnp.float32)


def pairing_boost(key):
    devices = ALL_ROWS // TOK
    width_block = D // devices
    pairing = jax.random.permutation(key, devices)
    paired = pairing[jnp.arange(ALL_ROWS) // TOK]
    return jnp.where(paired[:, None] == (jnp.arange(D) // width_block)[None, :], 3.0, 1.0)


def draw_act_student(key, part):
    row_sign = shared_signs(key, 101)
    key = jax.random.fold_in(key, 1)
    key_jitter, key_dir = jax.random.split(key)
    direction = jax.random.truncated_normal(key_dir, -3.0, 3.0, (F,), jnp.float32)
    jitter = jax.random.truncated_normal(key_jitter, -4.0, 4.0, (F, ALL_ROWS), jnp.float32)
    return (jitter + 0.2 * direction[:, None] * row_sign[None, :]).astype(jnp.bfloat16)


def draw_cot_student(key, part):
    row_sign = shared_signs(key, 101)
    key = jax.random.fold_in(key, 2)
    key_jitter, key_dir, key_pair = jax.random.split(key, 3)
    direction = jax.random.truncated_normal(key_dir, -3.0, 3.0, (D,), jnp.float32)
    boost = pairing_boost(key_pair)
    jitter = jax.random.truncated_normal(key_jitter, -4.0, 4.0, (ALL_ROWS, D), jnp.float32)
    return (jitter * boost + 0.2 * row_sign[:, None] * direction[None, :]).astype(jnp.bfloat16)


def draw_act_fake(key, part):
    row_sign = shared_signs(key, 202)
    key = jax.random.fold_in(key, 3)
    key_jitter, key_dir = jax.random.split(key)
    direction = jax.random.truncated_normal(key_dir, -3.0, 3.0, (F,), jnp.float32)
    jitter = jax.random.truncated_normal(key_jitter, -4.0, 4.0, (F, ALL_ROWS), jnp.float32)
    return (jitter + 0.2 * direction[:, None] * row_sign[None, :]).astype(jnp.bfloat16)


def draw_cot_fake(key, part):
    row_sign = shared_signs(key, 202)
    key = jax.random.fold_in(key, 4)
    key_jitter, key_dir, key_pair = jax.random.split(key, 3)
    direction = jax.random.truncated_normal(key_dir, -3.0, 3.0, (D,), jnp.float32)
    boost = pairing_boost(key_pair)
    jitter = jax.random.truncated_normal(key_jitter, -4.0, 4.0, (ALL_ROWS, D), jnp.float32)
    return (jitter * boost + 0.2 * row_sign[:, None] * direction[None, :]).astype(jnp.bfloat16)


def place_ends(entries, stream_key, low, largest):
    longest = entries.shape.index(max(entries.shape))
    spots = []
    for shift in (0, 1):
        where = [jax.random.randint(jax.random.fold_in(stream_key, axis), (), 0, length) for axis, length in enumerate(entries.shape)]
        where[longest] = (where[longest] + shift) % entries.shape[longest]
        spots.append(tuple(where))
    return entries.at[spots[0]].set(low).at[spots[1]].set(largest)


def shard_levels(key, dims, pieces, low, largest):
    gain, own = 1.0, jax.random.fold_in(key, 6)
    for dim, parts in pieces:
        heights = jnp.exp(jax.random.uniform(jax.random.fold_in(own, dim), (parts,), jnp.float32, low / len(pieces), largest / len(pieces)))
        gain = gain * jnp.repeat(heights, dims[dim] // parts).reshape([-1 if axis == dim else 1 for axis in range(len(dims))])
    return gain


def gaussian(rng, dims, scale, reach, shards=(), kind=jnp.bfloat16):
    values = scale * jax.random.normal(rng, dims, jnp.float32)
    if shards:
        values = values * shard_levels(rng, dims, shards, -0.22, 0.18)
    return jnp.clip(values, -reach, reach).astype(kind)


def setup_inputs(seed: int = 0) -> dict:
    streams_of = jax.random.split(jax.random.key(seed), 14)
    cot_student = draw_cot_student(jax.random.fold_in(streams_of[13], 71), 0)
    cot_fake = draw_cot_fake(jax.random.fold_in(streams_of[13], 71), 0)
    act_student = draw_act_student(jax.random.fold_in(streams_of[13], 71), 0)
    act_fake = draw_act_fake(jax.random.fold_in(streams_of[13], 71), 0)
    weight_student = gaussian(streams_of[4], (F, D), D ** -0.5, 0.125, ((0, 2),))
    weight_fake = gaussian(streams_of[5], (F, D), D ** -0.5, 0.125, ((0, 2),))
    master_student = gaussian(streams_of[6], (F, D), F ** -0.5, 0.15625, ((0, 2), (1, 16)), jnp.float32)
    first_student = gaussian(streams_of[7], (F, D), 1.0, 6.0, ((0, 2), (1, 16)), jnp.float32)
    second_student = jnp.clip(jnp.exp(math.log(4.0) - 2.7725887 * jax.random.uniform(streams_of[8], (F, D), jnp.float32) ** shard_levels(streams_of[8], (F, D), ((0, 2), (1, 16)), -0.2, 0.2)), 0.25, 4.0)
    master_fake = gaussian(streams_of[9], (F, D), F ** -0.5, 0.15625, ((0, 2), (1, 16)), jnp.float32)
    first_fake = gaussian(streams_of[10], (F, D), 1.0, 6.0, ((0, 2), (1, 16)), jnp.float32)
    second_fake = jnp.clip(jnp.exp(math.log(4.0) - 2.7725887 * jax.random.uniform(streams_of[11], (F, D), jnp.float32) ** shard_levels(streams_of[11], (F, D), ((0, 2), (1, 16)), -0.2, 0.2)), 0.25, 4.0)
    timesteps = place_ends(jax.random.randint(streams_of[12], (N_DP, 2, SAMPLES), 0, 1000), jax.random.fold_in(streams_of[12], 1), 0, 999).astype(jnp.int32)
    return {"cot_student": cot_student, "cot_fake": cot_fake, "act_student": act_student, "act_fake": act_fake, "weight_student": weight_student, "weight_fake": weight_fake, "master_student": master_student, "first_student": first_student, "second_student": second_student, "master_fake": master_fake, "first_fake": first_fake, "second_fake": second_fake, "timesteps": timesteps}


FIRST_CORRECTION = 0.9999734386011124
SECOND_CORRECTION = 0.0952078529183

def row_scale(steps_net):
    weights = 1.0 / (0.1 + steps_net.astype(jnp.float32) / 1000.0)
    return jnp.repeat(weights, ROWS, axis=1).reshape(-1)

def update_net(cot, act, weight, master, first, second, scale):
    scaled = (act.astype(jnp.float32) * scale[None, :]).astype(jnp.bfloat16)
    back = (jnp.dot(weight, cot.T, preferred_element_type=jnp.float32) * scale[None, :]).astype(jnp.bfloat16)
    grad = jnp.dot(scaled, cot, preferred_element_type=jnp.float32)
    squares = jnp.sum(grad * grad)
    clip = jnp.minimum(1.0, jnp.sqrt(jnp.float32(D * F)) / jnp.sqrt(squares + 1e-06))
    clipped = grad * clip
    new_first = 0.9 * first + 0.1 * clipped
    new_second = 0.999 * second + 0.001 * clipped * clipped
    step_dir = new_first / FIRST_CORRECTION / (jnp.sqrt(new_second / SECOND_CORRECTION) + 1e-08)
    new_master = master * (1.0 - 0.01 * 0.01) - 0.01 * step_dir
    return (back, new_master, new_first, new_second, new_master.astype(jnp.bfloat16))

def reference(cot_student, cot_fake, act_student, act_fake, weight_student, weight_fake, master_student, first_student, second_student, master_fake, first_fake, second_fake, timesteps):
    back_s, master_s, first_s, second_s, params_s = update_net(cot_student, act_student, weight_student, master_student, first_student, second_student, row_scale(timesteps[:, 0, :]))
    back_f, master_f, first_f, second_f, params_f = update_net(cot_fake, act_fake, weight_fake, master_fake, first_fake, second_fake, row_scale(timesteps[:, 1, :]))
    return (back_s, back_f, master_s, first_s, second_s, master_f, first_f, second_f, params_s, params_f)
```

```python
import jax
import jax.numpy as jnp
from jax import lax
from jax.sharding import PartitionSpec as P

D = 2432
F = 1216
ROWS = 1024


FIRST_CORRECTION = 0.9999734386011124
SECOND_CORRECTION = 0.0952078529183

OUTER = 4


def sample_scale(steps, count):
    weights = 1.0 / (0.1 + steps.astype(jnp.float32) / 1000.0)
    which = jnp.arange(count) // ROWS
    onehot = which[:, None] == jnp.arange(steps.shape[0])[None, :]
    return jnp.sum(jnp.where(onehot, weights[None, :], 0.0), axis=1)


def adam_update(grad, squares, master, first, second):
    clip = jnp.minimum(1.0, jnp.sqrt(jnp.float32(D * F)) / jnp.sqrt(squares + 1e-06))
    clipped = grad * clip
    new_first = 0.9 * first + 0.1 * clipped
    new_second = 0.999 * second + 0.001 * clipped * clipped
    step_dir = new_first / FIRST_CORRECTION / (jnp.sqrt(new_second / SECOND_CORRECTION) + 1e-08)
    new_master = master * (1.0 - 0.01 * 0.01) - 0.01 * step_dir
    return (new_master, new_first, new_second)


def after(value, *others):
    return lax.optimization_barrier((value, *others))[0]


def solution(mesh):
    n_dp, n_tensor = mesh.shape["dp"], mesh.shape["tensor"]
    inner = n_dp // (2 * OUTER)

    def split(p):
        return (p >> inner.bit_length()) & (OUTER - 1), (p >> 1) & (inner - 1), p & 1

    def join(z, m, c):
        return (z * inner + m) * 2 + c

    def move_dp(value, where):
        perm = [(p, join(*where(*split(p)))) for p in range(n_dp)]
        return lax.ppermute(value, "dp", perm)

    def to_plane(value, k):
        return move_dp(value, lambda z, m, c: ((z + k) & (OUTER - 1), m, c))

    def to_middle(value, k):
        return move_dp(value, lambda z, m, c: (z, (m + k) & (inner - 1), c))

    def to_core(value):
        return move_dp(value, lambda z, m, c: (z, m, 1 - c))

    def from_tensor(value, k):
        perm = [(s, (s - k) & (n_tensor - 1)) for s in range(n_tensor)]
        return lax.ppermute(value, "tensor", perm)

    def all_sum(value):
        step = 1
        while step < n_dp:
            value = value + lax.ppermute(value, "dp", [(p, p ^ step) for p in range(n_dp)])
            step *= 2
        step = 1
        while step < n_tensor:
            value = value + lax.ppermute(value, "tensor", [(p, p ^ step) for p in range(n_tensor)])
            step *= 2
        return value

    def per_device(
        cot_student, cot_fake, act_student, act_fake, weight_student, weight_fake,
        master_student, first_student, second_student, master_fake, first_fake, second_fake,
        timesteps,
    ):
        t = lax.axis_index("tensor")
        z, m, c = split(lax.axis_index("dp"))
        f, count = act_student.shape
        r = cot_student.shape[0]
        width = D // n_dp
        plane = D // OUTER

        def pick(value, index):
            return lax.dynamic_index_in_dim(value, index, 0, keepdims=False)

        def rows_of(value, k):
            start = ((t + k) & (n_tensor - 1)) * r
            return lax.dynamic_slice(value, (0, start), (value.shape[0], r))

        nets = (
            (cot_student, act_student, timesteps[0, 0]),
            (cot_fake, act_fake, timesteps[0, 1]),
        )
        prepared = []
        for cot, act, steps in nets:
            scale = sample_scale(steps, count)
            scaled = (act.astype(jnp.float32) * scale[None, :]).astype(jnp.bfloat16)
            prepared.append((cot.T, scaled, scale))

        order = [(n, k) for n in range(2) for k in reversed(range(OUTER))]
        pieces, arrived = {}, []
        for place, (n, k) in enumerate(order):
            own = lax.dynamic_slice(
                prepared[n][0], (plane * ((z + k) & (OUTER - 1)), 0), (plane, r)
            )
            if place >= 2:
                own = after(own, arrived[place - 2])
            others = [from_tensor(own, i) for i in range(1, n_tensor)]
            arrived.append(others[-1])
            pieces[n, k] = [own, *others]

        totals = [None, None]
        for n, k in order:
            grad = None
            for i, piece in enumerate(pieces[n, k]):
                term = lax.dot_general(
                    piece, rows_of(prepared[n][1], i), (((1,), (1,)), ((), ())),
                    preferred_element_type=jnp.float32,
                )
                grad = term if grad is None else grad + term
            grad = grad.reshape(inner, 2, width, f).swapaxes(0, 1)
            grad = pick(grad, c) + to_core(pick(grad, 1 - c))
            mine = pick(grad, m)
            for i in range(1, inner):
                mine = mine + to_middle(pick(grad, (m + i) & (inner - 1)), i)
            if k:
                mine = to_plane(mine, k)
            totals[n] = mine if totals[n] is None else totals[n] + mine

        states = (
            (master_student, first_student, second_student),
            (master_fake, first_fake, second_fake),
        )
        updated, params = [], []
        for n in range(2):
            squares = all_sum(jnp.sum(totals[n] * totals[n]))
            new = adam_update(totals[n], squares, *(state.T for state in states[n]))
            updated.append([value.T for value in new])
            own = new[0].astype(jnp.bfloat16)
            planes = []
            for k in range(OUTER):
                got = to_plane(own, -k) if k else own
                planes.append([got] + [to_middle(got, -i) for i in range(1, inner)])
            stack = jnp.stack([jnp.stack(row) for row in planes])
            stack = jnp.concatenate([stack, stack], axis=0)
            stack = lax.dynamic_slice_in_dim(stack, (OUTER - z) & (OUTER - 1), OUTER, 0)
            stack = jnp.concatenate([stack, stack], axis=1)
            stack = lax.dynamic_slice_in_dim(stack, (inner - m) & (inner - 1), inner, 1)
            other = to_core(stack)
            both = jnp.stack(
                [jnp.where(c == 0, stack, other), jnp.where(c == 0, other, stack)], axis=2
            )
            params.append(both.reshape(D, f).T)

        backs = []
        for n, weight in enumerate((weight_student, weight_fake)):
            scale = prepared[n][2]
            cols = []
            for i in range(n_tensor):
                whole = jnp.concatenate([pieces[n, k][i] for k in range(OUTER)], axis=0)
                whole = jnp.concatenate([whole, whole], axis=0)
                whole = lax.dynamic_slice_in_dim(whole, plane * ((OUTER - z) & (OUTER - 1)), D, 0)
                cols.append(
                    lax.dot_general(
                        weight, whole, (((1,), (0,)), ((), ())),
                        preferred_element_type=jnp.float32,
                    )
                )
            product = jnp.concatenate(cols + cols, axis=1)
            product = lax.dynamic_slice_in_dim(
                product, r * ((n_tensor - t) & (n_tensor - 1)), count, 1
            )
            backs.append((product * scale[None, :]).astype(jnp.bfloat16))

        return (
            backs[0], backs[1], *updated[0], *updated[1], params[0], params[1],
        )

    placed = (
        P(("dp", "tensor"), None),
        P(("dp", "tensor"), None),
        P("tensor", "dp"),
        P("tensor", "dp"),
        P("tensor", None),
        P("tensor", None),
        P("tensor", "dp"),
        P("tensor", "dp"),
        P("tensor", "dp"),
        P("tensor", "dp"),
        P("tensor", "dp"),
        P("tensor", "dp"),
        P("dp", None, None),
    )
    return jax.shard_map(
        per_device,
        mesh=mesh,
        in_specs=placed,
        out_specs=(
            P("tensor", "dp"),
            P("tensor", "dp"),
            P("tensor", "dp"),
            P("tensor", "dp"),
            P("tensor", "dp"),
            P("tensor", "dp"),
            P("tensor", "dp"),
            P("tensor", "dp"),
            P("tensor", None),
            P("tensor", None),
        ),
        check_vma=False,
    )
```

```python
import functools

import jax
import jax.numpy as jnp
from jax import lax
from jax.experimental import pallas as pl
from jax.experimental.pallas import tpu as pltpu
from jax.sharding import PartitionSpec as P

D = 2432
F = 1216
ROWS = 1024


FIRST_CORRECTION = 0.9999734386011124
SECOND_CORRECTION = 0.0952078529183

OUTER = 4
HALF_LIMIT = 60000.0
TILE = 256
VMEM_LIMIT = 48 * 1024 * 1024

NT = (((1,), (1,)), ((), ()))
NN = (((1,), (0,)), ((), ()))


def sample_scale(steps, count):
    weights = 1.0 / (0.1 + steps.astype(jnp.float32) / 1000.0)
    which = jnp.arange(count) // ROWS
    onehot = which[:, None] == jnp.arange(steps.shape[0])[None, :]
    return jnp.sum(jnp.where(onehot, weights[None, :], 0.0), axis=1)


def adam_update(grad, squares, master, first, second):
    clip = jnp.minimum(1.0, jnp.sqrt(jnp.float32(D * F)) / jnp.sqrt(squares + 1e-06))
    clipped = grad * clip
    new_first = 0.9 * first + 0.1 * clipped
    new_second = 0.999 * second + 0.001 * clipped * clipped
    step_dir = new_first / FIRST_CORRECTION / (jnp.sqrt(new_second / SECOND_CORRECTION) + 1e-08)
    new_master = master * (1.0 - 0.01 * 0.01) - 0.01 * step_dir
    return (new_master, new_first, new_second)


def dot(a, b, dims):
    return lax.dot_general(a, b, dims, preferred_element_type=jnp.float32)


def identity(size):
    rows = lax.broadcasted_iota(jnp.int32, (size, size), 0)
    cols = lax.broadcasted_iota(jnp.int32, (size, size), 1)
    return jnp.where(rows == cols, 1.0, 0.0).astype(jnp.bfloat16)


def after(value, *others):
    return lax.optimization_barrier((value, *others))[0]


def cost(flops, nbytes):
    return pl.CostEstimate(flops=flops, bytes_accessed=nbytes, transcendentals=0)


def params_of(**kwargs):
    return pltpu.CompilerParams(vmem_limit_bytes=VMEM_LIMIT, **kwargs)


def solution(mesh):
    n_dp, n_tensor = mesh.shape["dp"], mesh.shape["tensor"]
    inner = n_dp // (2 * OUTER)
    width = D // n_dp

    def split(p):
        return (p >> inner.bit_length()) & (OUTER - 1), (p >> 1) & (inner - 1), p & 1

    def join(z, m, c):
        return (z * inner + m) * 2 + c

    def move_dp(value, where):
        perm = [(p, join(*where(*split(p)))) for p in range(n_dp)]
        return lax.ppermute(value, "dp", perm)

    def to_plane(value, k):
        return move_dp(value, lambda z, m, c: ((z + k) & (OUTER - 1), m, c))

    def to_middle(value, k):
        return move_dp(value, lambda z, m, c: (z, (m + k) & (inner - 1), c))

    def to_core(value):
        return move_dp(value, lambda z, m, c: (z, m, 1 - c))

    def from_tensor(value, k):
        perm = [(s, (s - k) & (n_tensor - 1)) for s in range(n_tensor)]
        return lax.ppermute(value, "tensor", perm)

    def butterfly(value, combine):
        for axis, size in (("dp", n_dp), ("tensor", n_tensor)):
            step = 1
            while step < size:
                perm = [(p, p ^ step) for p in range(size)]
                value = combine(value, lax.ppermute(value, axis, perm))
                step *= 2
        return value

    def relative(place_ref, p):
        z, m, c = split(p)
        return (
            (z - place_ref[0]) & (OUTER - 1),
            (m - place_ref[1]) & (inner - 1),
            c ^ place_ref[2],
        )

    def turn(cot, place, planes_first):
        r = cot.shape[0]
        step = min(r, TILE)

        def kernel(place_ref, cot_ref, out_ref, wide_ref):
            eye = identity(TILE)
            for start in range(0, D, TILE):
                size = min(TILE, D - start)
                wide_ref[start : start + size, :] = dot(
                    eye[:size, :size], cot_ref[:, start : start + size], NT
                )
            for p in range(n_dp):
                k, i, other = relative(place_ref, p)
                block = wide_ref[p * width : (p + 1) * width, :].astype(jnp.bfloat16)
                if planes_first:
                    out_ref[k, other, i] = block
                else:
                    out_ref[other, i, k] = block

        lead = (OUTER, 2, inner) if planes_first else (2, inner, OUTER)
        return pl.pallas_call(
            kernel,
            out_shape=jax.ShapeDtypeStruct((*lead, width, r), jnp.bfloat16),
            grid=(r // step,),
            in_specs=[
                pl.BlockSpec(memory_space=pltpu.SMEM),
                pl.BlockSpec((step, D), lambda s: (s, 0)),
            ],
            out_specs=pl.BlockSpec((*lead, width, step), lambda s: (0, 0, 0, 0, s)),
            scratch_shapes=[pltpu.VMEM((D, step), jnp.float32)],
            compiler_params=params_of(),
            cost_estimate=cost(2 * TILE * D * r, 4 * D * r),
        )(place, cot)

    def back_other(weight, pieces, scale, place):
        f = weight.shape[0]
        r = pieces[0].shape[-1]

        def kernel(place_ref, weight_ref, *refs):
            piece_refs, (scale_ref, out_ref, wide_ref) = refs[:OUTER], refs[OUTER:]
            z, m, c = (place_ref[n] for n in range(3))
            for k in range(OUTER):
                for other in range(2):
                    for i in range(inner):
                        p = join((z + k) & (OUTER - 1), (m + i) & (inner - 1), c ^ other)
                        wide_ref[p] = piece_refs[k][other, i].astype(jnp.float32)
            turned = wide_ref[...].reshape(D, r).astype(jnp.bfloat16)
            out_ref[...] = (dot(weight_ref[...], turned, NN) * scale_ref[...]).astype(jnp.bfloat16)

        whole = pl.BlockSpec(memory_space=pltpu.VMEM)
        return pl.pallas_call(
            kernel,
            out_shape=jax.ShapeDtypeStruct((f, r), jnp.bfloat16),
            in_specs=[pl.BlockSpec(memory_space=pltpu.SMEM)] + [whole] * (OUTER + 2),
            out_specs=whole,
            scratch_shapes=[pltpu.VMEM((n_dp, width, r), jnp.float32)],
            compiler_params=params_of(),
            cost_estimate=cost(2 * f * D * r, 2 * (f * D + D * r + f * r)),
        )(place, weight, *pieces, scale)

    def spread(blocks, net, place):
        f = blocks[0].shape[-1]

        def kernel(place_ref, *refs):
            block_refs, (out_ref, wide_ref) = refs[:-2], refs[-2:]
            z, m, c = (place_ref[n] for n in range(3))
            at = 0
            for other in range(2):
                for k in range(OUTER):
                    for i in range(inner):
                        p = join((z + k) & (OUTER - 1), (m + i) & (inner - 1), c ^ other)
                        wide_ref[p] = block_refs[at][...].reshape(width, f).astype(jnp.float32)
                        at += 1
            flat = wide_ref[...].reshape(D, f).astype(jnp.bfloat16)
            eye = identity(TILE)
            for start in range(0, f, TILE):
                size = min(TILE, f - start)
                out_ref[start : start + size, :] = dot(
                    eye[:size, :size], flat[:, start : start + size], NT
                ).astype(jnp.bfloat16)

        specs, operands = [], []
        for array, lead in blocks_index(blocks):
            zeros = (0,) * (array.ndim - 2 - len(lead) - 1)
            index = (*lead, net, *zeros, 0, 0)
            specs.append(
                pl.BlockSpec((1,) * (array.ndim - 2) + (width, f), functools.partial(lambda index, s: index, index))
            )
            operands.append(array)
        return pl.pallas_call(
            kernel,
            out_shape=jax.ShapeDtypeStruct((f, D), jnp.bfloat16),
            grid=(1,),
            in_specs=[pl.BlockSpec(memory_space=pltpu.SMEM)] + specs,
            out_specs=pl.BlockSpec((f, D), lambda s: (0, 0)),
            scratch_shapes=[pltpu.VMEM((n_dp, width, f), jnp.float32)],
            compiler_params=params_of(),
            cost_estimate=cost(2 * TILE * D * f, 4 * D * f),
        )(place, *operands)

    def blocks_index(blocks):
        for block in blocks:
            if block.ndim == 3:
                yield block, ()
            else:
                for at in range(block.shape[0]):
                    yield block, (at,)

    def per_device(
        cot_student, cot_fake, act_student, act_fake, weight_student, weight_fake,
        master_student, first_student, second_student, master_fake, first_fake, second_fake,
        timesteps,
    ):
        t = lax.axis_index("tensor")
        z, m, c = split(lax.axis_index("dp"))
        place = jnp.stack([z, m, c]).astype(jnp.int32)
        f, count = act_student.shape
        r = cot_student.shape[0]

        def rows_of(value, k):
            start = ((t + k) & (n_tensor - 1)) * r
            return lax.dynamic_slice_in_dim(value, start, r, value.ndim - 1)

        def scaled_by(act, scale):
            return (act.astype(jnp.float32) * scale[None, :]).astype(jnp.bfloat16)

        scale_student = sample_scale(timesteps[0, 0], count)
        scale_fake = sample_scale(timesteps[0, 1], count)

        acts = [
            from_tensor(rows_of(act_fake, j), -j) for j in range(1, n_tensor)
        ]
        acts = [rows_of(act_fake, 0), *acts]
        own_scale = rows_of(scale_fake, 0)
        scaled_fake = [scaled_by(act, own_scale) for act in acts]
        scaled_student = scaled_by(act_student, scale_student)

        turned_student = turn(cot_student, place, True)
        turned_fake = turn(cot_fake, place, False).reshape(2, -1, r)

        def bound(cot, act, scale):
            return (
                jnp.max(jnp.abs(cot)).astype(jnp.float32)
                * jnp.max(jnp.abs(act)).astype(jnp.float32)
                * jnp.max(scale)
            )

        bounds = butterfly(
            jnp.stack(
                [
                    bound(cot_student, act_student, scale_student),
                    bound(cot_fake, act_fake, scale_fake),
                ]
            ),
            jnp.maximum,
        )
        bounds = jnp.maximum(bounds, 1e-30) * (1.01 * count * n_dp / HALF_LIMIT)

        def shrink(value, net):
            return (value * (1.0 / bounds[net])).astype(jnp.float16)

        def widen(value, net):
            return value.astype(jnp.float32) * bounds[net]

        def over_middle(blocks, net):
            mine = blocks[0]
            for i in range(1, inner):
                mine = mine + widen(to_middle(shrink(blocks[i], net), i), net)
            return mine

        parts_fake = []
        for scaled in scaled_fake:
            keep = dot(turned_fake[0], scaled, NT)
            send = dot(turned_fake[1], scaled, NT)
            both = (keep + to_core(send)).reshape(inner, OUTER, width, f)
            mine = over_middle(both, 1)
            total = mine[0]
            for k in range(1, OUTER):
                total = total + widen(to_plane(shrink(mine[k], 1), k), 1)
            parts_fake.append(total)

        order = (3, 1, 2, 0)
        pieces, arrived = {}, [scaled_fake[-1]]
        total_student = None
        for at, k in enumerate(order):
            own = turned_student[k]
            if at >= 2:
                own = after(own, arrived[at - 2])
            others = [from_tensor(own, j) for j in range(1, n_tensor)]
            arrived.append(others[-1])
            pieces[k] = others
            halves = [own, *others]
            sums = []
            for other in range(2):
                grad = None
                for j, piece in enumerate(halves):
                    term = dot(piece[other].reshape(-1, r), rows_of(scaled_student, j), NT)
                    grad = term if grad is None else grad + term
                sums.append(grad)
            both = (sums[0] + to_core(sums[1])).reshape(inner, width, f)
            mine = over_middle(both, 0)
            if k:
                mine = widen(to_plane(shrink(mine, 0), k), 0)
            total_student = mine if total_student is None else total_student + mine

        total_fake = parts_fake[0]
        last = None
        for j in range(1, n_tensor):
            last = shrink(parts_fake[j], 1)
            total_fake = total_fake + widen(from_tensor(last, j), 1)

        raw = after(cot_fake, last, arrived[-2])
        cots_fake = [cot_fake] + [from_tensor(raw, j) for j in range(1, n_tensor)]

        totals = (total_student, total_fake)
        squares = butterfly(jnp.stack([jnp.sum(total * total) for total in totals]), jnp.add)
        states = (
            (master_student, first_student, second_student),
            (master_fake, first_fake, second_fake),
        )
        updated = [
            adam_update(totals[n], squares[n], *(state.T for state in states[n])) for n in range(2)
        ]
        own = jnp.stack([new[0].astype(jnp.bfloat16) for new in updated])
        mine = []
        for k in range(OUTER):
            got = to_plane(own, -k) if k else own
            mine.append(got)
            for i in range(1, inner):
                mine.append(to_middle(got, -i))
        half = len(mine) // 2
        theirs = [to_core(jnp.stack(mine[:half])), to_core(jnp.stack(mine[half:]))]
        params = [spread([*mine, *theirs], n, place) for n in range(2)]

        def assemble(parts):
            whole = jnp.concatenate(parts + parts, axis=1)
            return lax.dynamic_slice_in_dim(
                whole, r * ((n_tensor - t) & (n_tensor - 1)), count, 1
            )

        def back_rows(weight, cot, scale):
            return (dot(weight, cot, NT) * scale[None, :]).astype(jnp.bfloat16)

        back_student = [back_rows(weight_student, cot_student, rows_of(scale_student, 0))]
        back_student += [
            back_other(
                weight_student,
                [pieces[k][j - 1] for k in range(OUTER)],
                rows_of(scale_student, j)[None, :],
                place,
            )
            for j in range(1, n_tensor)
        ]
        back_fake = [
            back_rows(weight_fake, cots_fake[j], rows_of(scale_fake, j)) for j in range(n_tensor)
        ]

        new_states = [value.T for new in updated for value in new]
        return (assemble(back_student), assemble(back_fake), *new_states, *params)

    placed = (
        P(("dp", "tensor"), None),
        P(("dp", "tensor"), None),
        P("tensor", "dp"),
        P("tensor", "dp"),
        P("tensor", None),
        P("tensor", None),
        P("tensor", "dp"),
        P("tensor", "dp"),
        P("tensor", "dp"),
        P("tensor", "dp"),
        P("tensor", "dp"),
        P("tensor", "dp"),
        P("dp", None, None),
    )
    return jax.shard_map(
        per_device,
        mesh=mesh,
        in_specs=placed,
        out_specs=(
            P("tensor", "dp"),
            P("tensor", "dp"),
            P("tensor", "dp"),
            P("tensor", "dp"),
            P("tensor", "dp"),
            P("tensor", "dp"),
            P("tensor", "dp"),
            P("tensor", "dp"),
            P("tensor", None),
            P("tensor", None),
        ),
        check_vma=False,
    )
```

```python
import functools

import jax
import jax.numpy as jnp
from jax import lax
from jax.experimental import pallas as pl
from jax.experimental.pallas import tpu as pltpu
from jax.sharding import PartitionSpec as P

D = 2432
F = 1216
ROWS = 1024


FIRST_CORRECTION = 0.9999734386011124
SECOND_CORRECTION = 0.0952078529183

OUTER = 4
HALF_LIMIT = 60000.0
TILE = 256
VMEM_LIMIT = 48 * 1024 * 1024

NT = (((1,), (1,)), ((), ()))
NN = (((1,), (0,)), ((), ()))


def sample_scale(steps, count):
    weights = 1.0 / (0.1 + steps.astype(jnp.float32) / 1000.0)
    which = jnp.arange(count) // ROWS
    onehot = which[:, None] == jnp.arange(steps.shape[0])[None, :]
    return jnp.sum(jnp.where(onehot, weights[None, :], 0.0), axis=1)


def adam_update(grad, squares, master, first, second):
    clip = jnp.minimum(1.0, jnp.sqrt(jnp.float32(D * F)) / jnp.sqrt(squares + 1e-06))
    clipped = grad * clip
    new_first = 0.9 * first + 0.1 * clipped
    new_second = 0.999 * second + 0.001 * clipped * clipped
    step_dir = new_first / FIRST_CORRECTION / (jnp.sqrt(new_second / SECOND_CORRECTION) + 1e-08)
    new_master = master * (1.0 - 0.01 * 0.01) - 0.01 * step_dir
    return (new_master, new_first, new_second)


def dot(a, b, dims):
    return lax.dot_general(a, b, dims, preferred_element_type=jnp.float32)


def identity(size):
    rows = lax.broadcasted_iota(jnp.int32, (size, size), 0)
    cols = lax.broadcasted_iota(jnp.int32, (size, size), 1)
    return jnp.where(rows == cols, 1.0, 0.0).astype(jnp.bfloat16)


def cost(flops, nbytes):
    return pl.CostEstimate(flops=flops, bytes_accessed=nbytes, transcendentals=0)


def params_of(**kwargs):
    return pltpu.CompilerParams(vmem_limit_bytes=VMEM_LIMIT, **kwargs)


def solution(mesh):
    n_dp, n_tensor = mesh.shape["dp"], mesh.shape["tensor"]
    inner = n_dp // (2 * OUTER)
    width = D // n_dp

    def split(p):
        return (p >> inner.bit_length()) & (OUTER - 1), (p >> 1) & (inner - 1), p & 1

    def join(z, m, c):
        return (z * inner + m) * 2 + c

    def move_dp(value, where):
        perm = [(p, join(*where(*split(p)))) for p in range(n_dp)]
        return lax.ppermute(value, "dp", perm)

    def to_plane(value, k):
        return move_dp(value, lambda z, m, c: ((z + k) & (OUTER - 1), m, c))

    def to_middle(value, k):
        return move_dp(value, lambda z, m, c: (z, (m + k) & (inner - 1), c))

    def to_core(value):
        return move_dp(value, lambda z, m, c: (z, m, 1 - c))

    def from_tensor(value, k):
        perm = [(s, (s - k) & (n_tensor - 1)) for s in range(n_tensor)]
        return lax.ppermute(value, "tensor", perm)

    def relative(place_ref, p):
        z, m, c = split(p)
        return (
            (z - place_ref[0]) & (OUTER - 1),
            (m - place_ref[1]) & (inner - 1),
            c ^ place_ref[2],
        )

    def turn(cot, place, by_planes):
        r = cot.shape[0]
        step = min(r, TILE)
        count = OUTER if by_planes else 2
        lead = (2, inner) if by_planes else (inner, OUTER)

        def kernel(place_ref, cot_ref, *refs):
            out_refs, (top_ref, wide_ref) = refs[:count], refs[count:]
            eye = identity(TILE)
            for start in range(0, D, TILE):
                size = min(TILE, D - start)
                wide_ref[start : start + size, :] = dot(
                    eye[:size, :size], cot_ref[:, start : start + size], NT
                )
            top = jnp.max(jnp.abs(wide_ref[...]).reshape(D // 8, 8, step), axis=0)
            top = jnp.broadcast_to(jnp.max(top), (8, 128))

            @pl.when(pl.program_id(0) == 0)
            def _():
                top_ref[...] = top

            @pl.when(pl.program_id(0) > 0)
            def _():
                top_ref[...] = jnp.maximum(top_ref[...], top)

            for p in range(n_dp):
                k, i, other = relative(place_ref, p)
                block = wide_ref[p * width : (p + 1) * width, :].astype(jnp.bfloat16)
                which, at = (k, (other, i)) if by_planes else (other, (i, k))
                for n in range(count):

                    @pl.when(which == n)
                    def _(n=n, at=at, block=block):
                        out_refs[n][at] = block

        *outs, top = pl.pallas_call(
            kernel,
            out_shape=[jax.ShapeDtypeStruct((*lead, width, r), jnp.bfloat16)] * count
            + [jax.ShapeDtypeStruct((8, 128), jnp.float32)],
            grid=(r // step,),
            in_specs=[
                pl.BlockSpec(memory_space=pltpu.SMEM),
                pl.BlockSpec((step, D), lambda s: (s, 0)),
            ],
            out_specs=[pl.BlockSpec((*lead, width, step), lambda s: (0, 0, 0, s))] * count
            + [pl.BlockSpec((8, 128), lambda s: (0, 0))],
            scratch_shapes=[pltpu.VMEM((D, step), jnp.float32)],
            compiler_params=params_of(),
            cost_estimate=cost(2 * TILE * D * r, 4 * D * r),
        )(place, cot)
        return outs, top

    def back_other(weight, pieces, scale, place):
        f = weight.shape[0]
        r = pieces[0].shape[-1]

        def kernel(place_ref, weight_ref, *refs):
            piece_refs, (scale_ref, out_ref, wide_ref) = refs[:OUTER], refs[OUTER:]
            z, m, c = (place_ref[n] for n in range(3))
            for k in range(OUTER):
                for other in range(2):
                    for i in range(inner):
                        p = join((z + k) & (OUTER - 1), (m + i) & (inner - 1), c ^ other)
                        wide_ref[p] = piece_refs[k][other, i].astype(jnp.float32)
            turned = wide_ref[...].reshape(D, r).astype(jnp.bfloat16)
            out_ref[...] = (dot(weight_ref[...], turned, NN) * scale_ref[...]).astype(jnp.bfloat16)

        whole = pl.BlockSpec(memory_space=pltpu.VMEM)
        return pl.pallas_call(
            kernel,
            out_shape=jax.ShapeDtypeStruct((f, r), jnp.bfloat16),
            in_specs=[pl.BlockSpec(memory_space=pltpu.SMEM)] + [whole] * (OUTER + 2),
            out_specs=whole,
            scratch_shapes=[pltpu.VMEM((n_dp, width, r), jnp.float32)],
            compiler_params=params_of(),
            cost_estimate=cost(2 * f * D * r, 2 * (f * D + D * r + f * r)),
        )(place, weight, *pieces, scale)

    def spread(blocks, net, place):
        f = blocks[0].shape[-1]

        def kernel(place_ref, *refs):
            block_refs, (out_ref, wide_ref) = refs[:-2], refs[-2:]
            z, m, c = (place_ref[n] for n in range(3))
            at = 0
            for other in range(2):
                for k in range(OUTER):
                    for i in range(inner):
                        p = join((z + k) & (OUTER - 1), (m + i) & (inner - 1), c ^ other)
                        wide_ref[p] = block_refs[at][...].reshape(width, f).astype(jnp.float32)
                        at += 1
            flat = wide_ref[...].reshape(D, f).astype(jnp.bfloat16)
            eye = identity(TILE)
            for start in range(0, f, TILE):
                size = min(TILE, f - start)
                out_ref[start : start + size, :] = dot(
                    eye[:size, :size], flat[:, start : start + size], NT
                ).astype(jnp.bfloat16)

        specs, operands = [], []
        for array, lead in blocks_index(blocks):
            zeros = (0,) * (array.ndim - 2 - len(lead) - 1)
            index = (*lead, net, *zeros, 0, 0)
            specs.append(
                pl.BlockSpec((1,) * (array.ndim - 2) + (width, f), functools.partial(lambda index, s: index, index))
            )
            operands.append(array)
        return pl.pallas_call(
            kernel,
            out_shape=jax.ShapeDtypeStruct((f, D), jnp.bfloat16),
            grid=(1,),
            in_specs=[pl.BlockSpec(memory_space=pltpu.SMEM)] + specs,
            out_specs=pl.BlockSpec((f, D), lambda s: (0, 0)),
            scratch_shapes=[pltpu.VMEM((n_dp, width, f), jnp.float32)],
            compiler_params=params_of(),
            cost_estimate=cost(2 * TILE * D * f, 4 * D * f),
        )(place, *operands)

    def blocks_index(blocks):
        for block in blocks:
            if block.ndim == 3:
                yield block, ()
            else:
                for at in range(block.shape[0]):
                    yield block, (at,)

    def per_device(
        cot_student, cot_fake, act_student, act_fake, weight_student, weight_fake,
        master_student, first_student, second_student, master_fake, first_fake, second_fake,
        timesteps,
    ):
        t = lax.axis_index("tensor")
        z, m, c = split(lax.axis_index("dp"))
        place = jnp.stack([z, m, c]).astype(jnp.int32)
        f, count = act_student.shape
        r = cot_student.shape[0]

        def rows_of(value, k):
            start = ((t + k) & (n_tensor - 1)) * r
            return lax.dynamic_slice_in_dim(value, start, r, value.ndim - 1)

        def scaled_by(act, scale):
            return (act.astype(jnp.float32) * scale[None, :]).astype(jnp.bfloat16)

        scale_student = sample_scale(timesteps[0, 0], count)
        scale_fake = sample_scale(timesteps[0, 1], count)

        token = []

        def step(work, *inputs):
            if token:
                *inputs, _ = lax.optimization_barrier((*inputs, token[0]))
            out = work(*inputs)
            token[:] = jax.tree.leaves(out)[:1]
            return out

        row = lax.broadcasted_iota(jnp.int32, (8, 128), 0)

        def pair(student, fake):
            return jnp.where(row == 0, student, fake)

        def gather_planes(value, combine):
            got = [to_plane(value, k) for k in range(1, OUTER)]
            return lambda: step(lambda *all_of: functools.reduce(combine, all_of), value, *got)

        def gather_chips(value, combine):
            got = [
                move_dp(value, lambda z, m, c, i=i, o=o: (z, (m + i) & (inner - 1), c ^ o))
                for i in range(inner)
                for o in range(2)
                if i or o
            ]
            return lambda: step(lambda *all_of: functools.reduce(combine, all_of), value, *got)

        own_scale = rows_of(scale_fake, 0)
        act_sent = step(lambda act: [rows_of(act, j) for j in range(1, n_tensor)], act_fake)
        acts = [from_tensor(act, -j) for j, act in enumerate(act_sent, 1)]
        planes, top_student = step(lambda cot: turn(cot, place, True), cot_student)
        order = (3, 1, 2, 0)
        others = {k: [from_tensor(planes[k], j) for j in range(1, n_tensor)] for k in order}
        cores, top_fake = step(lambda cot: turn(cot, place, False), cot_fake)
        cores = [core.reshape(-1, r) for core in cores]

        def bound(top_s, top_f, act_s, act_f):
            tops = [
                top[0, 0] * jnp.max(jnp.abs(act)).astype(jnp.float32) * jnp.max(scale)
                for top, act, scale in (
                    (top_s, act_s, scale_student),
                    (top_f, act_f, scale_fake),
                )
            ]
            return pair(*tops)

        bounds = step(bound, top_student, top_fake, act_student, act_fake)
        finish = gather_planes(bounds, jnp.maximum)
        scaled = step(lambda act: scaled_by(rows_of(act, 0), own_scale), act_fake)
        sends, keeps = [], []
        sends.append(to_core(step(lambda a, b: dot(a, b, NT), cores[1], scaled)))
        bounds = finish()
        finish = gather_chips(bounds, jnp.maximum)
        keeps.append(step(lambda a, b: dot(a, b, NT), cores[0], scaled))
        scaled_student = [
            step(lambda act, j=j: scaled_by(rows_of(act, j), rows_of(scale_student, j)), act_student)
            for j in range(n_tensor)
        ]
        bounds = finish()

        def factors(bounds):
            bounds = jnp.maximum(bounds, 1e-30) * (1.01 * count * n_dp / HALF_LIMIT)
            return bounds[:2, 0], 1.0 / bounds[:2, 0]

        grow, fit = step(factors, bounds)

        def shrink(value, net):
            return (value * fit[net]).astype(jnp.float16)

        def widen(value, net):
            return value.astype(jnp.float32) * grow[net]

        halves = ((2, 3), (0, 1))

        def fake_middle(keep, send):
            both = (keep + send).reshape(inner, OUTER, width, f)
            sent = [
                [shrink(both[i, lo : hi + 1], 1) for i in range(1, inner)] for lo, hi in halves
            ]
            return sent, [both[0, lo : hi + 1] for lo, hi in halves]

        def start_middle(keep, send):
            sent, mine = step(fake_middle, keep, send)
            return [
                (own, [to_middle(value, i) for i, value in enumerate(values, 1)])
                for own, values in zip(mine, sent)
            ]

        middles = [start_middle(keeps[0], sends[0])]
        for act in acts:
            scaled = step(lambda act: scaled_by(act, own_scale), act)
            sends.append(to_core(step(lambda a, b: dot(a, b, NT), cores[1], scaled)))
            keeps.append(step(lambda a, b: dot(a, b, NT), cores[0], scaled))
        for keep, send in zip(keeps[1:], sends[1:]):
            middles.append(start_middle(keep, send))

        def own_term(piece, scaled):
            return [dot(piece[other].reshape(-1, r), scaled, NT) for other in range(2)]

        own_terms = {k: step(own_term, planes[k], scaled_student[0]) for k in order}
        kept = {}

        def multiply(k):
            def half(other, *operands):
                term, *operands = operands
                pieces, scales = operands[: n_tensor - 1], operands[n_tensor - 1 :]
                for piece, scaled in zip(pieces, scales):
                    term = term + dot(piece[other].reshape(-1, r), scaled, NT)
                return term

            operands = [*others[k], *scaled_student[1:]]
            send = to_core(step(functools.partial(half, 1), own_terms[k][1], *operands))
            kept[k] = step(functools.partial(half, 0), own_terms[k][0], *operands), send

        crossing = {}

        def cross_middle(k):
            def work(keep, send):
                both = (keep + send).reshape(inner, width, f)
                return [shrink(both[i], 0) for i in range(1, inner)], both[0]

            sent, own = step(work, *kept[k])
            crossing[k] = own, [to_middle(value, i) for i, value in enumerate(sent, 1)]

        to_sum = []

        def cross_planes(k):
            def work(own, *got):
                for value in got:
                    own = own + widen(value, 0)
                return shrink(own, 0) if k else own

            own, got = crossing[k]
            value = step(work, own, *got)
            to_sum.append(to_plane(value, k) if k else value)

        fake_sums = [[] for _ in range(n_tensor)]

        def fake_planes(j, part):
            lo, hi = halves[part]

            def work(own, *got):
                for value in got:
                    own = own + widen(value, 1)
                return [shrink(own[k - lo], 1) if k else own[0] for k in range(hi, lo - 1, -1)]

            own, got = middles[j][part]
            values = step(work, own, *got)
            for k, value in zip(range(hi, lo - 1, -1), values):
                fake_sums[j].append(to_plane(value, k) if k else value)

        def fake_total(j):
            def work(*values):
                total = values[-1]
                for value in values[:-1]:
                    total = total + widen(value, 1)
                return total

            return step(work, *fake_sums[j])

        fake_planes(0, 0)
        multiply(3)
        cross_middle(3)
        fake_planes(0, 1)
        multiply(1)
        cross_middle(1)
        for j in range(1, n_tensor):
            fake_planes(j, 0)
        multiply(2)
        cross_middle(2)
        for j in range(1, n_tensor):
            fake_planes(j, 1)
        cross_planes(3)
        fake_mine = fake_total(0)
        fake_others = [fake_total(j) for j in range(1, n_tensor)]
        fake_got = [from_tensor(value, j) for j, value in enumerate(fake_others, 1)]

        quarter = r // 4
        cuts = ((0, quarter), (quarter, 3 * quarter), (3 * quarter, r))
        raw_first = step(lambda cot: cot[: cuts[0][1]], cot_fake)
        raw = [[from_tensor(raw_first, j) for j in range(1, n_tensor)]]
        cross_planes(1)
        multiply(0)
        cross_planes(2)
        cross_middle(0)

        def student_partial(*values):
            total = widen(values[0], 0)
            for value in values[1:]:
                total = total + widen(value, 0)
            return total

        total_student = step(student_partial, *to_sum)
        to_sum.clear()

        def fake_all(mine, *got):
            for value in got:
                mine = mine + value
            return mine, jnp.sum(mine * mine)

        total_fake, square_fake = step(fake_all, fake_mine, *fake_got)
        cross_planes(0)

        def student_all(total, value, square_fake):
            total = total + value
            return pair(jnp.sum(total * total), square_fake), total

        squares, total_student = step(student_all, total_student, to_sum[0], square_fake)
        squares = gather_planes(squares, jnp.add)()
        squares = gather_chips(squares, jnp.add)()
        got = [from_tensor(squares, j) for j in range(1, n_tensor)]
        for lo, hi in cuts[1:]:
            rows = step(lambda cot: cot[lo:hi], cot_fake)
            raw.append([from_tensor(rows, j) for j in range(1, n_tensor)])
        squares = step(lambda *values: functools.reduce(jnp.add, values), squares, *got)

        totals = (total_student, total_fake)
        states = (
            (master_student, first_student, second_student),
            (master_fake, first_fake, second_fake),
        )

        def update(squares, *totals):
            updated = [
                adam_update(totals[n], squares[n, 0], *(state.T for state in states[n]))
                for n in range(2)
            ]
            return jnp.stack([new[0].astype(jnp.bfloat16) for new in updated]), updated

        own, updated = step(update, squares, *totals)

        def back_rows(weight, cot, scale):
            return (dot(weight, cot, NT) * scale[None, :]).astype(jnp.bfloat16)

        mine = {}

        def spread_middle(k, value):
            mine[k] = [value] + [to_middle(value, -i) for i in range(1, inner)]

        planes_got = {k: to_plane(own, -k) for k in (1, 3, 2)}
        spread_middle(0, own)
        back_student = [
            step(lambda w, cot: back_rows(w, cot, rows_of(scale_student, 0)), weight_student, cot_student)
        ]
        spread_middle(1, step(lambda value: value, planes_got[1]))
        for j in range(1, n_tensor):
            back_student.append(
                step(
                    lambda w, *pieces: back_other(
                        w, pieces, rows_of(scale_student, j)[None, :], place
                    ),
                    weight_student,
                    *[others[k][j - 1] for k in range(OUTER)],
                )
            )
        spread_middle(3, step(lambda value: value, planes_got[3]))
        back_fake_own = step(
            lambda w, cot: back_rows(w, cot, rows_of(scale_fake, 0)), weight_fake, cot_fake
        )
        first_half = step(lambda *values: jnp.stack(values), *mine[0], *mine[1])
        theirs = [to_core(first_half)]
        spread_middle(2, step(lambda value: value, planes_got[2]))
        second_half = step(lambda *values: jnp.stack(values), *mine[2], *mine[3])
        theirs.append(to_core(second_half))
        blocks = [first_half, second_half, *theirs]
        params = [spread(blocks, n, place) for n in range(2)]

        def assemble(parts):
            whole = jnp.concatenate(parts + parts, axis=1)
            return lax.dynamic_slice_in_dim(
                whole, r * ((n_tensor - t) & (n_tensor - 1)), count, 1
            )

        back_fake = [back_fake_own]
        for j in range(1, n_tensor):
            scale = rows_of(scale_fake, j)
            parts = [
                back_rows(weight_fake, raw[n][j - 1], scale[lo:hi])
                for n, (lo, hi) in enumerate(cuts)
            ]
            back_fake.append(jnp.concatenate(parts, axis=1))

        new_states = [value.T for new in updated for value in new]
        return (assemble(back_student), assemble(back_fake), *new_states, *params)

    placed = (
        P(("dp", "tensor"), None),
        P(("dp", "tensor"), None),
        P("tensor", "dp"),
        P("tensor", "dp"),
        P("tensor", None),
        P("tensor", None),
        P("tensor", "dp"),
        P("tensor", "dp"),
        P("tensor", "dp"),
        P("tensor", "dp"),
        P("tensor", "dp"),
        P("tensor", "dp"),
        P("dp", None, None),
    )
    return jax.shard_map(
        per_device,
        mesh=mesh,
        in_specs=placed,
        out_specs=(
            P("tensor", "dp"),
            P("tensor", "dp"),
            P("tensor", "dp"),
            P("tensor", "dp"),
            P("tensor", "dp"),
            P("tensor", "dp"),
            P("tensor", "dp"),
            P("tensor", "dp"),
            P("tensor", None),
            P("tensor", None),
        ),
        check_vma=False,
    )
```

```python
import functools

import jax
import jax.numpy as jnp
from jax import lax
from jax.experimental import pallas as pl
from jax.experimental.pallas import tpu as pltpu
from jax.sharding import PartitionSpec as P

D = 2432
F = 1216
ROWS = 1024


FIRST_CORRECTION = 0.9999734386011124
SECOND_CORRECTION = 0.0952078529183

OUTER = 4
HALF_LIMIT = 60000.0
TILE = 256
LANES = 128

NT = (((1,), (1,)), ((), ()))
NN = (((1,), (0,)), ((), ()))

SMEM = pl.BlockSpec(memory_space=pltpu.SMEM)
VMEM = pl.BlockSpec(memory_space=pltpu.VMEM)
ANY = pl.BlockSpec(memory_space=pl.ANY)


def adam_update(grad, squares, master, first, second):
    clip = jnp.minimum(1.0, jnp.sqrt(jnp.float32(D * F)) / jnp.sqrt(squares + 1e-06))
    clipped = grad * clip
    new_first = 0.9 * first + 0.1 * clipped
    new_second = 0.999 * second + 0.001 * clipped * clipped
    step_dir = new_first / FIRST_CORRECTION / (jnp.sqrt(new_second / SECOND_CORRECTION) + 1e-08)
    new_master = master * (1.0 - 0.01 * 0.01) - 0.01 * step_dir
    return (new_master, new_first, new_second)


def dot(a, b, dims):
    return lax.dot_general(a, b, dims, preferred_element_type=jnp.float32)


def identity(size):
    rows = lax.broadcasted_iota(jnp.int32, (size, size), 0)
    cols = lax.broadcasted_iota(jnp.int32, (size, size), 1)
    return jnp.where(rows == cols, 1.0, 0.0).astype(jnp.bfloat16)


def array(shape, dtype):
    return jax.ShapeDtypeStruct(shape, dtype)


def call(kernel, out_shape, *operands, mib=12, **kwargs):
    return pl.pallas_call(
        kernel,
        out_shape=out_shape,
        compiler_params=pltpu.CompilerParams(vmem_limit_bytes=mib * 1024 * 1024),
        cost_estimate=pl.CostEstimate(flops=0, bytes_accessed=0, transcendentals=0),
        **kwargs,
    )(*operands)


def solution(mesh):
    n_dp, n_tensor = mesh.shape["dp"], mesh.shape["tensor"]
    inner = n_dp // (2 * OUTER)
    width = D // n_dp

    def split(p):
        return (p >> inner.bit_length()) & (OUTER - 1), (p >> 1) & (inner - 1), p & 1

    def join(z, m, c):
        return (z * inner + m) * 2 + c

    def move_dp(value, where):
        perm = [(p, join(*where(*split(p)))) for p in range(n_dp)]
        return lax.ppermute(value, "dp", perm)

    def to_plane(value, k):
        return move_dp(value, lambda z, m, c: ((z + k) & (OUTER - 1), m, c))

    def to_middle(value, k):
        return move_dp(value, lambda z, m, c: (z, (m + k) & (inner - 1), c))

    def to_core(value):
        return move_dp(value, lambda z, m, c: (z, m, 1 - c))

    def from_tensor(value, k):
        perm = [(s, (s - k) & (n_tensor - 1)) for s in range(n_tensor)]
        return lax.ppermute(value, "tensor", perm)

    def my_place():
        return split(lax.axis_index("dp"))

    def relative(p):
        z, m, c = split(p)
        my_z, my_m, my_c = my_place()
        return (z - my_z) & (OUTER - 1), (m - my_m) & (inner - 1), c ^ my_c

    def owner(k, i, other):
        z, m, c = my_place()
        return join((z + k) & (OUTER - 1), (m + i) & (inner - 1), c ^ other)

    def first_row(j, r):
        start = ((lax.axis_index("tensor") + j) & (n_tensor - 1)) * r
        return pl.multiple_of(start, LANES)

    def cut_acts(act, r):
        count = n_tensor - 1

        def kernel(act_ref, *refs):
            out_refs, sem = refs[:-1], refs[-1]
            copies = [
                pltpu.make_async_copy(
                    act_ref.at[:, pl.ds(first_row(j + 1, r), r)], out_refs[j], sem.at[j]
                )
                for j in range(count)
            ]
            for copy in copies:
                copy.start()
            for copy in copies:
                copy.wait()

        return call(
            kernel,
            [array((act.shape[0], r), act.dtype)] * count,
            act,
            in_specs=[ANY],
            out_specs=[VMEM] * count,
            scratch_shapes=[pltpu.SemaphoreType.DMA((count,))],
        )

    def turn(cot, by_planes):
        r = cot.shape[0]
        step = min(r, TILE)
        count = OUTER if by_planes else 2
        lead = (2, inner) if by_planes else (inner, OUTER)

        def kernel(cot_ref, *refs):
            out_refs, (top_ref, wide_ref) = refs[:count], refs[count:]
            eye = identity(TILE)
            for start in range(0, D, TILE):
                size = min(TILE, D - start)
                wide_ref[start : start + size, :] = dot(
                    eye[:size, :size], cot_ref[:, start : start + size], NT
                )
            top = jnp.max(jnp.abs(wide_ref[...]).reshape(D // 8, 8, step), axis=0)
            top = jnp.broadcast_to(jnp.max(top), (8, LANES))

            @pl.when(pl.program_id(0) == 0)
            def _():
                top_ref[...] = top

            @pl.when(pl.program_id(0) > 0)
            def _():
                top_ref[...] = jnp.maximum(top_ref[...], top)

            for p in range(n_dp):
                k, i, other = relative(p)
                block = wide_ref[p * width : (p + 1) * width, :].astype(jnp.bfloat16)
                which, at = (k, (other, i)) if by_planes else (other, (i, k))
                for n in range(count):

                    @pl.when(which == n)
                    def _(n=n, at=at, block=block):
                        out_refs[n][at] = block

        *outs, top = call(
            kernel,
            [array((*lead, width, r), jnp.bfloat16)] * count + [array((8, LANES), jnp.float32)],
            cot,
            grid=(r // step,),
            in_specs=[pl.BlockSpec((step, D), lambda s: (s, 0))],
            out_specs=[pl.BlockSpec((*lead, width, step), lambda s: (0, 0, 0, s))] * count
            + [pl.BlockSpec((8, LANES), lambda s: (0, 0))],
            scratch_shapes=[pltpu.VMEM((D, step), jnp.float32)],
        )
        return outs, top

    def prepare(act_s, act_f, top_s, top_f, scales, r):
        f = act_s.shape[0]

        def kernel(scale_ref, act_s_ref, act_f_ref, top_s_ref, top_f_ref, *refs):
            bound_ref, fake_ref, *student_refs = refs
            bounds = []
            for net, act_ref, top_ref in ((0, act_s_ref, top_s_ref), (1, act_f_ref, top_f_ref)):
                top = jnp.max(jnp.abs(act_ref[...].astype(jnp.float32)))
                bounds.append(top_ref[...] * (top * scale_ref[net]))
            rows = lax.broadcasted_iota(jnp.int32, (8, LANES), 0)
            bound_ref[...] = jnp.where(rows == 0, *bounds)
            own = act_f_ref[:, pl.ds(first_row(0, r), r)].astype(jnp.float32)
            fake_ref[...] = (own * scale_ref[1]).astype(jnp.bfloat16)
            for j, out_ref in enumerate(student_refs):
                part = act_s_ref[:, pl.ds(first_row(j, r), r)].astype(jnp.float32)
                out_ref[...] = (part * scale_ref[0]).astype(jnp.bfloat16)

        return call(
            kernel,
            [array((8, LANES), jnp.float32)] + [array((f, r), jnp.bfloat16)] * (1 + n_tensor),
            scales, act_s, act_f, top_s, top_f,
            in_specs=[SMEM] + [VMEM] * 4,
            out_specs=[VMEM] * (2 + n_tensor),
            mib=16,
        )

    def multiply_rows(pieces, scaled):
        rows, r = pieces[0].shape
        f = scaled[0].shape[0]
        step = D // (2 * OUTER)
        count = len(pieces)

        def kernel(*refs):
            piece_refs, scaled_refs, out_ref = refs[:count], refs[count:-1], refs[-1]
            total = dot(piece_refs[0][...], scaled_refs[0][...], NT)
            for piece_ref, scaled_ref in zip(piece_refs[1:], scaled_refs[1:]):
                total = total + dot(piece_ref[...], scaled_ref[...], NT)
            out_ref[...] = total

        return call(
            kernel,
            array((rows, f), jnp.float32),
            *pieces, *scaled,
            grid=(rows // step,),
            in_specs=[pl.BlockSpec((step, r), lambda s: (s, 0))] * count
            + [pl.BlockSpec((f, r), lambda s: (0, 0))] * count,
            out_specs=pl.BlockSpec((step, f), lambda s: (s, 0)),
        )

    def multiply_half(other, pieces, scaled):
        _, _, _, r = pieces[0].shape
        f = scaled[0].shape[0]
        count = len(pieces)

        def kernel(*refs):
            piece_refs, scaled_refs, out_ref = refs[:count], refs[count:-1], refs[-1]
            for i in range(inner):
                total = dot(piece_refs[0][0, i], scaled_refs[0][...], NT)
                for piece_ref, scaled_ref in zip(piece_refs[1:], scaled_refs[1:]):
                    total = total + dot(piece_ref[0, i], scaled_ref[...], NT)
                out_ref[i] = total

        return call(
            kernel,
            array((inner, width, f), jnp.float32),
            *pieces, *scaled,
            grid=(1,),
            in_specs=[pl.BlockSpec((1, inner, width, r), lambda s: (other, 0, 0, 0))] * count
            + [pl.BlockSpec((f, r), lambda s: (0, 0))] * count,
            out_specs=pl.BlockSpec((inner, width, f), lambda s: (0, 0, 0)),
        )

    def scale_rows(act, scales):
        def kernel(scale_ref, act_ref, out_ref):
            out_ref[...] = (act_ref[...].astype(jnp.float32) * scale_ref[1]).astype(jnp.bfloat16)

        return call(
            kernel, array(act.shape, jnp.bfloat16), scales, act,
            in_specs=[SMEM, VMEM], out_specs=VMEM,
        )

    def norms(total_s, total_f):
        def kernel(s_ref, f_ref, out_ref):
            sums = [jnp.sum(ref[...] * ref[...]) for ref in (s_ref, f_ref)]
            rows = lax.broadcasted_iota(jnp.int32, (8, LANES), 0)
            out_ref[...] = jnp.where(rows == 0, *sums)

        return call(
            kernel, array((8, LANES), jnp.float32), total_s, total_f,
            in_specs=[VMEM] * 2, out_specs=VMEM,
        )

    def update(squares, totals, states):
        shape = totals[0].shape

        def kernel(squares_ref, *refs):
            total_refs, state_refs, (own_ref, *out_refs) = refs[:2], refs[2:8], refs[8:]
            for net in range(2):
                new = adam_update(
                    total_refs[net][...],
                    squares_ref[net : net + 1, :1],
                    *(ref[...] for ref in state_refs[3 * net : 3 * net + 3]),
                )
                own_ref[net] = new[0].astype(jnp.bfloat16)
                for ref, value in zip(out_refs[3 * net :], new):
                    ref[...] = value

        own, *new = call(
            kernel,
            [array((2, *shape), jnp.bfloat16)] + [array(shape, jnp.float32)] * 6,
            squares, *totals, *states,
            in_specs=[VMEM] * 9,
            out_specs=[VMEM] * 7,
        )
        return own, new

    def back_part(whole, weight, pieces, scales, net, j, low, size, r, count):
        f = weight.shape[0]
        turned = len(pieces) > 1

        def kernel(scale_ref, weight_ref, *refs):
            piece_refs = refs[: len(pieces)]
            if turned:
                out_ref, done_ref, sem, wide_ref = refs[-4:]
                for k in range(OUTER):
                    for other in range(2):
                        for i in range(inner):
                            block = piece_refs[k][other, i].astype(jnp.float32)
                            wide_ref[owner(k, i, other)] = block
                flat = wide_ref[...].reshape(D, size).astype(jnp.bfloat16)
                product = dot(weight_ref[...], flat, NN)
            else:
                out_ref, done_ref, sem = refs[-3:]
                product = dot(weight_ref[...], piece_refs[0][...], NT)
            done_ref[...] = (product * scale_ref[net]).astype(jnp.bfloat16)
            start = pl.multiple_of(first_row(j, r) + low, LANES)
            copy = pltpu.make_async_copy(done_ref, out_ref.at[:, pl.ds(start, size)], sem)
            copy.start()
            copy.wait()

        scratch = [pltpu.VMEM((f, size), jnp.bfloat16), pltpu.SemaphoreType.DMA]
        if turned:
            scratch.append(pltpu.VMEM((n_dp, width, size), jnp.float32))
        operands = [scales, weight, *pieces]
        in_specs = [SMEM] + [VMEM] * (len(operands) - 1)
        aliases = {}
        if whole is not None:
            aliases = {len(operands): 0}
            operands.append(whole)
            in_specs.append(ANY)
        return call(
            kernel, array((f, count), jnp.bfloat16), *operands,
            in_specs=in_specs, out_specs=ANY, scratch_shapes=scratch,
            input_output_aliases=aliases, mib=20,
        )

    def spread(stacks, net):
        count, _, _, f = stacks[0].shape

        def kernel(*refs):
            stack_refs, (out_ref, wide_ref) = refs[:4], refs[4:]
            lanes = lax.broadcasted_iota(jnp.int32, (width, LANES), 1)
            inside = lanes + pl.program_id(0) * LANES < f
            for n, ref in enumerate(stack_refs):
                for at in range(count):
                    k, i = divmod((n & 1) * count + at, inner)
                    block = jnp.where(inside, ref[at, 0].astype(jnp.float32), 0.0)
                    wide_ref[owner(k, i, n >> 1)] = block
            flat = wide_ref[...].reshape(D, LANES).astype(jnp.bfloat16)
            out_ref[...] = dot(identity(LANES), flat, NT).astype(jnp.bfloat16)

        return call(
            kernel, array((f, D), jnp.bfloat16), *stacks,
            grid=(pl.cdiv(f, LANES),),
            in_specs=[pl.BlockSpec((count, 1, width, LANES), lambda s: (0, net, 0, s))] * 4,
            out_specs=pl.BlockSpec((LANES, D), lambda s: (s, 0)),
            scratch_shapes=[pltpu.VMEM((n_dp, width, LANES), jnp.float32)],
        )

    def per_device(
        cot_student, cot_fake, act_student, act_fake, weight_student, weight_fake,
        master_student, first_student, second_student, master_fake, first_fake, second_fake,
        timesteps,
    ):
        f, count = act_student.shape
        r = cot_student.shape[0]
        assert timesteps.shape[2] == 1 and count == ROWS

        token = []

        def step(work, *inputs):
            if token:
                *inputs, _ = lax.optimization_barrier((*inputs, token[0]))
            out = work(*inputs)
            token[:] = jax.tree.leaves(out)[:1]
            return out

        def reduced(combine, value, got):
            return step(lambda *values: functools.reduce(combine, values), value, *got)

        def gather_planes(value):
            return [to_plane(value, k) for k in range(1, OUTER)]

        def gather_chips(value):
            return [
                move_dp(value, lambda z, m, c, i=i, o=o: (z, (m + i) & (inner - 1), c ^ o))
                for i in range(inner)
                for o in range(2)
                if i or o
            ]

        acts = [from_tensor(act, -j) for j, act in enumerate(step(lambda act: cut_acts(act, r), act_fake), 1)]
        planes, top_student = step(lambda cot: turn(cot, True), cot_student)
        order = (3, 1, 2, 0)
        others = {k: [from_tensor(planes[k], j) for j in range(1, n_tensor)] for k in order}
        cores, top_fake = step(lambda cot: turn(cot, False), cot_fake)
        cores = [core.reshape(-1, r) for core in cores]

        scales = step(
            lambda steps: 1.0 / (0.1 + steps.astype(jnp.float32) / 1000.0), timesteps[0, :, 0]
        )
        bounds, scaled, *scaled_student = step(
            lambda *values: prepare(*values, r),
            act_student, act_fake, top_student, top_fake, scales,
        )
        got = gather_planes(bounds)
        sends, keeps = [], []
        for j in range(n_tensor):
            if j:
                scaled = step(scale_rows, acts[j - 1], scales)
            sends.append(to_core(step(lambda a, b: multiply_rows([a], [b]), cores[1], scaled)))
            keeps.append(step(lambda a, b: multiply_rows([a], [b]), cores[0], scaled))
        bounds = reduced(jnp.maximum, bounds, got)
        bounds = reduced(jnp.maximum, bounds, gather_chips(bounds))

        def factors(bounds):
            bounds = jnp.maximum(bounds, 1e-30) * (1.01 * count * n_dp / HALF_LIMIT)
            return bounds[:2, 0], 1.0 / bounds[:2, 0]

        grow, fit = step(factors, bounds)

        def shrink(value, net):
            return (value * fit[net]).astype(jnp.float16)

        def widen(value, net):
            return value.astype(jnp.float32) * grow[net]

        halves = ((2, 3), (0, 1))

        def fake_middle(keep, send):
            both = (keep + send).reshape(inner, OUTER, width, f)
            sent = [
                [shrink(both[i, lo : hi + 1], 1) for i in range(1, inner)] for lo, hi in halves
            ]
            return sent, [both[0, lo : hi + 1] for lo, hi in halves]

        def start_middle(keep, send):
            sent, mine = step(fake_middle, keep, send)
            return [
                (own, [to_middle(value, i) for i, value in enumerate(values, 1)])
                for own, values in zip(mine, sent)
            ]

        kept, crossing, to_sum = {}, {}, []

        def multiply(k):
            def half(other, *operands):
                pieces, scaled = operands[:n_tensor], operands[n_tensor:]
                return multiply_half(other, pieces, scaled)

            operands = [planes[k], *others[k], *scaled_student]
            send = to_core(step(functools.partial(half, 1), *operands))
            kept[k] = step(functools.partial(half, 0), *operands), send

        def cross_middle(k):
            def work(keep, send):
                both = keep + send
                return [shrink(both[i], 0) for i in range(1, inner)], both[0]

            sent, own = step(work, *kept[k])
            crossing[k] = own, [to_middle(value, i) for i, value in enumerate(sent, 1)]

        def cross_planes(k):
            def work(own, *got):
                for value in got:
                    own = own + widen(value, 0)
                return shrink(own, 0) if k else own

            own, got = crossing[k]
            value = step(work, own, *got)
            to_sum.append(to_plane(value, k) if k else value)

        fake_sums = [[] for _ in range(n_tensor)]

        def fake_planes(j, part):
            lo, hi = halves[part]

            def work(own, *got):
                for value in got:
                    own = own + widen(value, 1)
                return [shrink(own[k - lo], 1) if k else own[0] for k in range(hi, lo - 1, -1)]

            own, got = middles[j][part]
            values = step(work, own, *got)
            for k, value in zip(range(hi, lo - 1, -1), values):
                fake_sums[j].append(to_plane(value, k) if k else value)

        def fake_total(j):
            def work(*values):
                total = values[-1]
                for value in values[:-1]:
                    total = total + widen(value, 1)
                return total

            return step(work, *fake_sums[j])

        def back(whole, net, pieces, j, low, size):
            weight = (weight_student, weight_fake)[net]
            has = [] if whole is None else [whole]

            def work(weight, *values):
                return back_part(
                    values[-1] if has else None, weight, values[: len(pieces)], scales,
                    net, j, low, size, r, count,
                )

            return step(work, weight, *pieces, *has)

        multiply(3)
        middles = [start_middle(keep, send) for keep, send in zip(keeps, sends)]
        fake_planes(0, 0)
        fake_planes(0, 1)
        back_student = back(None, 0, [cot_student], 0, 0, r)
        multiply(1)
        cross_middle(3)
        for j in range(1, n_tensor):
            fake_planes(j, 0)
        back_fake = back(None, 1, [cot_fake], 0, 0, r)
        for j in range(1, n_tensor):
            fake_planes(j, 1)
        multiply(2)
        cross_middle(1)
        cross_planes(3)
        fake_others = [fake_total(j) for j in range(1, n_tensor)]
        fake_got = [from_tensor(value, j) for j, value in enumerate(fake_others, 1)]

        part = r // 4
        cuts = ((0, part), (part, 3 * part), (3 * part, r)) if part % LANES == 0 else ((0, r),)
        raw = []

        def send_raw(lo, hi):
            rows = step(lambda cot: cot[lo:hi], cot_fake)
            raw.append([from_tensor(rows, j) for j in range(1, n_tensor)])

        send_raw(*cuts[0])
        cross_middle(2)
        cross_planes(1)
        fake_mine = fake_total(0)
        cross_planes(2)
        multiply(0)
        cross_middle(0)

        def student_partial(*values):
            total = widen(values[0], 0)
            for value in values[1:]:
                total = total + widen(value, 0)
            return total

        total_student = step(student_partial, *to_sum)
        to_sum.clear()
        total_fake = reduced(jnp.add, fake_mine, fake_got)
        cross_planes(0)
        total_student = reduced(jnp.add, total_student, to_sum)
        squares = step(norms, total_student, total_fake)
        squares = reduced(jnp.add, squares, gather_planes(squares))
        squares = reduced(jnp.add, squares, gather_chips(squares))
        got = [from_tensor(squares, j) for j in range(1, n_tensor)]
        for lo, hi in cuts[1:]:
            send_raw(lo, hi)

        def back_raw(n):
            nonlocal back_fake
            lo, hi = cuts[n]
            for j in range(1, n_tensor):
                back_fake = back(back_fake, 1, [raw[n][j - 1]], j, lo, hi - lo)

        back_raw(0)
        squares = reduced(jnp.add, squares, got)

        states = (
            master_student, first_student, second_student, master_fake, first_fake, second_fake,
        )
        own, updated = step(
            lambda squares, *values: update(squares, values[:2], values[2:]),
            squares, total_student, total_fake, *(state.T for state in states),
        )

        mine = {}

        def spread_middle(k, value):
            mine[k] = [value] + [to_middle(value, -i) for i in range(1, inner)]

        planes_got = {k: to_plane(own, -k) for k in (1, 3, 2)}
        spread_middle(0, own)
        for j in range(1, n_tensor):
            pieces = [others[k][j - 1] for k in range(OUTER)]
            back_student = back(back_student, 0, pieces, j, 0, r)
        spread_middle(1, step(lambda value: value, planes_got[1]))
        spread_middle(3, step(lambda value: value, planes_got[3]))

        first_half = step(lambda *values: jnp.stack(values), *mine[0], *mine[1])
        theirs = [to_core(first_half)]
        spread_middle(2, step(lambda value: value, planes_got[2]))
        second_half = step(lambda *values: jnp.stack(values), *mine[2], *mine[3])
        theirs.append(to_core(second_half))
        for n in range(1, len(cuts)):
            back_raw(n)
        stacks = [first_half, second_half, *theirs]
        params = [step(lambda *values: spread(values, n), *stacks) for n in range(2)]

        new_states = [value.T for value in updated]
        return (back_student, back_fake, *new_states, *params)

    placed = (
        P(("dp", "tensor"), None),
        P(("dp", "tensor"), None),
        P("tensor", "dp"),
        P("tensor", "dp"),
        P("tensor", None),
        P("tensor", None),
        P("tensor", "dp"),
        P("tensor", "dp"),
        P("tensor", "dp"),
        P("tensor", "dp"),
        P("tensor", "dp"),
        P("tensor", "dp"),
        P("dp", None, None),
    )
    return jax.shard_map(
        per_device,
        mesh=mesh,
        in_specs=placed,
        out_specs=(
            P("tensor", "dp"),
            P("tensor", "dp"),
            P("tensor", "dp"),
            P("tensor", "dp"),
            P("tensor", "dp"),
            P("tensor", "dp"),
            P("tensor", "dp"),
            P("tensor", "dp"),
            P("tensor", None),
            P("tensor", None),
        ),
        check_vma=False,
    )
```

```python
import functools

import jax
import jax.numpy as jnp
from jax import lax
from jax.experimental import pallas as pl
from jax.experimental.pallas import tpu as pltpu
from jax.sharding import PartitionSpec as P

D = 2432
F = 1216
ROWS = 1024


FIRST_CORRECTION = 0.9999734386011124
SECOND_CORRECTION = 0.0952078529183

OUTER = 4
HALF_LIMIT = 60000.0
TILE = 256
LANES = 128

NT = (((1,), (1,)), ((), ()))
NN = (((1,), (0,)), ((), ()))

SMEM = pl.BlockSpec(memory_space=pltpu.SMEM)
VMEM = pl.BlockSpec(memory_space=pltpu.VMEM)
ANY = pl.BlockSpec(memory_space=pl.ANY)


def adam_update(grad, squares, master, first, second):
    clip = jnp.minimum(1.0, jnp.sqrt(jnp.float32(D * F)) / jnp.sqrt(squares + 1e-06))
    clipped = grad * clip
    new_first = 0.9 * first + 0.1 * clipped
    new_second = 0.999 * second + 0.001 * clipped * clipped
    step_dir = new_first / FIRST_CORRECTION / (jnp.sqrt(new_second / SECOND_CORRECTION) + 1e-08)
    new_master = master * (1.0 - 0.01 * 0.01) - 0.01 * step_dir
    return (new_master, new_first, new_second)


def dot(a, b, dims):
    return lax.dot_general(a, b, dims, preferred_element_type=jnp.float32)


def identity(size):
    rows = lax.broadcasted_iota(jnp.int32, (size, size), 0)
    cols = lax.broadcasted_iota(jnp.int32, (size, size), 1)
    return jnp.where(rows == cols, 1.0, 0.0).astype(jnp.bfloat16)


def array(shape, dtype):
    return jax.ShapeDtypeStruct(shape, dtype)


def call(kernel, out_shape, *operands, mib=12, **kwargs):
    return pl.pallas_call(
        kernel,
        out_shape=out_shape,
        compiler_params=pltpu.CompilerParams(vmem_limit_bytes=mib * 1024 * 1024),
        cost_estimate=pl.CostEstimate(flops=100 * 10**9, bytes_accessed=0, transcendentals=0),
        **kwargs,
    )(*operands)


def solution(mesh):
    n_dp, n_tensor = mesh.shape["dp"], mesh.shape["tensor"]
    inner = n_dp // (2 * OUTER)
    width = D // n_dp

    def split(p):
        return (p >> inner.bit_length()) & (OUTER - 1), (p >> 1) & (inner - 1), p & 1

    def join(z, m, c):
        return (z * inner + m) * 2 + c

    def move_dp(value, where):
        perm = [(p, join(*where(*split(p)))) for p in range(n_dp)]
        return lax.ppermute(value, "dp", perm)

    def to_plane(value, k):
        return move_dp(value, lambda z, m, c: ((z + k) & (OUTER - 1), m, c))

    def to_middle(value, k):
        return move_dp(value, lambda z, m, c: (z, (m + k) & (inner - 1), c))

    def to_core(value):
        return move_dp(value, lambda z, m, c: (z, m, 1 - c))

    def from_tensor(value, k):
        perm = [(s, (s - k) & (n_tensor - 1)) for s in range(n_tensor)]
        return lax.ppermute(value, "tensor", perm)

    def my_place():
        return split(lax.axis_index("dp"))

    def relative(p):
        z, m, c = split(p)
        my_z, my_m, my_c = my_place()
        return (z - my_z) & (OUTER - 1), (m - my_m) & (inner - 1), c ^ my_c

    def owner(k, i, other):
        z, m, c = my_place()
        return join((z + k) & (OUTER - 1), (m + i) & (inner - 1), c ^ other)

    def first_row(j, r):
        start = ((lax.axis_index("tensor") + j) & (n_tensor - 1)) * r
        return pl.multiple_of(start, LANES)

    def cut_acts(act, r):
        count = n_tensor - 1

        def kernel(act_ref, *refs):
            out_refs, sem = refs[:-1], refs[-1]
            copies = [
                pltpu.make_async_copy(
                    act_ref.at[:, pl.ds(first_row(j + 1, r), r)], out_refs[j], sem.at[j]
                )
                for j in range(count)
            ]
            for copy in copies:
                copy.start()
            for copy in copies:
                copy.wait()

        return call(
            kernel,
            [array((act.shape[0], r), act.dtype)] * count,
            act,
            in_specs=[ANY],
            out_specs=[VMEM] * count,
            scratch_shapes=[pltpu.SemaphoreType.DMA((count,))],
        )

    def turn(cot, by_planes):
        r = cot.shape[0]
        step = min(r, TILE)
        count = 2
        lead = (2, 2, inner) if by_planes else (inner, OUTER)

        def kernel(cot_ref, *refs):
            out_refs, (top_ref, wide_ref) = refs[:count], refs[count:]
            eye = identity(TILE)
            for start in range(0, D, TILE):
                size = min(TILE, D - start)
                wide_ref[start : start + size, :] = dot(
                    eye[:size, :size], cot_ref[:, start : start + size], NT
                )
            top = jnp.max(jnp.abs(wide_ref[...]).reshape(D // 8, 8, step), axis=0)
            top = jnp.broadcast_to(jnp.max(top), (8, LANES))

            @pl.when(pl.program_id(0) == 0)
            def _():
                top_ref[...] = top

            @pl.when(pl.program_id(0) > 0)
            def _():
                top_ref[...] = jnp.maximum(top_ref[...], top)

            for p in range(n_dp):
                k, i, other = relative(p)
                block = wide_ref[p * width : (p + 1) * width, :].astype(jnp.bfloat16)
                which, at = (1 - (k >> 1), (1 - (k & 1), other, i)) if by_planes else (other, (i, k))
                for n in range(count):

                    @pl.when(which == n)
                    def _(n=n, at=at, block=block):
                        out_refs[n][at] = block

        *outs, top = call(
            kernel,
            [array((*lead, width, r), jnp.bfloat16)] * count + [array((8, LANES), jnp.float32)],
            cot,
            grid=(r // step,),
            in_specs=[pl.BlockSpec((step, D), lambda s: (s, 0))],
            out_specs=[
                pl.BlockSpec((*lead, width, step), lambda s: (*(0 for _ in lead), 0, s))
            ] * count
            + [pl.BlockSpec((8, LANES), lambda s: (0, 0))],
            scratch_shapes=[pltpu.VMEM((D, step), jnp.float32)],
        )
        return outs, top

    def prepare(act_s, act_f, top_s, top_f, scales, r):
        f = act_s.shape[0]

        def kernel(scale_ref, act_s_ref, act_f_ref, top_s_ref, top_f_ref, *refs):
            bound_ref, fake_ref, *student_refs = refs
            bounds = []
            for net, act_ref, top_ref in ((0, act_s_ref, top_s_ref), (1, act_f_ref, top_f_ref)):
                top = jnp.max(jnp.abs(act_ref[...].astype(jnp.float32)))
                bounds.append(top_ref[...] * (top * scale_ref[net]))
            rows = lax.broadcasted_iota(jnp.int32, (8, LANES), 0)
            bound_ref[...] = jnp.where(rows == 0, *bounds)
            own = act_f_ref[:, pl.ds(first_row(0, r), r)].astype(jnp.float32)
            fake_ref[...] = (own * scale_ref[1]).astype(jnp.bfloat16)
            for j, out_ref in enumerate(student_refs):
                part = act_s_ref[:, pl.ds(first_row(j, r), r)].astype(jnp.float32)
                out_ref[...] = (part * scale_ref[0]).astype(jnp.bfloat16)

        return call(
            kernel,
            [array((8, LANES), jnp.float32)] + [array((f, r), jnp.bfloat16)] * (1 + n_tensor),
            scales, act_s, act_f, top_s, top_f,
            in_specs=[SMEM] + [VMEM] * 4,
            out_specs=[VMEM] * (2 + n_tensor),
            mib=16,
        )

    def multiply_rows(pieces, scaled):
        rows, r = pieces[0].shape
        f = scaled[0].shape[0]
        step = D // (2 * OUTER)
        count = len(pieces)

        def kernel(*refs):
            piece_refs, scaled_refs, out_ref = refs[:count], refs[count:-1], refs[-1]
            total = dot(piece_refs[0][...], scaled_refs[0][...], NT)
            for piece_ref, scaled_ref in zip(piece_refs[1:], scaled_refs[1:]):
                total = total + dot(piece_ref[...], scaled_ref[...], NT)
            out_ref[...] = total

        return call(
            kernel,
            array((rows, f), jnp.float32),
            *pieces, *scaled,
            grid=(rows // step,),
            in_specs=[pl.BlockSpec((step, r), lambda s: (s, 0))] * count
            + [pl.BlockSpec((f, r), lambda s: (0, 0))] * count,
            out_specs=pl.BlockSpec((step, f), lambda s: (s, 0)),
        )

    def multiply_half(other, pieces, scaled):
        r, f = pieces[0].shape[-1], scaled[0].shape[0]
        count = len(pieces)

        def kernel(*refs):
            piece_refs, scaled_refs, out_ref = refs[:count], refs[count:-1], refs[-1]
            for i in range(inner):
                total = dot(piece_refs[0][0, 0, i], scaled_refs[0][...], NT)
                for piece_ref, scaled_ref in zip(piece_refs[1:], scaled_refs[1:]):
                    total = total + dot(piece_ref[0, 0, i], scaled_ref[...], NT)
                out_ref[0, i] = total

        return call(
            kernel,
            array((2, inner, width, f), jnp.float32),
            *pieces, *scaled,
            grid=(2,),
            in_specs=[pl.BlockSpec((1, 1, inner, width, r), lambda s: (s, other, 0, 0, 0))] * count
            + [pl.BlockSpec((f, r), lambda s: (0, 0))] * count,
            out_specs=pl.BlockSpec((1, inner, width, f), lambda s: (s, 0, 0, 0)),
        )

    def scale_rows(act, scales):
        def kernel(scale_ref, act_ref, out_ref):
            out_ref[...] = (act_ref[...].astype(jnp.float32) * scale_ref[1]).astype(jnp.bfloat16)

        return call(
            kernel, array(act.shape, jnp.bfloat16), scales, act,
            in_specs=[SMEM, VMEM], out_specs=VMEM,
        )

    def norms(total_s, total_f):
        def kernel(s_ref, f_ref, out_ref):
            sums = [jnp.sum(ref[...] * ref[...]) for ref in (s_ref, f_ref)]
            rows = lax.broadcasted_iota(jnp.int32, (8, LANES), 0)
            out_ref[...] = jnp.where(rows == 0, *sums)

        return call(
            kernel, array((8, LANES), jnp.float32), total_s, total_f,
            in_specs=[VMEM] * 2, out_specs=VMEM,
        )

    def update(squares, totals, states):
        shape = totals[0].shape

        def kernel(squares_ref, *refs):
            total_refs, state_refs, (own_ref, *out_refs) = refs[:2], refs[2:8], refs[8:]
            for net in range(2):
                new = adam_update(
                    total_refs[net][...],
                    squares_ref[net : net + 1, :1],
                    *(ref[...] for ref in state_refs[3 * net : 3 * net + 3]),
                )
                own_ref[net] = new[0].astype(jnp.bfloat16)
                for ref, value in zip(out_refs[3 * net :], new):
                    ref[...] = value

        own, *new = call(
            kernel,
            [array((2, *shape), jnp.bfloat16)] + [array(shape, jnp.float32)] * 6,
            squares, *totals, *states,
            in_specs=[VMEM] * 9,
            out_specs=[VMEM] * 7,
        )
        return own, new

    def back_part(whole, weight, pieces, scales, net, j, low, size, r, count):
        f = weight.shape[0]
        turned = len(pieces) > 1

        def kernel(scale_ref, weight_ref, *refs):
            piece_refs = refs[: len(pieces)]
            if turned:
                out_ref, done_ref, sem, wide_ref = refs[-4:]
                for k in range(OUTER):
                    for other in range(2):
                        for i in range(inner):
                            block = piece_refs[1 - (k >> 1)][1 - (k & 1), other, i]
                            block = block.astype(jnp.float32)
                            wide_ref[owner(k, i, other)] = block
                flat = wide_ref[...].reshape(D, size).astype(jnp.bfloat16)
                product = dot(weight_ref[...], flat, NN)
            else:
                out_ref, done_ref, sem = refs[-3:]
                product = dot(weight_ref[...], piece_refs[0][...], NT)
            done_ref[...] = (product * scale_ref[net]).astype(jnp.bfloat16)
            start = pl.multiple_of(first_row(j, r) + low, LANES)
            copy = pltpu.make_async_copy(done_ref, out_ref.at[:, pl.ds(start, size)], sem)
            copy.start()
            copy.wait()

        scratch = [pltpu.VMEM((f, size), jnp.bfloat16), pltpu.SemaphoreType.DMA]
        if turned:
            scratch.append(pltpu.VMEM((n_dp, width, size), jnp.float32))
        operands = [scales, weight, *pieces]
        in_specs = [SMEM] + [VMEM] * (len(operands) - 1)
        aliases = {}
        if whole is not None:
            aliases = {len(operands): 0}
            operands.append(whole)
            in_specs.append(ANY)
        return call(
            kernel, array((f, count), jnp.bfloat16), *operands,
            in_specs=in_specs, out_specs=ANY, scratch_shapes=scratch,
            input_output_aliases=aliases, mib=20,
        )

    def spread(stacks, net):
        count, _, _, f = stacks[0].shape

        def kernel(*refs):
            stack_refs, (out_ref, wide_ref) = refs[:4], refs[4:]
            lanes = lax.broadcasted_iota(jnp.int32, (width, LANES), 1)
            inside = lanes + pl.program_id(0) * LANES < f
            for n, ref in enumerate(stack_refs):
                for at in range(count):
                    k, i = divmod((n & 1) * count + at, inner)
                    block = jnp.where(inside, ref[at, 0].astype(jnp.float32), 0.0)
                    wide_ref[owner(k, i, n >> 1)] = block
            flat = wide_ref[...].reshape(D, LANES).astype(jnp.bfloat16)
            out_ref[...] = dot(identity(LANES), flat, NT).astype(jnp.bfloat16)

        return call(
            kernel, array((f, D), jnp.bfloat16), *stacks,
            grid=(pl.cdiv(f, LANES),),
            in_specs=[pl.BlockSpec((count, 1, width, LANES), lambda s: (0, net, 0, s))] * 4,
            out_specs=pl.BlockSpec((LANES, D), lambda s: (s, 0)),
            scratch_shapes=[pltpu.VMEM((n_dp, width, LANES), jnp.float32)],
        )

    def per_device(
        cot_student, cot_fake, act_student, act_fake, weight_student, weight_fake,
        master_student, first_student, second_student, master_fake, first_fake, second_fake,
        timesteps,
    ):
        f, count = act_student.shape
        r = cot_student.shape[0]
        assert timesteps.shape[2] == 1 and count == ROWS

        token = []

        def step(work, *inputs):
            if token:
                *inputs, _ = lax.optimization_barrier((*inputs, token[0]))
            out = work(*inputs)
            token[:] = jax.tree.leaves(out)[:1]
            return out

        def reduced(combine, value, got):
            return step(lambda *values: functools.reduce(combine, values), value, *got)

        def gather_planes(value):
            return [to_plane(value, k) for k in range(1, OUTER)]

        def gather_chips(value):
            return [
                move_dp(value, lambda z, m, c, i=i, o=o: (z, (m + i) & (inner - 1), c ^ o))
                for i in range(inner)
                for o in range(2)
                if i or o
            ]

        acts = [from_tensor(act, -j) for j, act in enumerate(step(lambda a: cut_acts(a, r), act_fake), 1)]
        planes, top_student = step(lambda cot: turn(cot, True), cot_student)
        others = [[from_tensor(planes[0], j) for j in range(1, n_tensor)]]
        cores, top_fake = step(lambda cot: turn(cot, False), cot_fake)
        cores = [core.reshape(-1, r) for core in cores]

        scales = step(
            lambda steps: 1.0 / (0.1 + steps.astype(jnp.float32) / 1000.0), timesteps[0, :, 0]
        )
        bounds, scaled, *scaled_student = step(
            lambda *values: prepare(*values, r),
            act_student, act_fake, top_student, top_fake, scales,
        )
        pairs = []
        got = gather_planes(bounds)
        scaled_fake = [scaled] + [step(scale_rows, act, scales) for act in acts]
        bounds = reduced(jnp.maximum, bounds, got)
        got = gather_chips(bounds)
        for scaled in scaled_fake:
            send = to_core(step(lambda a, b: multiply_rows([a], [b]), cores[1], scaled))
            keep = step(lambda a, b: multiply_rows([a], [b]), cores[0], scaled)
            if not pairs:
                bounds = reduced(jnp.maximum, bounds, got)
            pairs.append((keep, send))

        def factors(bounds):
            bounds = jnp.maximum(bounds, 1e-30) * (1.01 * count * n_dp / HALF_LIMIT)
            return bounds[:2, 0], 1.0 / bounds[:2, 0]

        grow, fit = step(factors, bounds)

        def shrink(value, net):
            return (value * fit[net]).astype(jnp.float16)

        def widen(value, net):
            return value.astype(jnp.float32) * grow[net]

        def add_widened(total, values, net):
            for value in values:
                total = total + widen(value, net)
            return total

        def fake_middle(keep, send):
            both = (keep + send).reshape(inner, OUTER, width, f)
            return [shrink(both[i], 1) for i in range(1, inner)], both[0]

        middles = []
        for keep, send in pairs:
            sent, own = step(fake_middle, keep, send)
            middles.append((own, [to_middle(value, i) for i, value in enumerate(sent, 1)]))

        def back(whole, net, pieces, j, low, size):
            weight = (weight_student, weight_fake)[net]
            has = [] if whole is None else [whole]

            def work(weight, *values):
                return back_part(
                    values[-1] if has else None, weight, values[: len(pieces)], scales,
                    net, j, low, size, r, count,
                )

            return step(work, weight, *pieces, *has)

        fake_sums = {}

        def fake_planes(j):
            def work(own, *got):
                own = add_widened(own, got, 1)
                return [shrink(own[k], 1) for k in (3, 1, 2)], own[0]

            sent, own = step(work, middles[j][0], *middles[j][1])
            fake_sums[j] = own, [to_plane(value, k) for k, value in zip((3, 1, 2), sent)]

        def fake_total(j):
            own, got = fake_sums[j]
            return step(lambda own, *got: add_widened(own, got, 1), own, *got)

        kept = {}

        def multiply(n):
            def half(other, *operands):
                return multiply_half(other, operands[:n_tensor], operands[n_tensor:])

            operands = [planes[n], *others[n], *scaled_student]
            send = to_core(step(functools.partial(half, 1), *operands))
            kept[n] = step(functools.partial(half, 0), *operands), send

        second = step(lambda value: value, planes[1])
        others.append([from_tensor(second, j) for j in range(1, n_tensor)])
        back_student = back(None, 0, [cot_student], 0, 0, r)
        back_fake = back(None, 1, [cot_fake], 0, 0, r)
        multiply(0)
        fake_planes(0)

        def first_middle(keep, send):
            both = keep + send
            return [shrink(both[:, i], 0) for i in range(1, inner)], both[:, 0]

        sent, own = step(first_middle, *kept[0])
        got = [to_middle(value, i) for i, value in enumerate(sent, 1)]
        fake_mine = fake_total(0)
        for j in range(1, n_tensor):
            fake_planes(j)

        def first_planes(own, *got):
            own = add_widened(own, got, 0)
            return shrink(own[0], 0), shrink(own[1], 0)

        sent = step(first_planes, own, *got)
        first_got = [to_plane(value, k) for k, value in zip((3, 2), sent)]
        fake_others = [fake_total(j) for j in range(1, n_tensor)]
        fake_got = [from_tensor(value, j) for j, value in enumerate(fake_others, 1)]
        multiply(1)

        def second_middle(keep, send):
            both = keep + send
            sent = [[shrink(both[n, i], 0) for i in range(1, inner)] for n in range(2)]
            return sent, both[0, 0], both[1, 0]

        sent, own_next, own = step(second_middle, *kept[1])
        got_next, got = (
            [to_middle(value, i) for i, value in enumerate(values, 1)] for values in sent
        )
        next_sent = step(
            lambda own, *got: shrink(add_widened(own, got, 0), 0), own_next, *got_next
        )
        next_got = to_plane(next_sent, 1)
        total_fake = reduced(jnp.add, fake_mine, fake_got)
        total_student = step(
            lambda own, *got: add_widened(own, got, 0), own, *got, *first_got
        )
        total_student = step(
            lambda own, *got: add_widened(own, got, 0), total_student, next_got
        )
        squares = step(norms, total_student, total_fake)
        squares = reduced(
            jnp.add, squares, [from_tensor(squares, j) for j in range(1, n_tensor)]
        )

        raw_sent = step(lambda cot: cot, cot_fake)
        raw = [from_tensor(raw_sent, j) for j in range(1, n_tensor)]
        squares = reduced(jnp.add, squares, gather_planes(squares))
        squares = reduced(jnp.add, squares, gather_chips(squares))

        states = (
            master_student, first_student, second_student, master_fake, first_fake, second_fake,
        )
        own, updated = step(
            lambda squares, *values: update(squares, values[:2], values[2:]),
            squares, total_student, total_fake, *(state.T for state in states),
        )

        mine = {}

        def spread_middle(k, value):
            mine[k] = [value] + [to_middle(value, -i) for i in range(1, inner)]

        spread_middle(0, own)
        planes_got = {k: to_plane(own, -k) for k in (1, 3, 2)}
        for j in range(1, n_tensor):
            pieces = [group[j - 1] for group in others]
            back_student = back(back_student, 0, pieces, j, 0, r)
        spread_middle(1, step(lambda value: value, planes_got[1]))
        spread_middle(3, step(lambda value: value, planes_got[3]))
        first_half = step(lambda *values: jnp.stack(values), *mine[0], *mine[1])
        theirs = [to_core(first_half)]
        spread_middle(2, step(lambda value: value, planes_got[2]))
        second_half = step(lambda *values: jnp.stack(values), *mine[2], *mine[3])
        theirs.append(to_core(second_half))
        for j in range(1, n_tensor):
            back_fake = back(back_fake, 1, [raw[j - 1]], j, 0, r)
        stacks = [first_half, second_half, *theirs]
        params = [step(lambda *values: spread(values, n), *stacks) for n in range(2)]

        new_states = [value.T for value in updated]
        return (back_student, back_fake, *new_states, *params)

    placed = (
        P(("dp", "tensor"), None),
        P(("dp", "tensor"), None),
        P("tensor", "dp"),
        P("tensor", "dp"),
        P("tensor", None),
        P("tensor", None),
        P("tensor", "dp"),
        P("tensor", "dp"),
        P("tensor", "dp"),
        P("tensor", "dp"),
        P("tensor", "dp"),
        P("tensor", "dp"),
        P("dp", None, None),
    )
    return jax.shard_map(
        per_device,
        mesh=mesh,
        in_specs=placed,
        out_specs=(
            P("tensor", "dp"),
            P("tensor", "dp"),
            P("tensor", "dp"),
            P("tensor", "dp"),
            P("tensor", "dp"),
            P("tensor", "dp"),
            P("tensor", "dp"),
            P("tensor", "dp"),
            P("tensor", None),
            P("tensor", None),
        ),
        check_vma=False,
    )
```

```python
import functools

import jax
import jax.numpy as jnp
from jax import lax
from jax.experimental import pallas as pl
from jax.experimental.pallas import tpu as pltpu
from jax.sharding import PartitionSpec as P

D = 2432
F = 1216
ROWS = 1024


FIRST_CORRECTION = 0.9999734386011124
SECOND_CORRECTION = 0.0952078529183

OUTER = 4
HALF_LIMIT = 60000.0
TILE = 256
LANES = 128

NT = (((1,), (1,)), ((), ()))
NN = (((1,), (0,)), ((), ()))

SMEM = pl.BlockSpec(memory_space=pltpu.SMEM)
VMEM = pl.BlockSpec(memory_space=pltpu.VMEM)
ANY = pl.BlockSpec(memory_space=pl.ANY)


def adam_update(grad, squares, master, first, second):
    clip = jnp.minimum(1.0, jnp.sqrt(jnp.float32(D * F)) / jnp.sqrt(squares + 1e-06))
    clipped = grad * clip
    new_first = 0.9 * first + 0.1 * clipped
    new_second = 0.999 * second + 0.001 * clipped * clipped
    step_dir = new_first / FIRST_CORRECTION / (jnp.sqrt(new_second / SECOND_CORRECTION) + 1e-08)
    new_master = master * (1.0 - 0.01 * 0.01) - 0.01 * step_dir
    return (new_master, new_first, new_second)


def dot(a, b, dims):
    return lax.dot_general(a, b, dims, preferred_element_type=jnp.float32)


def identity(size):
    rows = lax.broadcasted_iota(jnp.int32, (size, size), 0)
    cols = lax.broadcasted_iota(jnp.int32, (size, size), 1)
    return jnp.where(rows == cols, 1.0, 0.0).astype(jnp.bfloat16)


def array(shape, dtype):
    return jax.ShapeDtypeStruct(shape, dtype)


def call(kernel, out_shape, *operands, mib=12, **kwargs):
    return pl.pallas_call(
        kernel,
        out_shape=out_shape,
        compiler_params=pltpu.CompilerParams(vmem_limit_bytes=mib * 1024 * 1024),
        cost_estimate=pl.CostEstimate(flops=100 * 10**9, bytes_accessed=0, transcendentals=0),
        **kwargs,
    )(*operands)


def solution(mesh):
    n_dp, n_tensor = mesh.shape["dp"], mesh.shape["tensor"]
    inner = n_dp // (2 * OUTER)
    width = D // n_dp

    def split(p):
        return (p >> inner.bit_length()) & (OUTER - 1), (p >> 1) & (inner - 1), p & 1

    def join(z, m, c):
        return (z * inner + m) * 2 + c

    def move_dp(value, where):
        perm = [(p, join(*where(*split(p)))) for p in range(n_dp)]
        return lax.ppermute(value, "dp", perm)

    def to_plane(value, k):
        return move_dp(value, lambda z, m, c: ((z + k) & (OUTER - 1), m, c))

    def to_middle(value, k):
        return move_dp(value, lambda z, m, c: (z, (m + k) & (inner - 1), c))

    def to_core(value):
        return move_dp(value, lambda z, m, c: (z, m, 1 - c))

    def from_tensor(value, k):
        perm = [(s, (s - k) & (n_tensor - 1)) for s in range(n_tensor)]
        return lax.ppermute(value, "tensor", perm)

    def from_diagonal(value, k):
        perm = []
        for p in range(n_dp):
            z, m, c = split(p)
            for t in range(n_tensor):
                target = join(z, m, 1 - c) * n_tensor + ((t - k) & (n_tensor - 1))
                perm.append((p * n_tensor + t, target))
        return lax.ppermute(value, ("dp", "tensor"), perm)

    def my_place():
        return split(lax.axis_index("dp"))

    def relative(p):
        z, m, c = split(p)
        my_z, my_m, my_c = my_place()
        return (z - my_z) & (OUTER - 1), (m - my_m) & (inner - 1), c ^ my_c

    def owner(k, i, other):
        z, m, c = my_place()
        return join((z + k) & (OUTER - 1), (m + i) & (inner - 1), c ^ other)

    def first_row(j, r):
        start = ((lax.axis_index("tensor") + j) & (n_tensor - 1)) * r
        return pl.multiple_of(start, LANES)

    def cut_acts(act, r):
        count = n_tensor - 1

        def kernel(act_ref, *refs):
            out_refs, sem = refs[:-1], refs[-1]
            copies = [
                pltpu.make_async_copy(
                    act_ref.at[:, pl.ds(first_row(j + 1, r), r)], out_refs[j], sem.at[j]
                )
                for j in range(count)
            ]
            for copy in copies:
                copy.start()
            for copy in copies:
                copy.wait()

        return call(
            kernel,
            [array((act.shape[0], r), act.dtype)] * count,
            act,
            in_specs=[ANY],
            out_specs=[VMEM] * count,
            scratch_shapes=[pltpu.SemaphoreType.DMA((count,))],
        )

    def bound_of(cots, acts, scales):
        r, f, count = cots[0].shape[0], acts[0].shape[0], acts[0].shape[1]
        steps = 4

        def kernel(scale_ref, *refs):
            ins, (out_ref, most_ref) = refs[:4], refs[4:]

            @pl.when(pl.program_id(0) == 0)
            def _():
                most_ref[...] = jnp.zeros_like(most_ref)

            for n, ref in enumerate(ins):
                value = jnp.abs(ref[...].astype(jnp.float32))
                rows, cols = value.shape
                value = jnp.max(value.reshape(rows // 8, 8, cols), axis=0)
                value = functools.reduce(
                    jnp.maximum, (value[:, at : at + LANES] for at in range(0, cols, LANES))
                )
                most_ref[n] = jnp.maximum(most_ref[n], value)

            @pl.when(pl.program_id(0) == steps - 1)
            def _():
                bounds = [
                    jnp.max(most_ref[net]) * jnp.max(most_ref[2 + net]) * scale_ref[net]
                    for net in range(2)
                ]
                rows = lax.broadcasted_iota(jnp.int32, (8, LANES), 0)
                out_ref[...] = jnp.where(rows == 0, *bounds)

        return call(
            kernel, array((8, LANES), jnp.float32), scales, *cots, *acts,
            grid=(steps,),
            in_specs=[SMEM]
            + [pl.BlockSpec((r // steps, D), lambda s: (s, 0))] * 2
            + [pl.BlockSpec((f, count // steps), lambda s: (0, s))] * 2,
            out_specs=pl.BlockSpec((8, LANES), lambda s: (0, 0)),
            scratch_shapes=[pltpu.VMEM((4, 8, LANES), jnp.float32)],
        )

    def turn(cot, by_planes):
        r = cot.shape[0]
        step = min(r, TILE)
        count = 4 if by_planes else 2
        lead = (2, inner) if by_planes else (inner, OUTER)

        def kernel(cot_ref, *refs):
            out_refs, wide_ref = refs[:count], refs[count]
            eye = identity(TILE)
            for start in range(0, D, TILE):
                size = min(TILE, D - start)
                wide_ref[start : start + size, :] = dot(
                    eye[:size, :size], cot_ref[:, start : start + size], NT
                )
            for p in range(n_dp):
                k, i, other = relative(p)
                block = wide_ref[p * width : (p + 1) * width, :].astype(jnp.bfloat16)
                which, at = other, (i, k)
                if by_planes:
                    which, at = 2 - 2 * (k >> 1) + other, (1 - (k & 1), i)
                for n in range(count):

                    @pl.when(which == n)
                    def _(n=n, at=at, block=block):
                        out_refs[n][at] = block

        return call(
            kernel,
            [array((*lead, width, r), jnp.bfloat16)] * count,
            cot,
            grid=(r // step,),
            in_specs=[pl.BlockSpec((step, D), lambda s: (s, 0))],
            out_specs=[
                pl.BlockSpec((*lead, width, step), lambda s: (*(0 for _ in lead), 0, s))
            ] * count,
            scratch_shapes=[pltpu.VMEM((D, step), jnp.float32)],
        )

    def prepare(net, act, scales, r, places):
        f = act.shape[0]

        def kernel(scale_ref, act_ref, out_ref):
            for j in range(places):
                part = act_ref[:, pl.ds(first_row(j, r), r)].astype(jnp.float32)
                out_ref[j] = (part * scale_ref[net]).astype(jnp.bfloat16)

        return call(
            kernel, array((places, f, r), jnp.bfloat16), scales, act,
            in_specs=[SMEM, VMEM], out_specs=VMEM,
        )

    def multiply(pieces, scaled, places):
        lead, r, f = pieces[0].shape[:-1], pieces[0].shape[-1], scaled[0].shape[1]
        pieces = [piece.reshape(-1, r) for piece in pieces]
        rows = pieces[0].shape[0]
        step = D // (2 * OUTER)
        count = len(pieces)

        def kernel(*refs):
            piece_refs, scaled_refs, out_ref = refs[:count], refs[count:-1], refs[-1]
            for start in range(0, rows, step):
                part = slice(start, start + step)
                total = None
                for piece_ref, (n, j) in zip(piece_refs, places):
                    term = dot(piece_ref[part], scaled_refs[n][j], NT)
                    total = term if total is None else total + term
                out_ref[part] = total

        out = call(
            kernel, array((rows, f), jnp.float32), *pieces, *scaled,
            in_specs=[VMEM] * (count + len(scaled)), out_specs=VMEM,
        )
        return out.reshape(*lead, f)

    def scale_rows(act, scales):
        def kernel(scale_ref, act_ref, out_ref):
            out_ref[0] = (act_ref[...].astype(jnp.float32) * scale_ref[1]).astype(jnp.bfloat16)

        return call(
            kernel, array((1, *act.shape), jnp.bfloat16), scales, act,
            in_specs=[SMEM, VMEM], out_specs=VMEM,
        )

    def norms(total_s, total_f):
        def kernel(s_ref, f_ref, out_ref):
            sums = [jnp.sum(ref[...] * ref[...]) for ref in (s_ref, f_ref)]
            rows = lax.broadcasted_iota(jnp.int32, (8, LANES), 0)
            out_ref[...] = jnp.where(rows == 0, *sums)

        return call(
            kernel, array((8, LANES), jnp.float32), total_s, total_f,
            in_specs=[VMEM] * 2, out_specs=VMEM,
        )

    def update(squares, totals, states):
        shape = totals[0].shape

        def kernel(squares_ref, *refs):
            total_refs, state_refs, (own_ref, *out_refs) = refs[:2], refs[2:8], refs[8:]
            for net in range(2):
                new = adam_update(
                    total_refs[net][...],
                    squares_ref[net : net + 1, :1],
                    *(ref[...] for ref in state_refs[3 * net : 3 * net + 3]),
                )
                own_ref[net] = new[0].astype(jnp.bfloat16)
                for ref, value in zip(out_refs[3 * net :], new):
                    ref[...] = value

        own, *new = call(
            kernel,
            [array((2, *shape), jnp.bfloat16)] + [array(shape, jnp.float32)] * 6,
            squares, *totals, *states,
            in_specs=[VMEM] * 9,
            out_specs=[VMEM] * 7,
        )
        return own, new

    def back_part(whole, weight, pieces, scales, net, j, low, size, r, count):
        f = weight.shape[0]
        turned = len(pieces) > 1

        def kernel(scale_ref, weight_ref, *refs):
            piece_refs = refs[: len(pieces)]
            if turned:
                out_ref, done_ref, sem, wide_ref = refs[-4:]
                for k in range(OUTER):
                    for other in range(2):
                        for i in range(inner):
                            block = piece_refs[2 - 2 * (k >> 1) + other][1 - (k & 1), i]
                            block = block.astype(jnp.float32)
                            wide_ref[owner(k, i, other)] = block
                flat = wide_ref[...].reshape(D, size).astype(jnp.bfloat16)
                product = dot(weight_ref[...], flat, NN)
            else:
                out_ref, done_ref, sem = refs[-3:]
                product = dot(weight_ref[...], piece_refs[0][...], NT)
            done_ref[...] = (product * scale_ref[net]).astype(jnp.bfloat16)
            start = pl.multiple_of(first_row(j, r) + low, LANES)
            copy = pltpu.make_async_copy(done_ref, out_ref.at[:, pl.ds(start, size)], sem)
            copy.start()
            copy.wait()

        scratch = [pltpu.VMEM((f, size), jnp.bfloat16), pltpu.SemaphoreType.DMA]
        if turned:
            scratch.append(pltpu.VMEM((n_dp, width, size), jnp.float32))
        operands = [scales, weight, *pieces]
        in_specs = [SMEM] + [VMEM] * (len(operands) - 1)
        aliases = {}
        if whole is not None:
            aliases = {len(operands): 0}
            operands.append(whole)
            in_specs.append(ANY)
        return call(
            kernel, array((f, count), jnp.bfloat16), *operands,
            in_specs=in_specs, out_specs=ANY, scratch_shapes=scratch,
            input_output_aliases=aliases, mib=20,
        )

    def spread(stacks, net):
        count, _, _, f = stacks[0].shape

        def kernel(*refs):
            stack_refs, (out_ref, wide_ref) = refs[:4], refs[4:]
            lanes = lax.broadcasted_iota(jnp.int32, (width, LANES), 1)
            inside = lanes + pl.program_id(0) * LANES < f
            for n, ref in enumerate(stack_refs):
                for at in range(count):
                    k, i = divmod((n & 1) * count + at, inner)
                    block = jnp.where(inside, ref[at, 0].astype(jnp.float32), 0.0)
                    wide_ref[owner(k, i, n >> 1)] = block
            flat = wide_ref[...].reshape(D, LANES).astype(jnp.bfloat16)
            out_ref[...] = dot(identity(LANES), flat, NT).astype(jnp.bfloat16)

        return call(
            kernel, array((f, D), jnp.bfloat16), *stacks,
            grid=(pl.cdiv(f, LANES),),
            in_specs=[pl.BlockSpec((count, 1, width, LANES), lambda s: (0, net, 0, s))] * 4,
            out_specs=pl.BlockSpec((LANES, D), lambda s: (s, 0)),
            scratch_shapes=[pltpu.VMEM((n_dp, width, LANES), jnp.float32)],
        )

    def per_device(
        cot_student, cot_fake, act_student, act_fake, weight_student, weight_fake,
        master_student, first_student, second_student, master_fake, first_fake, second_fake,
        timesteps,
    ):
        f, count = act_student.shape
        r = cot_student.shape[0]
        assert timesteps.shape[2] == 1 and count == ROWS

        token = []

        def step(work, *inputs):
            if token:
                *inputs, _ = lax.optimization_barrier((*inputs, token[0]))
            out = work(*inputs)
            token[:] = jax.tree.leaves(out)[:1]
            return out

        def reduced(combine, value, got):
            return step(lambda *values: functools.reduce(combine, values), value, *got)

        def hops(value, combine):
            distance = 1
            while distance < n_dp:
                perm = [(p, p ^ distance) for p in range(n_dp)]
                got = lax.ppermute(value, "dp", perm)
                yield
                value = step(combine, value, got)
                distance *= 2
            yield value

        acts = [from_tensor(act, -j) for j, act in enumerate(step(lambda a: cut_acts(a, r), act_fake), 1)]
        scales = step(
            lambda steps: 1.0 / (0.1 + steps.astype(jnp.float32) / 1000.0), timesteps[0, :, 0]
        )
        bounds = step(
            lambda a, b, c, d, scales: bound_of((a, b), (c, d), scales),
            cot_student, cot_fake, act_student, act_fake, scales,
        )
        bounds = hops(bounds, jnp.maximum)
        next(bounds)
        fake_blocks = step(lambda cot: turn(cot, False), cot_fake)
        mate_blocks = to_core(fake_blocks[1])
        next(bounds)
        scaled_own = step(lambda act: prepare(1, act, scales, r, 1), act_fake)
        scaled_fake = [[scaled_own, to_core(scaled_own)]]
        next(bounds)
        planes = step(lambda cot: turn(cot, True), cot_student)

        same, diagonal = [], []

        def send_planes(g, own, other):
            same.append([from_tensor(own, j) for j in range(1, n_tensor)])
            diagonal.append([from_diagonal(other, j) for j in range(1, n_tensor)])

        send_planes(0, planes[0], planes[1])
        next(bounds)
        scaled_student = step(lambda act: prepare(0, act, scales, r, n_tensor), act_student)
        while (final := next(bounds)) is None:
            pass

        def factors(bounds):
            bounds = jnp.maximum(bounds, 1e-30) * (1.01 * count * n_dp / HALF_LIMIT)
            return bounds[:2, 0], 1.0 / bounds[:2, 0]

        grow, fit = step(factors, final)

        def shrink(value, net):
            return (value * fit[net]).astype(jnp.float16)

        def widen(value, net):
            return value.astype(jnp.float32) * grow[net]

        def add_widened(total, values, net):
            for value in values:
                total = total + widen(value, net)
            return total

        parts_fake = []

        def multiply_fake(j):
            parts_fake.append(
                step(
                    lambda a, b, c, d: multiply([a, b], [c, d], [(0, 0), (1, 0)]),
                    fake_blocks[0], mate_blocks, *scaled_fake[j],
                )
            )

        for act in acts:
            scaled_other = step(scale_rows, act, scales)
            scaled_fake.append([scaled_other, to_core(scaled_other)])
        multiply_fake(0)
        mate_student = to_core(scaled_student)
        mate_planes = [to_core(planes[1]), to_core(planes[3])]
        for j in range(1, n_tensor):
            multiply_fake(j)
        mate_student, *mate_planes = step(lambda *values: values, mate_student, *mate_planes)

        middles = {}

        def fake_middle(j):
            def work(both):
                sent = [
                    [shrink(both[i, lo : lo + 2], 1) for i in range(1, inner)] for lo in (2, 0)
                ]
                return sent, both[0, 2:], both[0, :2]

            sent, *mine = step(work, parts_fake[j])
            middles[j] = [
                (own, [to_middle(value, i) for i, value in enumerate(values, 1)])
                for own, values in zip(mine, sent)
            ]

        for j in range(n_tensor):
            fake_middle(j)

        def back(whole, net, pieces, j, low, size):
            weight = (weight_student, weight_fake)[net]
            has = [] if whole is None else [whole]

            def work(weight, *values):
                return back_part(
                    values[-1] if has else None, weight, values[: len(pieces)], scales,
                    net, j, low, size, r, count,
                )

            return step(work, weight, *pieces, *has)

        fake_sums = {j: [] for j in range(n_tensor)}

        def fake_planes(j, part):
            def work(own, *got):
                own = add_widened(own, got, 1)
                if part == 0:
                    return shrink(own[1], 1), shrink(own[0], 1)
                return shrink(own[1], 1), own[0]

            own, got = middles[j][part]
            values = step(work, own, *got)
            for k, value in zip(((3, 2), (1, 0))[part], values):
                fake_sums[j].append(to_plane(value, k) if k else value)

        def fake_total(j):
            *got, own = fake_sums[j]
            return step(lambda own, *got: add_widened(own, got, 1), own, *got)

        def multiply_student(g):
            pieces, places = [planes[2 * g], mate_planes[g]], [(0, 0), (1, 0)]
            for j in range(1, n_tensor):
                pieces += [same[g][j - 1], diagonal[g][j - 1]]
                places += [(0, j), (1, j)]
            return step(
                lambda *values: multiply(values[:-2], values[-2:], places),
                *pieces, scaled_student, mate_student,
            )

        back_student = back(None, 0, [cot_student], 0, 0, r)
        fake_planes(0, 0)
        back_fake = back(None, 1, [cot_fake], 0, 0, r)
        fake_planes(0, 1)
        both = multiply_student(0)
        send_planes(1, *step(lambda a, b: (a, b), planes[2], planes[3]))

        def first_middle(both):
            return [shrink(both[:, i], 0) for i in range(1, inner)], both[:, 0]

        fake_mine = fake_total(0)
        sent, own = step(first_middle, both)
        got = [to_middle(value, i) for i, value in enumerate(sent, 1)]
        for j in range(1, n_tensor):
            fake_planes(j, 0)
        for j in range(1, n_tensor):
            fake_planes(j, 1)

        def first_planes(own, *got):
            own = add_widened(own, got, 0)
            return shrink(own[0], 0), shrink(own[1], 0)

        sent = step(first_planes, own, *got)
        first_got = [to_plane(value, k) for k, value in zip((3, 2), sent)]
        both = multiply_student(1)

        def second_middle(both):
            sent = [[shrink(both[n, i], 0) for i in range(1, inner)] for n in range(2)]
            return sent, both[0, 0], both[1, 0]

        sent, own_next, own = step(second_middle, both)
        got_next, got = (
            [to_middle(value, i) for i, value in enumerate(values, 1)] for values in sent
        )
        fake_others = [fake_total(j) for j in range(1, n_tensor)]
        fake_got = [from_tensor(value, j) for j, value in enumerate(fake_others, 1)]
        next_sent = step(
            lambda own, *got: shrink(add_widened(own, got, 0), 0), own_next, *got_next
        )
        next_got = to_plane(next_sent, 1)
        total_fake = reduced(jnp.add, fake_mine, fake_got)
        total_student = step(
            lambda own, *got: add_widened(own, got, 0), own, *got, *first_got
        )
        total_student = step(
            lambda own, *got: add_widened(own, got, 0), total_student, next_got
        )
        squares = step(norms, total_student, total_fake)
        squares = reduced(
            jnp.add, squares, [from_tensor(squares, j) for j in range(1, n_tensor)]
        )

        raw_sent = step(lambda cot: cot, cot_fake)
        raw = [from_tensor(raw_sent, j) for j in range(1, n_tensor)]
        hidden = step(lambda *values: values, *[value for group in diagonal for value in group])
        mate_others = [to_core(value) for value in hidden]
        *_, squares = hops(squares, jnp.add)
        squares, *mate_others = step(lambda *values: values, squares, *mate_others)
        mate_others = [mate_others[: n_tensor - 1], mate_others[n_tensor - 1 :]]

        states = (
            master_student, first_student, second_student, master_fake, first_fake, second_fake,
        )
        own, updated = step(
            lambda squares, *values: update(squares, values[:2], values[2:]),
            squares, total_student, total_fake, *(state.T for state in states),
        )

        mine = {}

        def spread_middle(k, value):
            mine[k] = [value] + [to_middle(value, -i) for i in range(1, inner)]

        spread_middle(0, own)
        planes_got = {k: to_plane(own, -k) for k in (1, 3, 2)}
        for j in range(1, n_tensor):
            pieces = [
                piece for g in range(2) for piece in (same[g][j - 1], mate_others[g][j - 1])
            ]
            back_student = back(back_student, 0, pieces, j, 0, r)
        spread_middle(1, step(lambda value: value, planes_got[1]))
        spread_middle(3, step(lambda value: value, planes_got[3]))
        first_half = step(lambda *values: jnp.stack(values), *mine[0], *mine[1])
        theirs = [to_core(first_half)]
        spread_middle(2, step(lambda value: value, planes_got[2]))
        second_half = step(lambda *values: jnp.stack(values), *mine[2], *mine[3])
        theirs.append(to_core(second_half))
        for j in range(1, n_tensor):
            back_fake = back(back_fake, 1, [raw[j - 1]], j, 0, r)
        stacks = [first_half, second_half, *theirs]
        params = [step(lambda *values: spread(values, n), *stacks) for n in range(2)]

        new_states = [value.T for value in updated]
        return (back_student, back_fake, *new_states, *params)

    placed = (
        P(("dp", "tensor"), None),
        P(("dp", "tensor"), None),
        P("tensor", "dp"),
        P("tensor", "dp"),
        P("tensor", None),
        P("tensor", None),
        P("tensor", "dp"),
        P("tensor", "dp"),
        P("tensor", "dp"),
        P("tensor", "dp"),
        P("tensor", "dp"),
        P("tensor", "dp"),
        P("dp", None, None),
    )
    return jax.shard_map(
        per_device,
        mesh=mesh,
        in_specs=placed,
        out_specs=(
            P("tensor", "dp"),
            P("tensor", "dp"),
            P("tensor", "dp"),
            P("tensor", "dp"),
            P("tensor", "dp"),
            P("tensor", "dp"),
            P("tensor", "dp"),
            P("tensor", "dp"),
            P("tensor", None),
            P("tensor", None),
        ),
        check_vma=False,
    )
```

```python
import functools

import jax
import jax.numpy as jnp
from jax import lax
from jax.experimental import pallas as pl
from jax.experimental.pallas import tpu as pltpu
from jax.sharding import PartitionSpec as P

D = 2432
F = 1216
ROWS = 1024


FIRST_CORRECTION = 0.9999734386011124
SECOND_CORRECTION = 0.0952078529183

OUTER = 4
HALF_LIMIT = 60000.0
TILE = 256
LANES = 128

NT = (((1,), (1,)), ((), ()))
NN = (((1,), (0,)), ((), ()))

SMEM = pl.BlockSpec(memory_space=pltpu.SMEM)
VMEM = pl.BlockSpec(memory_space=pltpu.VMEM)
ANY = pl.BlockSpec(memory_space=pl.ANY)


def adam_update(grad, squares, master, first, second):
    clip = jnp.minimum(1.0, jnp.sqrt(jnp.float32(D * F)) / jnp.sqrt(squares + 1e-06))
    clipped = grad * clip
    new_first = 0.9 * first + 0.1 * clipped
    new_second = 0.999 * second + 0.001 * clipped * clipped
    step_dir = new_first / FIRST_CORRECTION / (jnp.sqrt(new_second / SECOND_CORRECTION) + 1e-08)
    new_master = master * (1.0 - 0.01 * 0.01) - 0.01 * step_dir
    return (new_master, new_first, new_second)


def dot(a, b, dims):
    return lax.dot_general(a, b, dims, preferred_element_type=jnp.float32)


def identity(size):
    rows = lax.broadcasted_iota(jnp.int32, (size, size), 0)
    cols = lax.broadcasted_iota(jnp.int32, (size, size), 1)
    return jnp.where(rows == cols, 1.0, 0.0).astype(jnp.bfloat16)


def array(shape, dtype):
    return jax.ShapeDtypeStruct(shape, dtype)


def call(kernel, out_shape, *operands, mib=12, **kwargs):
    return pl.pallas_call(
        kernel,
        out_shape=out_shape,
        compiler_params=pltpu.CompilerParams(vmem_limit_bytes=mib * 1024 * 1024),
        cost_estimate=pl.CostEstimate(flops=0, bytes_accessed=0, transcendentals=0),
        **kwargs,
    )(*operands)


def solution(mesh):
    n_dp, n_tensor = mesh.shape["dp"], mesh.shape["tensor"]
    inner = n_dp // (2 * OUTER)
    width = D // n_dp

    def split(p):
        return (p >> inner.bit_length()) & (OUTER - 1), (p >> 1) & (inner - 1), p & 1

    def join(z, m, c):
        return (z * inner + m) * 2 + c

    def move_dp(value, where):
        perm = [(p, join(*where(*split(p)))) for p in range(n_dp)]
        return lax.ppermute(value, "dp", perm)

    def to_plane(value, k):
        return move_dp(value, lambda z, m, c: (z ^ k, m, c))

    def to_middle(value, k):
        return move_dp(value, lambda z, m, c: (z, (m + k) & (inner - 1), c))

    def to_core(value):
        return move_dp(value, lambda z, m, c: (z, m, 1 - c))

    def from_tensor(value, k):
        perm = [(s, (s - k) & (n_tensor - 1)) for s in range(n_tensor)]
        return lax.ppermute(value, "tensor", perm)

    def from_diagonal(value, k):
        perm = []
        for p in range(n_dp):
            z, m, c = split(p)
            for t in range(n_tensor):
                target = join(z, m, 1 - c) * n_tensor + ((t - k) & (n_tensor - 1))
                perm.append((p * n_tensor + t, target))
        return lax.ppermute(value, ("dp", "tensor"), perm)

    def my_place():
        return split(lax.axis_index("dp"))

    def relative(p):
        z, m, c = split(p)
        my_z, my_m, my_c = my_place()
        return z ^ my_z, (m - my_m) & (inner - 1), c ^ my_c

    def owner(k, i, other):
        z, m, c = my_place()
        return join(z ^ k, (m + i) & (inner - 1), c ^ other)

    def first_row(j, r):
        start = ((lax.axis_index("tensor") + j) & (n_tensor - 1)) * r
        return pl.multiple_of(start, LANES)

    def cut_acts(act, r):
        count = n_tensor - 1

        def kernel(act_ref, *refs):
            out_refs, sem = refs[:-1], refs[-1]
            copies = [
                pltpu.make_async_copy(
                    act_ref.at[:, pl.ds(first_row(j + 1, r), r)], out_refs[j], sem.at[j]
                )
                for j in range(count)
            ]
            for copy in copies:
                copy.start()
            for copy in copies:
                copy.wait()

        return call(
            kernel,
            [array((act.shape[0], r), act.dtype)] * count,
            act,
            in_specs=[ANY],
            out_specs=[VMEM] * count,
            scratch_shapes=[pltpu.SemaphoreType.DMA((count,))],
        )

    def bound_of(cots, acts, scales):
        r, f, count = cots[0].shape[0], acts[0].shape[0], acts[0].shape[1]
        steps = 4

        def kernel(scale_ref, *refs):
            ins, (out_ref, most_ref) = refs[:4], refs[4:]

            @pl.when(pl.program_id(0) == 0)
            def _():
                most_ref[...] = jnp.zeros_like(most_ref)

            for n, ref in enumerate(ins):
                value = jnp.abs(ref[...].astype(jnp.float32))
                rows, cols = value.shape
                value = jnp.max(value.reshape(rows // 8, 8, cols), axis=0)
                value = functools.reduce(
                    jnp.maximum, (value[:, at : at + LANES] for at in range(0, cols, LANES))
                )
                most_ref[n] = jnp.maximum(most_ref[n], value)

            @pl.when(pl.program_id(0) == steps - 1)
            def _():
                bounds = [
                    jnp.max(most_ref[net]) * jnp.max(most_ref[2 + net]) * scale_ref[net]
                    for net in range(2)
                ]
                rows = lax.broadcasted_iota(jnp.int32, (8, LANES), 0)
                out_ref[...] = jnp.where(rows == 0, *bounds)

        return call(
            kernel, array((8, LANES), jnp.float32), scales, *cots, *acts,
            grid=(steps,),
            in_specs=[SMEM]
            + [pl.BlockSpec((r // steps, D), lambda s: (s, 0))] * 2
            + [pl.BlockSpec((f, count // steps), lambda s: (0, s))] * 2,
            out_specs=pl.BlockSpec((8, LANES), lambda s: (0, 0)),
            scratch_shapes=[pltpu.VMEM((4, 8, LANES), jnp.float32)],
        )

    def turn(cot, by_planes):
        r = cot.shape[0]
        step = min(r, TILE)
        count = 4 if by_planes else 2
        lead = (2, inner) if by_planes else (inner, OUTER)

        def kernel(cot_ref, *refs):
            out_refs, wide_ref = refs[:count], refs[count]
            eye = identity(TILE)
            for start in range(0, D, TILE):
                size = min(TILE, D - start)
                wide_ref[start : start + size, :] = dot(
                    eye[:size, :size], cot_ref[:, start : start + size], NT
                )
            for p in range(n_dp):
                k, i, other = relative(p)
                block = wide_ref[p * width : (p + 1) * width, :].astype(jnp.bfloat16)
                which, at = other, (i, k)
                if by_planes:
                    even = 1 - (k & 1)
                    which, at = 2 * even + other, ((k >> 1) ^ even, i)
                for n in range(count):

                    @pl.when(which == n)
                    def _(n=n, at=at, block=block):
                        out_refs[n][at] = block

        return call(
            kernel,
            [array((*lead, width, r), jnp.bfloat16)] * count,
            cot,
            grid=(r // step,),
            in_specs=[pl.BlockSpec((step, D), lambda s: (s, 0))],
            out_specs=[
                pl.BlockSpec((*lead, width, step), lambda s: (*(0 for _ in lead), 0, s))
            ] * count,
            scratch_shapes=[pltpu.VMEM((D, step), jnp.float32)],
        )

    def prepare(net, act, scales, r, places):
        f = act.shape[0]

        def kernel(scale_ref, act_ref, out_ref):
            for j in range(places):
                part = act_ref[:, pl.ds(first_row(j, r), r)].astype(jnp.float32)
                out_ref[j] = (part * scale_ref[net]).astype(jnp.bfloat16)

        return call(
            kernel, array((places, f, r), jnp.bfloat16), scales, act,
            in_specs=[SMEM, VMEM], out_specs=VMEM,
        )

    def multiply(pieces, scaled, places):
        lead, r, f = pieces[0].shape[:-1], pieces[0].shape[-1], scaled[0].shape[1]
        pieces = [piece.reshape(-1, r) for piece in pieces]
        rows = pieces[0].shape[0]
        step = D // (2 * OUTER)
        count = len(pieces)

        def kernel(*refs):
            piece_refs, scaled_refs, out_ref = refs[:count], refs[count:-1], refs[-1]
            for start in range(0, rows, step):
                part = slice(start, start + step)
                total = None
                for piece_ref, (n, j) in zip(piece_refs, places):
                    term = dot(piece_ref[part], scaled_refs[n][j], NT)
                    total = term if total is None else total + term
                out_ref[part] = total

        out = call(
            kernel, array((rows, f), jnp.float32), *pieces, *scaled,
            in_specs=[VMEM] * (count + len(scaled)), out_specs=VMEM,
        )
        return out.reshape(*lead, f)

    def scale_rows(act, scales):
        def kernel(scale_ref, act_ref, out_ref):
            out_ref[0] = (act_ref[...].astype(jnp.float32) * scale_ref[1]).astype(jnp.bfloat16)

        return call(
            kernel, array((1, *act.shape), jnp.bfloat16), scales, act,
            in_specs=[SMEM, VMEM], out_specs=VMEM,
        )

    def norms(total_s, total_f):
        def kernel(s_ref, f_ref, out_ref):
            sums = [jnp.sum(ref[...] * ref[...]) for ref in (s_ref, f_ref)]
            rows = lax.broadcasted_iota(jnp.int32, (8, LANES), 0)
            out_ref[...] = jnp.where(rows == 0, *sums)

        return call(
            kernel, array((8, LANES), jnp.float32), total_s, total_f,
            in_specs=[VMEM] * 2, out_specs=VMEM,
        )

    def update(squares, totals, states):
        shape = totals[0].shape

        def kernel(squares_ref, *refs):
            total_refs, state_refs, (own_ref, *out_refs) = refs[:2], refs[2:8], refs[8:]
            for net in range(2):
                new = adam_update(
                    total_refs[net][...],
                    squares_ref[net : net + 1, :1],
                    *(ref[...] for ref in state_refs[3 * net : 3 * net + 3]),
                )
                own_ref[net] = new[0].astype(jnp.bfloat16)
                for ref, value in zip(out_refs[3 * net :], new):
                    ref[...] = value

        own, *new = call(
            kernel,
            [array((2, *shape), jnp.bfloat16)] + [array(shape, jnp.float32)] * 6,
            squares, *totals, *states,
            in_specs=[VMEM] * 9,
            out_specs=[VMEM] * 7,
        )
        return own, new

    def back_part(whole, weight, pieces, scales, net, j, low, size, r, count):
        f = weight.shape[0]
        turned = len(pieces) > 1

        def kernel(scale_ref, weight_ref, *refs):
            piece_refs = refs[: len(pieces)]
            if turned:
                out_ref, done_ref, sem, wide_ref = refs[-4:]
                for k in range(OUTER):
                    for other in range(2):
                        for i in range(inner):
                            even = 1 - (k & 1)
                            block = piece_refs[2 * even + other][(k >> 1) ^ even, i]
                            block = block.astype(jnp.float32)
                            wide_ref[owner(k, i, other)] = block
                flat = wide_ref[...].reshape(D, size).astype(jnp.bfloat16)
                product = dot(weight_ref[...], flat, NN)
            else:
                out_ref, done_ref, sem = refs[-3:]
                product = dot(weight_ref[...], piece_refs[0][...], NT)
            done_ref[...] = (product * scale_ref[net]).astype(jnp.bfloat16)
            start = pl.multiple_of(first_row(j, r) + low, LANES)
            copy = pltpu.make_async_copy(done_ref, out_ref.at[:, pl.ds(start, size)], sem)
            copy.start()
            copy.wait()

        scratch = [pltpu.VMEM((f, size), jnp.bfloat16), pltpu.SemaphoreType.DMA]
        if turned:
            scratch.append(pltpu.VMEM((n_dp, width, size), jnp.float32))
        operands = [scales, weight, *pieces]
        in_specs = [SMEM] + [VMEM] * (len(operands) - 1)
        aliases = {}
        if whole is not None:
            aliases = {len(operands): 0}
            operands.append(whole)
            in_specs.append(ANY)
        return call(
            kernel, array((f, count), jnp.bfloat16), *operands,
            in_specs=in_specs, out_specs=ANY, scratch_shapes=scratch,
            input_output_aliases=aliases, mib=20,
        )

    def spread(stacks, net):
        count, _, _, f = stacks[0].shape

        def kernel(*refs):
            stack_refs, (out_ref, wide_ref) = refs[:4], refs[4:]
            lanes = lax.broadcasted_iota(jnp.int32, (width, LANES), 1)
            inside = lanes + pl.program_id(0) * LANES < f
            for n, ref in enumerate(stack_refs):
                for at in range(count):
                    k, i = divmod((n & 1) * count + at, inner)
                    block = jnp.where(inside, ref[at, 0].astype(jnp.float32), 0.0)
                    wide_ref[owner(k, i, n >> 1)] = block
            flat = wide_ref[...].reshape(D, LANES).astype(jnp.bfloat16)
            out_ref[...] = dot(identity(LANES), flat, NT).astype(jnp.bfloat16)

        return call(
            kernel, array((f, D), jnp.bfloat16), *stacks,
            grid=(pl.cdiv(f, LANES),),
            in_specs=[pl.BlockSpec((count, 1, width, LANES), lambda s: (0, net, 0, s))] * 4,
            out_specs=pl.BlockSpec((LANES, D), lambda s: (s, 0)),
            scratch_shapes=[pltpu.VMEM((n_dp, width, LANES), jnp.float32)],
        )

    def per_device(
        cot_student, cot_fake, act_student, act_fake, weight_student, weight_fake,
        master_student, first_student, second_student, master_fake, first_fake, second_fake,
        timesteps,
    ):
        f, count = act_student.shape
        r = cot_student.shape[0]
        assert timesteps.shape[2] == 1 and count == ROWS

        token = []

        def step(work, *inputs):
            if token:
                *inputs, _ = lax.optimization_barrier((*inputs, token[0]))
            out = work(*inputs)
            token[:] = jax.tree.leaves(out)[:1]
            return out

        def reduced(combine, value, got):
            return step(lambda *values: functools.reduce(combine, values), value, *got)

        def hops(value, combine):
            distance = 1
            while distance < n_dp:
                perm = [(p, p ^ distance) for p in range(n_dp)]
                got = lax.ppermute(value, "dp", perm)
                yield
                value = step(combine, value, got)
                distance *= 2
            yield value

        acts = [from_tensor(act, -j) for j, act in enumerate(step(lambda a: cut_acts(a, r), act_fake), 1)]
        scales = step(
            lambda steps: 1.0 / (0.1 + steps.astype(jnp.float32) / 1000.0), timesteps[0, :, 0]
        )
        bounds = step(
            lambda a, b, c, d, scales: bound_of((a, b), (c, d), scales),
            cot_student, cot_fake, act_student, act_fake, scales,
        )
        bounds = hops(bounds, jnp.maximum)
        next(bounds)
        fake_blocks = step(lambda cot: turn(cot, False), cot_fake)
        mate_blocks = to_core(fake_blocks[1])
        scaled_own = step(lambda act: prepare(1, act, scales, r, 1), act_fake)
        scaled_fake = [[scaled_own, to_core(scaled_own)]]
        planes = step(lambda cot: turn(cot, True), cot_student)

        same, diagonal = [], []

        def send_planes(g, own, other):
            same.append([from_tensor(own, j) for j in range(1, n_tensor)])
            diagonal.append([from_diagonal(other, j) for j in range(1, n_tensor)])

        send_planes(0, planes[0], planes[1])
        scaled_student = step(lambda act: prepare(0, act, scales, r, n_tensor), act_student)
        for act in acts:
            scaled_other = step(scale_rows, act, scales)
            scaled_fake.append([scaled_other, to_core(scaled_other)])
        parts_fake = []
        for j in range(n_tensor):
            if j < 2:
                next(bounds)
            parts_fake.append(
                step(
                    lambda a, b, c, d: multiply([a, b], [c, d], [(0, 0), (1, 0)]),
                    fake_blocks[0], mate_blocks, *scaled_fake[j],
                )
            )
        while (final := next(bounds)) is None:
            pass

        def factors(bounds):
            bounds = jnp.maximum(bounds, 1e-30) * (1.01 * count * n_dp / HALF_LIMIT)
            return bounds[:2, 0], 1.0 / bounds[:2, 0]

        grow, fit = step(factors, final)

        def shrink(value, net):
            return (value * fit[net]).astype(jnp.float16)

        def widen(value, net):
            return value.astype(jnp.float32) * grow[net]

        def add_widened(total, values, net):
            for value in values:
                total = total + widen(value, net)
            return total

        fake_own, fake_got = {}, {}

        def fake_middle(j):
            def work(both):
                sent = [shrink(both[i], 1) for i in range(1, inner)]
                return sent, both[0]

            sent, fake_own[j] = step(work, parts_fake[j])
            fake_got[j] = [to_middle(value, i) for i, value in enumerate(sent, 1)]

        def fake_near(j):
            def work(own, *got):
                own = add_widened(own, got, 1)
                return shrink(own[1::2], 1), own[0::2]

            sent, fake_own[j] = step(work, fake_own[j], *fake_got[j])
            fake_got[j] = [to_plane(sent, 1)]

        def fake_far(j):
            def work(own, *got):
                own = add_widened(own, got, 1)
                return shrink(own[1], 1), own[0]

            sent, fake_own[j] = step(work, fake_own[j], *fake_got[j])
            fake_got[j] = [to_plane(sent, 2)]

        def fake_total(j):
            return step(
                lambda own, *got: add_widened(own, got, 1), fake_own[j], *fake_got[j]
            )

        mate_student = to_core(scaled_student)
        mate_planes = [to_core(planes[1]), to_core(planes[3])]
        for j in range(n_tensor):
            fake_middle(j)
        mate_student, *mate_planes = step(lambda *values: values, mate_student, *mate_planes)

        def back(whole, net, pieces, j, low, size):
            weight = (weight_student, weight_fake)[net]
            has = [] if whole is None else [whole]

            def work(weight, *values):
                return back_part(
                    values[-1] if has else None, weight, values[: len(pieces)], scales,
                    net, j, low, size, r, count,
                )

            return step(work, weight, *pieces, *has)

        def multiply_student(g):
            pieces, places = [planes[2 * g], mate_planes[g]], [(0, 0), (1, 0)]
            for j in range(1, n_tensor):
                pieces += [same[g][j - 1], diagonal[g][j - 1]]
                places += [(0, j), (1, j)]
            return step(
                lambda *values: multiply(values[:-2], values[-2:], places),
                *pieces, scaled_student, mate_student,
            )

        back_student = back(None, 0, [cot_student], 0, 0, r)
        send_planes(1, *step(lambda a, b: (a, b), planes[2], planes[3]))
        back_fake = back(None, 1, [cot_fake], 0, 0, r)
        both = multiply_student(0)

        def first_middle(both):
            return [shrink(both[:, i], 0) for i in range(1, inner)], both[:, 0]

        sent, own = step(first_middle, both)
        got = [to_middle(value, i) for i, value in enumerate(sent, 1)]
        for j in range(n_tensor):
            fake_near(j)

        def first_planes(own, *got):
            return shrink(add_widened(own, got, 0), 0)

        near = to_plane(step(first_planes, own, *got), 1)
        for j in range(n_tensor):
            fake_far(j)
        both = multiply_student(1)

        def second_middle(both):
            sent = [[shrink(both[n, i], 0) for i in range(1, inner)] for n in range(2)]
            return sent, both[0, 0], both[1, 0]

        sent, own_far, own = step(second_middle, both)
        got_far, got = (
            [to_middle(value, i) for i, value in enumerate(values, 1)] for values in sent
        )
        fake_mine = fake_total(0)
        fake_others = [fake_total(j) for j in range(1, n_tensor)]
        others_got = [from_tensor(value, j) for j, value in enumerate(fake_others, 1)]

        def far_plane(own, near, *got):
            return shrink(add_widened(own, (near[1], *got), 0), 0)

        far = to_plane(step(far_plane, own_far, near, *got_far), 2)
        total_student = step(
            lambda own, near, *got: add_widened(own, (near[0], *got), 0), own, near, *got
        )
        total_fake = reduced(jnp.add, fake_mine, others_got)
        total_student = step(
            lambda own, got: add_widened(own, (got,), 0), total_student, far
        )
        squares = step(norms, total_student, total_fake)
        squares = reduced(
            jnp.add, squares, [from_tensor(squares, j) for j in range(1, n_tensor)]
        )

        rows = step(lambda cot: cot, cot_fake)
        raw = [from_tensor(rows, j) for j in range(1, n_tensor)]

        hidden = step(lambda *values: values, *[value for group in diagonal for value in group])
        mate_others = [to_core(value) for value in hidden]
        *_, squares = hops(squares, jnp.add)
        squares, *mate_others = step(lambda *values: values, squares, *mate_others)
        mate_others = [mate_others[: n_tensor - 1], mate_others[n_tensor - 1 :]]

        states = (
            master_student, first_student, second_student, master_fake, first_fake, second_fake,
        )
        own, updated = step(
            lambda squares, *values: update(squares, values[:2], values[2:]),
            squares, total_student, total_fake, *(state.T for state in states),
        )

        mine = {}

        def spread_middle(k, value):
            mine[k] = [value] + [to_middle(value, -i) for i in range(1, inner)]

        spread_middle(0, own)
        planes_got = {k: to_plane(own, k) for k in (1, 3, 2)}
        for j in range(1, n_tensor):
            pieces = [
                piece for g in range(2) for piece in (same[g][j - 1], mate_others[g][j - 1])
            ]
            back_student = back(back_student, 0, pieces, j, 0, r)
        spread_middle(1, step(lambda value: value, planes_got[1]))
        spread_middle(3, step(lambda value: value, planes_got[3]))
        spread_middle(2, step(lambda value: value, planes_got[2]))
        first_half = step(lambda *values: jnp.stack(values), *mine[0], *mine[1])
        theirs = [to_core(first_half)]
        for j in range(1, n_tensor):
            back_fake = back(back_fake, 1, [raw[j - 1]], j, 0, r)
        second_half = step(lambda *values: jnp.stack(values), *mine[2], *mine[3])
        theirs.append(to_core(second_half))
        stacks = [first_half, second_half, *theirs]
        params = [step(lambda *values: spread(values, n), *stacks) for n in range(2)]

        new_states = [value.T for value in updated]
        return (back_student, back_fake, *new_states, *params)

    placed = (
        P(("dp", "tensor"), None),
        P(("dp", "tensor"), None),
        P("tensor", "dp"),
        P("tensor", "dp"),
        P("tensor", None),
        P("tensor", None),
        P("tensor", "dp"),
        P("tensor", "dp"),
        P("tensor", "dp"),
        P("tensor", "dp"),
        P("tensor", "dp"),
        P("tensor", "dp"),
        P("dp", None, None),
    )
    return jax.shard_map(
        per_device,
        mesh=mesh,
        in_specs=placed,
        out_specs=(
            P("tensor", "dp"),
            P("tensor", "dp"),
            P("tensor", "dp"),
            P("tensor", "dp"),
            P("tensor", "dp"),
            P("tensor", "dp"),
            P("tensor", "dp"),
            P("tensor", "dp"),
            P("tensor", None),
            P("tensor", None),
        ),
        check_vma=False,
    )
```

```python
import functools

import jax
import jax.numpy as jnp
from jax import lax
from jax.experimental import pallas as pl
from jax.experimental.pallas import tpu as pltpu
from jax.sharding import PartitionSpec as P

D = 2432
F = 1216
ROWS = 1024


FIRST_CORRECTION = 0.9999734386011124
SECOND_CORRECTION = 0.0952078529183

OUTER = 4
HALF_BITS = 15.0
TILE = 256
LANES = 128

NT = (((1,), (1,)), ((), ()))
NN = (((1,), (0,)), ((), ()))

SMEM = pl.BlockSpec(memory_space=pltpu.SMEM)
VMEM = pl.BlockSpec(memory_space=pltpu.VMEM)
ANY = pl.BlockSpec(memory_space=pl.ANY)


def adam_update(grad, squares, master, first, second):
    clip = jnp.minimum(1.0, jnp.sqrt(jnp.float32(D * F)) / jnp.sqrt(squares + 1e-06))
    clipped = grad * clip
    new_first = 0.9 * first + 0.1 * clipped
    new_second = 0.999 * second + 0.001 * clipped * clipped
    step_dir = new_first / FIRST_CORRECTION / (jnp.sqrt(new_second / SECOND_CORRECTION) + 1e-08)
    new_master = master * (1.0 - 0.01 * 0.01) - 0.01 * step_dir
    return (new_master, new_first, new_second)


def dot(a, b, dims):
    return lax.dot_general(a, b, dims, preferred_element_type=jnp.float32)


def identity(size):
    rows = lax.broadcasted_iota(jnp.int32, (size, size), 0)
    cols = lax.broadcasted_iota(jnp.int32, (size, size), 1)
    return jnp.where(rows == cols, 1.0, 0.0).astype(jnp.bfloat16)


def array(shape, dtype):
    return jax.ShapeDtypeStruct(shape, dtype)


def call(kernel, out_shape, *operands, mib=12, **kwargs):
    return pl.pallas_call(
        kernel,
        out_shape=out_shape,
        compiler_params=pltpu.CompilerParams(vmem_limit_bytes=mib * 1024 * 1024),
        cost_estimate=pl.CostEstimate(flops=0, bytes_accessed=0, transcendentals=0),
        **kwargs,
    )(*operands)


def solution(mesh):
    n_dp, n_tensor = mesh.shape["dp"], mesh.shape["tensor"]
    inner = n_dp // (2 * OUTER)
    width = D // n_dp

    def split(p):
        return (p >> inner.bit_length()) & (OUTER - 1), (p >> 1) & (inner - 1), p & 1

    def join(z, m, c):
        return (z * inner + m) * 2 + c

    def move_dp(value, where):
        perm = [(p, join(*where(*split(p)))) for p in range(n_dp)]
        return lax.ppermute(value, "dp", perm)

    def to_plane(value, k):
        return move_dp(value, lambda z, m, c: (z ^ k, m, c))

    def to_middle(value, k):
        return move_dp(value, lambda z, m, c: (z, (m + k) & (inner - 1), c))

    def to_core(value):
        return move_dp(value, lambda z, m, c: (z, m, 1 - c))

    def from_tensor(value, k):
        perm = [(s, (s - k) & (n_tensor - 1)) for s in range(n_tensor)]
        return lax.ppermute(value, "tensor", perm)

    def from_diagonal(value, k):
        perm = []
        for p in range(n_dp):
            z, m, c = split(p)
            for t in range(n_tensor):
                target = join(z, m, 1 - c) * n_tensor + ((t - k) & (n_tensor - 1))
                perm.append((p * n_tensor + t, target))
        return lax.ppermute(value, ("dp", "tensor"), perm)

    def my_place():
        return split(lax.axis_index("dp"))

    def relative(p):
        z, m, c = split(p)
        my_z, my_m, my_c = my_place()
        return z ^ my_z, (m - my_m) & (inner - 1), c ^ my_c

    def owner(k, i, other):
        z, m, c = my_place()
        return join(z ^ k, (m + i) & (inner - 1), c ^ other)

    def first_row(j, r):
        start = ((lax.axis_index("tensor") + j) & (n_tensor - 1)) * r
        return pl.multiple_of(start, LANES)

    def turn(cot, by_planes):
        r = cot.shape[0]
        step = min(r, TILE)
        count = 4 if by_planes else 2
        lead = (2, inner) if by_planes else (inner, OUTER)

        def kernel(cot_ref, *refs):
            out_refs, wide_ref = refs[:count], refs[count]
            eye = identity(TILE)
            for start in range(0, D, TILE):
                size = min(TILE, D - start)
                wide_ref[start : start + size, :] = dot(
                    eye[:size, :size], cot_ref[:, start : start + size], NT
                )
            for p in range(n_dp):
                k, i, other = relative(p)
                block = wide_ref[p * width : (p + 1) * width, :].astype(jnp.bfloat16)
                which, at = other, (i, k)
                if by_planes:
                    even = 1 - (k & 1)
                    which, at = 2 * even + other, ((k >> 1) ^ even, i)
                for n in range(count):

                    @pl.when(which == n)
                    def _(n=n, at=at, block=block):
                        out_refs[n][at] = block

        return call(
            kernel,
            [array((*lead, width, r), jnp.bfloat16)] * count,
            cot,
            grid=(r // step,),
            in_specs=[pl.BlockSpec((step, D), lambda s: (s, 0))],
            out_specs=[
                pl.BlockSpec((*lead, width, step), lambda s: (*(0 for _ in lead), 0, s))
            ] * count,
            scratch_shapes=[pltpu.VMEM((D, step), jnp.float32)],
        )

    def prepare(net, act, scales, r, together):
        f = act.shape[0]
        lead = (n_tensor,) if together else (1,)
        count = 1 if together else n_tensor

        def kernel(scale_ref, act_ref, *out_refs):
            for j in range(n_tensor):
                part = act_ref[:, pl.ds(first_row(j, r), r)].astype(jnp.float32)
                part = (part * scale_ref[net]).astype(jnp.bfloat16)
                if together:
                    out_refs[0][j] = part
                else:
                    out_refs[j][0] = part

        return call(
            kernel, [array((*lead, f, r), jnp.bfloat16)] * count, scales, act,
            in_specs=[SMEM, VMEM], out_specs=[VMEM] * count,
        )

    def multiply(pieces, scaled, places):
        lead, r, f = pieces[0].shape[:-1], pieces[0].shape[-1], scaled[0].shape[1]
        pieces = [piece.reshape(-1, r) for piece in pieces]
        rows = pieces[0].shape[0]
        step = D // (2 * OUTER)
        count = len(pieces)

        def kernel(*refs):
            piece_refs, scaled_refs = refs[:count], refs[count:-2]
            out_ref, power_ref = refs[-2:]
            most = jnp.zeros((8, f), jnp.float32)
            for start in range(0, rows, step):
                part = slice(start, start + step)
                total = None
                for piece_ref, (n, j) in zip(piece_refs, places):
                    term = dot(piece_ref[part], scaled_refs[n][j], NT)
                    total = term if total is None else total + term
                out_ref[part] = total
                top = jnp.max(jnp.abs(total).reshape(step // 8, 8, f), axis=0)
                most = jnp.maximum(most, top)
            most = jnp.full((8, LANES), jnp.maximum(jnp.max(most), 1e-30))
            power_ref[...] = jnp.floor(jnp.log2(most)) + 2.0

        out, power = call(
            kernel, [array((rows, f), jnp.float32), array((8, LANES), jnp.float32)],
            *pieces, *scaled,
            in_specs=[VMEM] * (count + len(scaled)), out_specs=[VMEM] * 2,
        )
        return out.reshape(*lead, f), power[0, 0]

    def norms(total_s, total_f):
        def kernel(s_ref, f_ref, out_ref):
            sums = [jnp.sum(ref[...] * ref[...]) for ref in (s_ref, f_ref)]
            rows = lax.broadcasted_iota(jnp.int32, (8, LANES), 0)
            out_ref[...] = jnp.where(rows == 0, *sums)

        return call(
            kernel, array((8, LANES), jnp.float32), total_s, total_f,
            in_specs=[VMEM] * 2, out_specs=VMEM,
        )

    def update(squares, totals, states):
        shape = states[0].shape

        def kernel(squares_ref, *refs):
            total_refs, state_refs, (own_ref, *out_refs) = refs[:2], refs[2:8], refs[8:]
            for net in range(2):
                new = adam_update(
                    total_refs[net][...],
                    squares_ref[net : net + 1, :1],
                    *(ref[...] for ref in state_refs[3 * net : 3 * net + 3]),
                )
                own_ref[net] = new[0].astype(jnp.bfloat16)
                for ref, value in zip(out_refs[3 * net :], new):
                    ref[...] = value

        own, *new = call(
            kernel,
            [array((2, *shape), jnp.bfloat16)] + [array(shape, jnp.float32)] * 6,
            squares, *totals, *states,
            in_specs=[VMEM] * 9,
            out_specs=[VMEM] * 7,
        )
        return own, new

    def back_part(whole, weight, pieces, scales, net, j, low, size, r, count):
        f = weight.shape[0]
        turned = len(pieces) > 1

        def kernel(scale_ref, weight_ref, *refs):
            piece_refs = refs[: len(pieces)]
            if turned:
                out_ref, done_ref, sem, wide_ref = refs[-4:]
                for k in range(OUTER):
                    for other in range(2):
                        for i in range(inner):
                            even = 1 - (k & 1)
                            block = piece_refs[2 * even + other][(k >> 1) ^ even, i]
                            block = block.astype(jnp.float32)
                            wide_ref[owner(k, i, other)] = block
                flat = wide_ref[...].reshape(D, size).astype(jnp.bfloat16)
                product = dot(weight_ref[...], flat, NN)
            else:
                out_ref, done_ref, sem = refs[-3:]
                product = dot(weight_ref[...], piece_refs[0][...], NT)
            done_ref[...] = (product * scale_ref[net]).astype(jnp.bfloat16)
            start = pl.multiple_of(first_row(j, r) + low, LANES)
            copy = pltpu.make_async_copy(done_ref, out_ref.at[:, pl.ds(start, size)], sem)
            copy.start()
            copy.wait()

        scratch = [pltpu.VMEM((f, size), jnp.bfloat16), pltpu.SemaphoreType.DMA]
        if turned:
            scratch.append(pltpu.VMEM((n_dp, width, size), jnp.float32))
        operands = [scales, weight, *pieces]
        in_specs = [SMEM] + [VMEM] * (len(operands) - 1)
        aliases = {}
        if whole is not None:
            aliases = {len(operands): 0}
            operands.append(whole)
            in_specs.append(ANY)
        return call(
            kernel, array((f, count), jnp.bfloat16), *operands,
            in_specs=in_specs, out_specs=ANY, scratch_shapes=scratch,
            input_output_aliases=aliases, mib=20,
        )

    def spread(stacks):
        count, _, _, f = stacks[0].shape
        tiles = [
            (net, start, min(TILE, f - start)) for net in range(2) for start in range(0, f, TILE)
        ]

        def kernel(*refs):
            stack_refs, out_refs, (wide_ref, done_ref, sem) = refs[:4], refs[4:6], refs[6:]
            eye = identity(TILE)
            copies = []
            for step, (net, start, size) in enumerate(tiles):
                for n, ref in enumerate(stack_refs):
                    for at in range(count):
                        k, i = divmod((n & 1) * count + at, inner)
                        block = ref[at, net, :, start : start + size].astype(jnp.float32)
                        wide_ref[owner(k, i, n >> 1), :, :size] = block
                flat = wide_ref[:, :, :size].reshape(D, size).astype(jnp.bfloat16)
                slot = step & 1
                if step >= 2:
                    copies[step - 2].wait()
                done_ref[slot, :size, :] = dot(eye[:size, :size], flat, NT).astype(jnp.bfloat16)
                copy = pltpu.make_async_copy(
                    done_ref.at[slot, pl.ds(0, size)],
                    out_refs[net].at[pl.ds(start, size)],
                    sem.at[slot],
                )
                copy.start()
                copies.append(copy)
            for copy in copies[-2:]:
                copy.wait()

        return call(
            kernel, [array((f, D), jnp.bfloat16)] * 2, *stacks,
            in_specs=[VMEM] * 4, out_specs=[ANY] * 2,
            scratch_shapes=[
                pltpu.VMEM((n_dp, width, TILE), jnp.float32),
                pltpu.VMEM((2, TILE, D), jnp.bfloat16),
                pltpu.SemaphoreType.DMA((2,)),
            ],
            mib=24,
        )

    def per_device(
        cot_student, cot_fake, act_student, act_fake, weight_student, weight_fake,
        master_student, first_student, second_student, master_fake, first_fake, second_fake,
        timesteps,
    ):
        f, count = act_student.shape
        r = cot_student.shape[0]
        assert timesteps.shape[2] == 1 and count == ROWS

        token = []

        def step(work, *inputs):
            if token:
                *inputs, _ = lax.optimization_barrier((*inputs, token[0]))
            out = work(*inputs)
            token[:] = jax.tree.leaves(out)[:1]
            return out

        def reduced(combine, value, got):
            return step(lambda *values: functools.reduce(combine, values), value, *got)

        def hops(value, combine):
            distance = 1
            while distance < n_dp:
                perm = [(p, p ^ distance) for p in range(n_dp)]
                got = lax.ppermute(value, "dp", perm)
                yield
                value = step(combine, value, got)
                distance *= 2
            yield value

        scales = step(
            lambda steps: 1.0 / (0.1 + steps.astype(jnp.float32) / 1000.0), timesteps[0, :, 0]
        )
        scaled_own, *sent = step(lambda act: prepare(1, act, scales, r, False), act_fake)
        acts = [from_tensor(value, -j) for j, value in enumerate(sent, 1)]
        scaled_fake = [[value, to_core(value)] for value in (scaled_own, *acts)]
        fake_blocks = step(lambda cot: turn(cot, False), cot_fake)
        mate_blocks = to_core(fake_blocks[1])
        (scaled_student,) = step(lambda act: prepare(0, act, scales, r, True), act_student)
        planes = step(lambda cot: turn(cot, True), cot_student)

        same, diagonal = [], []

        def send_planes(g, own, other):
            same.append([from_tensor(own, j) for j in range(1, n_tensor)])
            diagonal.append([from_diagonal(other, j) for j in range(1, n_tensor)])

        send_planes(0, planes[0], planes[1])

        def shrink(value, power):
            scaled = value * jnp.exp2(HALF_BITS - power)
            width_more = [(0, 0)] * (value.ndim - 1) + [(0, 1)]
            lanes = lax.broadcasted_iota(jnp.int32, (*value.shape[:-1], f + 1), value.ndim - 1)
            return jnp.where(lanes == f, power, jnp.pad(scaled, width_more)).astype(jnp.float16)

        def widen(value):
            power = value.reshape(-1)[f].astype(jnp.float32)
            return value[..., :f].astype(jnp.float32) * jnp.exp2(power - HALF_BITS), power

        def add(total, power, values):
            for value in values:
                value, other = widen(value)
                total, power = total + value, jnp.maximum(power, other) + 1.0
            return total, power

        fake_own, fake_got = {}, {}

        def fake_middle(j):
            def work(both, power):
                return [shrink(both[i], power) for i in range(1, inner)], (both[0], power)

            both = step(
                lambda a, b, c, d: multiply([a, b], [c, d], [(0, 0), (1, 0)]),
                fake_blocks[0], mate_blocks, *scaled_fake[j],
            )
            sent, fake_own[j] = step(work, *both)
            fake_got[j] = [to_middle(value, i) for i, value in enumerate(sent, 1)]

        def fake_near(j):
            def work(own, power, *got):
                own, power = add(own, power, got)
                return shrink(own[1::2], power), (own[0::2], power)

            sent, fake_own[j] = step(work, *fake_own[j], *fake_got[j])
            fake_got[j] = [to_plane(sent, 1)]

        def fake_far(j):
            def work(own, power, *got):
                own, power = add(own, power, got)
                return shrink(own[1], power), (own[0], power)

            sent, fake_own[j] = step(work, *fake_own[j], *fake_got[j])
            fake_got[j] = [to_plane(sent, 2)]

        def fake_total(j):
            return step(
                lambda own, power, *got: add(own, power, got)[0], *fake_own[j], *fake_got[j]
            )

        mate_student = to_core(scaled_student)
        mate_planes = [to_core(planes[1]), to_core(planes[3])]
        for j in range(n_tensor):
            fake_middle(j)
        mate_student, *mate_planes = step(lambda *values: values, mate_student, *mate_planes)

        def back(whole, net, pieces, j, low, size):
            weight = (weight_student, weight_fake)[net]
            has = [] if whole is None else [whole]

            def work(weight, *values):
                return back_part(
                    values[-1] if has else None, weight, values[: len(pieces)], scales,
                    net, j, low, size, r, count,
                )

            return step(work, weight, *pieces, *has)

        def multiply_student(g):
            pieces, places = [planes[2 * g], mate_planes[g]], [(0, 0), (1, 0)]
            for j in range(1, n_tensor):
                pieces += [same[g][j - 1], diagonal[g][j - 1]]
                places += [(0, j), (1, j)]
            return step(
                lambda *values: multiply(values[:-2], values[-2:], places),
                *pieces, scaled_student, mate_student,
            )

        back_student = back(None, 0, [cot_student], 0, 0, r)
        send_planes(1, *step(lambda a, b: (a, b), planes[2], planes[3]))
        back_fake = back(None, 1, [cot_fake], 0, 0, r)
        both = multiply_student(0)

        def first_middle(both, power):
            return [shrink(both[:, i], power) for i in range(1, inner)], both[:, 0], power

        sent, own, power = step(first_middle, *both)
        got = [to_middle(value, i) for i, value in enumerate(sent, 1)]
        for j in range(n_tensor):
            fake_near(j)
        near = to_plane(
            step(lambda own, power, *got: shrink(*add(own, power, got)), own, power, *got), 1
        )
        for j in range(n_tensor):
            fake_far(j)
        both = multiply_student(1)

        def second_middle(both, power):
            sent = [[shrink(both[n, i], power) for i in range(1, inner)] for n in range(2)]
            return sent, both[0, 0], both[1, 0], power

        sent, own_far, own, power = step(second_middle, *both)
        got_far, got = (
            [to_middle(value, i) for i, value in enumerate(values, 1)] for values in sent
        )
        fake_mine = fake_total(0)
        fake_others = [fake_total(j) for j in range(1, n_tensor)]
        others_got = [from_tensor(value, j) for j, value in enumerate(fake_others, 1)]

        def far_plane(own, power, near, *got):
            return shrink(*add(own, power, [near[1], *got]))

        far = to_plane(step(far_plane, own_far, power, near, *got_far), 2)
        total_student = step(
            lambda own, power, near, *got: add(own, power, [near[0], *got])[0],
            own, power, near, *got,
        )
        total_fake = reduced(jnp.add, fake_mine, others_got)
        total_student = step(lambda own, got: own + widen(got)[0], total_student, far)
        squares = step(norms, total_student, total_fake)
        squares = reduced(
            jnp.add, squares, [from_tensor(squares, j) for j in range(1, n_tensor)]
        )

        rows = step(lambda cot: cot, cot_fake)
        raw = [from_tensor(rows, j) for j in range(1, n_tensor)]

        hidden = step(lambda *values: values, *[value for group in diagonal for value in group])
        mate_others = [to_core(value) for value in hidden]
        *_, squares = hops(squares, jnp.add)
        squares, *mate_others = step(lambda *values: values, squares, *mate_others)
        mate_others = [mate_others[: n_tensor - 1], mate_others[n_tensor - 1 :]]
        states = (
            master_student, first_student, second_student, master_fake, first_fake, second_fake,
        )
        own, updated = step(
            lambda squares, *values: update(squares, values[:2], values[2:]),
            squares, total_student, total_fake, *(state.T for state in states),
        )

        mine = {}

        def spread_middle(k, value):
            mine[k] = [value] + [to_middle(value, -i) for i in range(1, inner)]

        spread_middle(0, own)
        planes_got = {k: to_plane(own, k) for k in (1, 3, 2)}
        spread_middle(1, step(lambda value: value, planes_got[1]))
        spread_middle(3, step(lambda value: value, planes_got[3]))
        first_half = step(lambda *values: jnp.stack(values), *mine[0], *mine[1])
        theirs = [to_core(first_half)]
        for j in range(1, n_tensor):
            pieces = [
                piece for g in range(2) for piece in (same[g][j - 1], mate_others[g][j - 1])
            ]
            back_student = back(back_student, 0, pieces, j, 0, r)
        spread_middle(2, step(lambda value: value, planes_got[2]))
        for j in range(1, n_tensor):
            back_fake = back(back_fake, 1, [raw[j - 1]], j, 0, r)
        second_half = step(lambda *values: jnp.stack(values), *mine[2], *mine[3])
        theirs.append(to_core(second_half))
        stacks = [first_half, second_half, *theirs]
        params = step(lambda *values: spread(values), *stacks)

        new_states = [value.T for value in updated]
        return (back_student, back_fake, *new_states, *params)

    placed = (
        P(("dp", "tensor"), None),
        P(("dp", "tensor"), None),
        P("tensor", "dp"),
        P("tensor", "dp"),
        P("tensor", None),
        P("tensor", None),
        P("tensor", "dp"),
        P("tensor", "dp"),
        P("tensor", "dp"),
        P("tensor", "dp"),
        P("tensor", "dp"),
        P("tensor", "dp"),
        P("dp", None, None),
    )
    return jax.shard_map(
        per_device,
        mesh=mesh,
        in_specs=placed,
        out_specs=(
            P("tensor", "dp"),
            P("tensor", "dp"),
            P("tensor", "dp"),
            P("tensor", "dp"),
            P("tensor", "dp"),
            P("tensor", "dp"),
            P("tensor", "dp"),
            P("tensor", "dp"),
            P("tensor", None),
            P("tensor", None),
        ),
        check_vma=False,
    )
```

```python
import functools

import jax
import jax.numpy as jnp
from jax import lax
from jax.experimental import pallas as pl
from jax.experimental.pallas import tpu as pltpu
from jax.sharding import PartitionSpec as P

D = 2432
F = 1216
ROWS = 1024


FIRST_CORRECTION = 0.9999734386011124
SECOND_CORRECTION = 0.0952078529183

OUTER = 4
HALF_LIMIT = 60000.0
TILE = 256
LANES = 128

NT = (((1,), (1,)), ((), ()))
NN = (((1,), (0,)), ((), ()))

SMEM = pl.BlockSpec(memory_space=pltpu.SMEM)
VMEM = pl.BlockSpec(memory_space=pltpu.VMEM)
ANY = pl.BlockSpec(memory_space=pl.ANY)


def adam_update(grad, squares, master, first, second):
    clip = jnp.minimum(1.0, jnp.sqrt(jnp.float32(D * F)) / jnp.sqrt(squares + 1e-06))
    clipped = grad * clip
    new_first = 0.9 * first + 0.1 * clipped
    new_second = 0.999 * second + 0.001 * clipped * clipped
    step_dir = new_first / FIRST_CORRECTION / (jnp.sqrt(new_second / SECOND_CORRECTION) + 1e-08)
    new_master = master * (1.0 - 0.01 * 0.01) - 0.01 * step_dir
    return (new_master, new_first, new_second)


def dot(a, b, dims):
    return lax.dot_general(a, b, dims, preferred_element_type=jnp.float32)


def identity(size):
    rows = lax.broadcasted_iota(jnp.int32, (size, size), 0)
    cols = lax.broadcasted_iota(jnp.int32, (size, size), 1)
    return jnp.where(rows == cols, 1.0, 0.0).astype(jnp.bfloat16)


def array(shape, dtype):
    return jax.ShapeDtypeStruct(shape, dtype)


def call(kernel, out_shape, *operands, mib=12, **kwargs):
    return pl.pallas_call(
        kernel,
        out_shape=out_shape,
        compiler_params=pltpu.CompilerParams(vmem_limit_bytes=mib * 1024 * 1024),
        cost_estimate=pl.CostEstimate(flops=0, bytes_accessed=0, transcendentals=0),
        **kwargs,
    )(*operands)


def solution(mesh):
    n_dp, n_tensor = mesh.shape["dp"], mesh.shape["tensor"]
    inner = n_dp // (2 * OUTER)
    width = D // n_dp

    def split(p):
        return (p >> inner.bit_length()) & (OUTER - 1), (p >> 1) & (inner - 1), p & 1

    def join(z, m, c):
        return (z * inner + m) * 2 + c

    def move_dp(value, where):
        perm = [(p, join(*where(*split(p)))) for p in range(n_dp)]
        return lax.ppermute(value, "dp", perm)

    def to_plane(value, k):
        return move_dp(value, lambda z, m, c: (z ^ k, m, c))

    def to_middle(value, k):
        return move_dp(value, lambda z, m, c: (z, (m + k) & (inner - 1), c))

    def to_core(value):
        return move_dp(value, lambda z, m, c: (z, m, 1 - c))

    def from_tensor(value, k):
        perm = [(s, (s - k) & (n_tensor - 1)) for s in range(n_tensor)]
        return lax.ppermute(value, "tensor", perm)

    def from_diagonal(value, k):
        perm = []
        for p in range(n_dp):
            z, m, c = split(p)
            for t in range(n_tensor):
                target = join(z, m, 1 - c) * n_tensor + ((t - k) & (n_tensor - 1))
                perm.append((p * n_tensor + t, target))
        return lax.ppermute(value, ("dp", "tensor"), perm)

    def my_place():
        return split(lax.axis_index("dp"))

    def relative(p):
        z, m, c = split(p)
        my_z, my_m, my_c = my_place()
        return z ^ my_z, (m - my_m) & (inner - 1), c ^ my_c

    def owner(k, i, other):
        z, m, c = my_place()
        return join(z ^ k, (m + i) & (inner - 1), c ^ other)

    def first_row(j, r):
        start = ((lax.axis_index("tensor") + j) & (n_tensor - 1)) * r
        return pl.multiple_of(start, LANES)

    def turn(cot, by_planes):
        r = cot.shape[0]
        step = min(r, TILE)
        count = 4 if by_planes else 2
        lead = (2, inner) if by_planes else (inner, OUTER)

        def kernel(cot_ref, *refs):
            out_refs, (top_ref, wide_ref) = refs[:count], refs[count:]
            eye = identity(TILE)
            for start in range(0, D, TILE):
                size = min(TILE, D - start)
                wide_ref[start : start + size, :] = dot(
                    eye[:size, :size], cot_ref[:, start : start + size], NT
                )
            top = jnp.max(jnp.abs(wide_ref[...]).reshape(D // 8, 8, step), axis=0)
            top = jnp.broadcast_to(jnp.max(top), (8, LANES))

            @pl.when(pl.program_id(0) == 0)
            def _():
                top_ref[...] = top

            @pl.when(pl.program_id(0) > 0)
            def _():
                top_ref[...] = jnp.maximum(top_ref[...], top)

            for p in range(n_dp):
                k, i, other = relative(p)
                block = wide_ref[p * width : (p + 1) * width, :].astype(jnp.bfloat16)
                which, at = other, (i, k)
                if by_planes:
                    even = 1 - (k & 1)
                    which, at = 2 * even + other, ((k >> 1) ^ even, i)
                for n in range(count):

                    @pl.when(which == n)
                    def _(n=n, at=at, block=block):
                        out_refs[n][at] = block

        *outs, top = call(
            kernel,
            [array((*lead, width, r), jnp.bfloat16)] * count + [array((8, LANES), jnp.float32)],
            cot,
            grid=(r // step,),
            in_specs=[pl.BlockSpec((step, D), lambda s: (s, 0))],
            out_specs=[
                pl.BlockSpec((*lead, width, step), lambda s: (*(0 for _ in lead), 0, s))
            ] * count
            + [pl.BlockSpec((8, LANES), lambda s: (0, 0))],
            scratch_shapes=[pltpu.VMEM((D, step), jnp.float32)],
        )
        return outs, top

    def prepare_fake(act, scales, r):
        f = act.shape[0]

        def kernel(scale_ref, act_ref, top_ref, *out_refs):
            most = jnp.max(jnp.abs(act_ref[...].astype(jnp.float32)))
            top_ref[...] = jnp.full((8, LANES), most * scale_ref[1])
            for j, out_ref in enumerate(out_refs):
                part = act_ref[:, pl.ds(first_row(j, r), r)].astype(jnp.float32)
                out_ref[0] = (part * scale_ref[1]).astype(jnp.bfloat16)

        return call(
            kernel,
            [array((8, LANES), jnp.float32)] + [array((1, f, r), jnp.bfloat16)] * n_tensor,
            scales, act,
            in_specs=[SMEM, VMEM], out_specs=[VMEM] * (1 + n_tensor),
        )

    def prepare_student(act, top_s, top_f, top_act_f, scales, r):
        f = act.shape[0]

        def kernel(scale_ref, act_ref, top_s_ref, top_f_ref, top_act_f_ref, top_ref, out_ref):
            most = jnp.max(jnp.abs(act_ref[...].astype(jnp.float32)))
            most = jnp.full((8, LANES), most * scale_ref[0])
            rows = lax.broadcasted_iota(jnp.int32, (8, LANES), 0)
            tops = jnp.where(rows == 0, top_s_ref[...], most)
            tops = jnp.where(rows == 2, top_f_ref[...], tops)
            top_ref[...] = jnp.where(rows == 3, top_act_f_ref[...], tops)
            for j in range(n_tensor):
                part = act_ref[:, pl.ds(first_row(j, r), r)].astype(jnp.float32)
                out_ref[j] = (part * scale_ref[0]).astype(jnp.bfloat16)

        return call(
            kernel,
            [array((8, LANES), jnp.float32), array((n_tensor, f, r), jnp.bfloat16)],
            scales, act, top_s, top_f, top_act_f,
            in_specs=[SMEM] + [VMEM] * 4, out_specs=[VMEM] * 2,
        )

    def multiply(pieces, scaled, places):
        lead, r, f = pieces[0].shape[:-1], pieces[0].shape[-1], scaled[0].shape[1]
        pieces = [piece.reshape(-1, r) for piece in pieces]
        rows = pieces[0].shape[0]
        step = D // (2 * OUTER)
        count = len(pieces)

        def kernel(*refs):
            piece_refs, scaled_refs, out_ref = refs[:count], refs[count:-1], refs[-1]
            for start in range(0, rows, step):
                part = slice(start, start + step)
                total = None
                for piece_ref, (n, j) in zip(piece_refs, places):
                    term = dot(piece_ref[part], scaled_refs[n][j], NT)
                    total = term if total is None else total + term
                out_ref[part] = total

        out = call(
            kernel, array((rows, f), jnp.float32), *pieces, *scaled,
            in_specs=[VMEM] * (count + len(scaled)), out_specs=VMEM,
        )
        return out.reshape(*lead, f)

    def norms(total_s, total_f):
        def kernel(s_ref, f_ref, out_ref):
            sums = [jnp.sum(ref[...] * ref[...]) for ref in (s_ref, f_ref)]
            rows = lax.broadcasted_iota(jnp.int32, (8, LANES), 0)
            out_ref[...] = jnp.where(rows == 0, *sums)

        return call(
            kernel, array((8, LANES), jnp.float32), total_s, total_f,
            in_specs=[VMEM] * 2, out_specs=VMEM,
        )

    def update(squares, totals, states):
        shape = totals[0].shape

        def kernel(squares_ref, *refs):
            total_refs, state_refs, (own_ref, *out_refs) = refs[:2], refs[2:8], refs[8:]
            for net in range(2):
                new = adam_update(
                    total_refs[net][...],
                    squares_ref[net : net + 1, :1],
                    *(ref[...] for ref in state_refs[3 * net : 3 * net + 3]),
                )
                own_ref[net] = new[0].astype(jnp.bfloat16)
                for ref, value in zip(out_refs[3 * net :], new):
                    ref[...] = value

        own, *new = call(
            kernel,
            [array((2, *shape), jnp.bfloat16)] + [array(shape, jnp.float32)] * 6,
            squares, *totals, *states,
            in_specs=[VMEM] * 9,
            out_specs=[VMEM] * 7,
        )
        return own, new

    def back_part(whole, weight, pieces, scales, net, j, low, size, r, count):
        f = weight.shape[0]
        turned = len(pieces) > 1

        def kernel(scale_ref, weight_ref, *refs):
            piece_refs = refs[: len(pieces)]
            if turned:
                out_ref, done_ref, sem, wide_ref = refs[-4:]
                for k in range(OUTER):
                    for other in range(2):
                        for i in range(inner):
                            even = 1 - (k & 1)
                            block = piece_refs[2 * even + other][(k >> 1) ^ even, i]
                            block = block.astype(jnp.float32)
                            wide_ref[owner(k, i, other)] = block
                flat = wide_ref[...].reshape(D, size).astype(jnp.bfloat16)
                product = dot(weight_ref[...], flat, NN)
            else:
                out_ref, done_ref, sem = refs[-3:]
                product = dot(weight_ref[...], piece_refs[0][...], NT)
            done_ref[...] = (product * scale_ref[net]).astype(jnp.bfloat16)
            start = pl.multiple_of(first_row(j, r) + low, LANES)
            copy = pltpu.make_async_copy(done_ref, out_ref.at[:, pl.ds(start, size)], sem)
            copy.start()
            copy.wait()

        scratch = [pltpu.VMEM((f, size), jnp.bfloat16), pltpu.SemaphoreType.DMA]
        if turned:
            scratch.append(pltpu.VMEM((n_dp, width, size), jnp.float32))
        operands = [scales, weight, *pieces]
        in_specs = [SMEM] + [VMEM] * (len(operands) - 1)
        aliases = {}
        if whole is not None:
            aliases = {len(operands): 0}
            operands.append(whole)
            in_specs.append(ANY)
        return call(
            kernel, array((f, count), jnp.bfloat16), *operands,
            in_specs=in_specs, out_specs=ANY, scratch_shapes=scratch,
            input_output_aliases=aliases, mib=20,
        )

    def spread(stacks):
        count, _, _, f = stacks[0].shape
        tiles = [
            (net, start, min(TILE, f - start)) for net in range(2) for start in range(0, f, TILE)
        ]

        def kernel(*refs):
            stack_refs, out_refs, (wide_ref, done_ref, sem) = refs[:4], refs[4:6], refs[6:]
            eye = identity(TILE)
            copies = []
            for step, (net, start, size) in enumerate(tiles):
                for n, ref in enumerate(stack_refs):
                    for at in range(count):
                        k, i = divmod((n & 1) * count + at, inner)
                        block = ref[at, net, :, start : start + size].astype(jnp.float32)
                        wide_ref[owner(k, i, n >> 1), :, :size] = block
                flat = wide_ref[:, :, :size].reshape(D, size).astype(jnp.bfloat16)
                slot = step & 1
                if step >= 2:
                    copies[step - 2].wait()
                done_ref[slot, :size, :] = dot(eye[:size, :size], flat, NT).astype(jnp.bfloat16)
                copy = pltpu.make_async_copy(
                    done_ref.at[slot, pl.ds(0, size)],
                    out_refs[net].at[pl.ds(start, size)],
                    sem.at[slot],
                )
                copy.start()
                copies.append(copy)
            for copy in copies[-2:]:
                copy.wait()

        return call(
            kernel, [array((f, D), jnp.bfloat16)] * 2, *stacks,
            in_specs=[VMEM] * 4, out_specs=[ANY] * 2,
            scratch_shapes=[
                pltpu.VMEM((n_dp, width, TILE), jnp.float32),
                pltpu.VMEM((2, TILE, D), jnp.bfloat16),
                pltpu.SemaphoreType.DMA((2,)),
            ],
            mib=24,
        )

    def per_device(
        cot_student, cot_fake, act_student, act_fake, weight_student, weight_fake,
        master_student, first_student, second_student, master_fake, first_fake, second_fake,
        timesteps,
    ):
        f, count = act_student.shape
        r = cot_student.shape[0]
        assert timesteps.shape[2] == 1 and count == ROWS

        token = []

        def step(work, *inputs):
            if token:
                *inputs, _ = lax.optimization_barrier((*inputs, token[0]))
            out = work(*inputs)
            token[:] = jax.tree.leaves(out)[:1]
            return out

        def reduced(combine, value, got):
            return step(lambda *values: functools.reduce(combine, values), value, *got)

        def hops(value, combine, *axes):
            for axis in axes:
                distance = 1
                while distance < mesh.shape[axis]:
                    perm = [(p, p ^ distance) for p in range(mesh.shape[axis])]
                    got = lax.ppermute(value, axis, perm)
                    yield
                    value = step(combine, value, got)
                    distance *= 2
            yield value

        scales = step(
            lambda steps: 1.0 / (0.1 + steps.astype(jnp.float32) / 1000.0), timesteps[0, :, 0]
        )
        top_act, scaled_own, *sent = step(lambda act: prepare_fake(act, scales, r), act_fake)
        acts = [from_tensor(value, -j) for j, value in enumerate(sent, 1)]
        scaled_fake = [[scaled_own, to_core(scaled_own)]]
        fake_blocks, top_fake = step(lambda cot: turn(cot, False), cot_fake)
        mate_blocks = to_core(fake_blocks[1])
        planes, top_student = step(lambda cot: turn(cot, True), cot_student)

        same, diagonal = [], []

        def send_planes(g, own, other):
            same.append([from_tensor(own, j) for j in range(1, n_tensor)])
            diagonal.append([from_diagonal(other, j) for j in range(1, n_tensor)])

        tops, scaled_student = step(
            lambda *values: prepare_student(*values, scales, r),
            act_student, top_student, top_fake, top_act,
        )
        tops = hops(tops, jnp.maximum, "tensor", "dp")
        next(tops)
        send_planes(0, planes[0], planes[1])
        parts_fake = []

        def multiply_fake(j):
            parts_fake.append(
                step(
                    lambda a, b, c, d: multiply([a, b], [c, d], [(0, 0), (1, 0)]),
                    fake_blocks[0], mate_blocks, *scaled_fake[j],
                )
            )

        multiply_fake(0)
        acts = step(lambda *values: values, *acts)
        scaled_fake += [[act, to_core(act)] for act in acts]
        next(tops)
        next(tops)
        for j in range(1, n_tensor):
            multiply_fake(j)
        while (final := next(tops)) is None:
            pass

        def factors(tops):
            bounds = tops[0:3:2, 0] * tops[1:4:2, 0]
            bounds = jnp.maximum(bounds, 1e-30) * (1.01 * count * n_dp / HALF_LIMIT)
            return bounds, 1.0 / bounds

        grow, fit = step(factors, final)

        def shrink(value, net):
            return (value * fit[net]).astype(jnp.float16)

        def widen(value, net):
            return value.astype(jnp.float32) * grow[net]

        def add_widened(total, values, net):
            for value in values:
                total = total + widen(value, net)
            return total

        fake_own, fake_got = {}, {}

        def fake_middle(j):
            def work(both):
                sent = [shrink(both[i], 1) for i in range(1, inner)]
                return sent, both[0]

            sent, fake_own[j] = step(work, parts_fake[j])
            fake_got[j] = [to_middle(value, i) for i, value in enumerate(sent, 1)]

        def fake_near(j):
            def work(own, *got):
                own = add_widened(own, got, 1)
                return shrink(own[1::2], 1), own[0::2]

            sent, fake_own[j] = step(work, fake_own[j], *fake_got[j])
            fake_got[j] = [to_plane(sent, 1)]

        def fake_far(j):
            def work(own, *got):
                own = add_widened(own, got, 1)
                return shrink(own[1], 1), own[0]

            sent, fake_own[j] = step(work, fake_own[j], *fake_got[j])
            fake_got[j] = [to_plane(sent, 2)]

        def fake_total(j):
            return step(
                lambda own, *got: add_widened(own, got, 1), fake_own[j], *fake_got[j]
            )

        mate_student = to_core(scaled_student)
        mate_planes = [to_core(planes[1]), to_core(planes[3])]
        for j in range(n_tensor):
            fake_middle(j)
        mate_student, *mate_planes = step(lambda *values: values, mate_student, *mate_planes)

        def back(whole, net, pieces, j, low, size):
            weight = (weight_student, weight_fake)[net]
            has = [] if whole is None else [whole]

            def work(weight, *values):
                return back_part(
                    values[-1] if has else None, weight, values[: len(pieces)], scales,
                    net, j, low, size, r, count,
                )

            return step(work, weight, *pieces, *has)

        def multiply_student(g):
            pieces, places = [planes[2 * g], mate_planes[g]], [(0, 0), (1, 0)]
            for j in range(1, n_tensor):
                pieces += [same[g][j - 1], diagonal[g][j - 1]]
                places += [(0, j), (1, j)]
            return step(
                lambda *values: multiply(values[:-2], values[-2:], places),
                *pieces, scaled_student, mate_student,
            )

        back_student = back(None, 0, [cot_student], 0, 0, r)
        send_planes(1, *step(lambda a, b: (a, b), planes[2], planes[3]))
        back_fake = back(None, 1, [cot_fake], 0, 0, r)
        both = multiply_student(0)

        def first_middle(both):
            return [shrink(both[:, i], 0) for i in range(1, inner)], both[:, 0]

        sent, own = step(first_middle, both)
        got = [to_middle(value, i) for i, value in enumerate(sent, 1)]
        for j in range(n_tensor):
            fake_near(j)

        def first_planes(own, *got):
            return shrink(add_widened(own, got, 0), 0)

        near = to_plane(step(first_planes, own, *got), 1)
        for j in range(n_tensor):
            fake_far(j)
        both = multiply_student(1)

        def second_middle(both):
            sent = [[shrink(both[n, i], 0) for i in range(1, inner)] for n in range(2)]
            return sent, both[0, 0], both[1, 0]

        sent, own_far, own = step(second_middle, both)
        got_far, got = (
            [to_middle(value, i) for i, value in enumerate(values, 1)] for values in sent
        )
        fake_mine = fake_total(0)
        fake_others = [fake_total(j) for j in range(1, n_tensor)]
        others_got = [from_tensor(value, j) for j, value in enumerate(fake_others, 1)]

        def far_plane(own, near, *got):
            return shrink(add_widened(own, (near[1], *got), 0), 0)

        far = to_plane(step(far_plane, own_far, near, *got_far), 2)
        total_student = step(
            lambda own, near, *got: add_widened(own, (near[0], *got), 0), own, near, *got
        )
        total_fake = reduced(jnp.add, fake_mine, others_got)
        total_student = step(
            lambda own, got: add_widened(own, (got,), 0), total_student, far
        )
        squares = step(norms, total_student, total_fake)
        squares = reduced(
            jnp.add, squares, [from_tensor(squares, j) for j in range(1, n_tensor)]
        )

        rows = step(lambda cot: cot, cot_fake)
        raw = [from_tensor(rows, j) for j in range(1, n_tensor)]

        *_, squares = hops(squares, jnp.add, "dp")
        states = (
            master_student, first_student, second_student, master_fake, first_fake, second_fake,
        )
        own, updated = step(
            lambda squares, *values: update(squares, values[:2], values[2:]),
            squares, total_student, total_fake, *(state.T for state in states),
        )

        mine = {}

        def spread_middle(k, value):
            mine[k] = [value] + [to_middle(value, -i) for i in range(1, inner)]

        spread_middle(0, own)
        planes_got = {k: to_plane(own, k) for k in (1, 3, 2)}
        spread_middle(1, step(lambda value: value, planes_got[1]))
        spread_middle(3, step(lambda value: value, planes_got[3]))
        early = [value for k in (0, 1, 3) for value in mine[k]]
        early = step(lambda *values: values, *early)
        mine = {k: list(early[n * inner : (n + 1) * inner]) for n, k in enumerate((0, 1, 3))}
        spread_middle(2, step(lambda value: value, planes_got[2]))
        first_half = step(lambda *values: jnp.stack(values), *mine[0], *mine[1])
        theirs = [to_core(first_half)]
        hidden = step(lambda *values: values, *[value for group in diagonal for value in group])
        mate_others = [to_core(value) for value in hidden]
        mate_others = [mate_others[: n_tensor - 1], mate_others[n_tensor - 1 :]]
        for j in range(1, n_tensor):
            pieces = [
                piece for g in range(2) for piece in (same[g][j - 1], mate_others[g][j - 1])
            ]
            back_student = back(back_student, 0, pieces, j, 0, r)
        for j in range(1, n_tensor):
            back_fake = back(back_fake, 1, [raw[j - 1]], j, 0, r)
        second_half = step(lambda *values: jnp.stack(values), *mine[2], *mine[3])
        theirs.append(to_core(second_half))
        stacks = [first_half, second_half, *theirs]
        params = step(lambda *values: spread(values), *stacks)

        new_states = [value.T for value in updated]
        return (back_student, back_fake, *new_states, *params)

    placed = (
        P(("dp", "tensor"), None),
        P(("dp", "tensor"), None),
        P("tensor", "dp"),
        P("tensor", "dp"),
        P("tensor", None),
        P("tensor", None),
        P("tensor", "dp"),
        P("tensor", "dp"),
        P("tensor", "dp"),
        P("tensor", "dp"),
        P("tensor", "dp"),
        P("tensor", "dp"),
        P("dp", None, None),
    )
    return jax.shard_map(
        per_device,
        mesh=mesh,
        in_specs=placed,
        out_specs=(
            P("tensor", "dp"),
            P("tensor", "dp"),
            P("tensor", "dp"),
            P("tensor", "dp"),
            P("tensor", "dp"),
            P("tensor", "dp"),
            P("tensor", "dp"),
            P("tensor", "dp"),
            P("tensor", None),
            P("tensor", None),
        ),
        check_vma=False,
    )
```

```python
import functools

import jax
import jax.numpy as jnp
from jax import lax
from jax.experimental import pallas as pl
from jax.experimental.pallas import tpu as pltpu
from jax.sharding import PartitionSpec as P

D = 2432
F = 1216
ROWS = 1024


FIRST_CORRECTION = 0.9999734386011124
SECOND_CORRECTION = 0.0952078529183

OUTER = 4
HALF_LIMIT = 60000.0
TILE = 256
LANES = 128

NT = (((1,), (1,)), ((), ()))
NN = (((1,), (0,)), ((), ()))

SMEM = pl.BlockSpec(memory_space=pltpu.SMEM)
VMEM = pl.BlockSpec(memory_space=pltpu.VMEM)
ANY = pl.BlockSpec(memory_space=pl.ANY)


def adam_update(grad, squares, master, first, second):
    clip = jnp.minimum(1.0, jnp.sqrt(jnp.float32(D * F)) / jnp.sqrt(squares + 1e-06))
    clipped = grad * clip
    new_first = 0.9 * first + 0.1 * clipped
    new_second = 0.999 * second + 0.001 * clipped * clipped
    step_dir = new_first / FIRST_CORRECTION / (jnp.sqrt(new_second / SECOND_CORRECTION) + 1e-08)
    new_master = master * (1.0 - 0.01 * 0.01) - 0.01 * step_dir
    return (new_master, new_first, new_second)


def dot(a, b, dims):
    return lax.dot_general(a, b, dims, preferred_element_type=jnp.float32)


def identity(size):
    rows = lax.broadcasted_iota(jnp.int32, (size, size), 0)
    cols = lax.broadcasted_iota(jnp.int32, (size, size), 1)
    return jnp.where(rows == cols, 1.0, 0.0).astype(jnp.bfloat16)


def array(shape, dtype):
    return jax.ShapeDtypeStruct(shape, dtype)


def call(kernel, out_shape, *operands, mib=12, **kwargs):
    return pl.pallas_call(
        kernel,
        out_shape=out_shape,
        compiler_params=pltpu.CompilerParams(vmem_limit_bytes=mib * 1024 * 1024),
        cost_estimate=pl.CostEstimate(flops=0, bytes_accessed=0, transcendentals=0),
        **kwargs,
    )(*operands)


def solution(mesh):
    n_dp, n_tensor = mesh.shape["dp"], mesh.shape["tensor"]
    inner = n_dp // (2 * OUTER)
    width = D // n_dp

    def split(p):
        return (p >> inner.bit_length()) & (OUTER - 1), (p >> 1) & (inner - 1), p & 1

    def join(z, m, c):
        return (z * inner + m) * 2 + c

    def move_dp(value, where):
        perm = [(p, join(*where(*split(p)))) for p in range(n_dp)]
        return lax.ppermute(value, "dp", perm)

    def to_plane(value, k):
        return move_dp(value, lambda z, m, c: (z ^ k, m, c))

    def to_middle(value, k):
        return move_dp(value, lambda z, m, c: (z, (m + k) & (inner - 1), c))

    def to_core(value):
        return move_dp(value, lambda z, m, c: (z, m, 1 - c))

    def from_tensor(value, k):
        perm = [(s, (s - k) & (n_tensor - 1)) for s in range(n_tensor)]
        return lax.ppermute(value, "tensor", perm)

    def from_diagonal(value, k):
        perm = []
        for p in range(n_dp):
            z, m, c = split(p)
            for t in range(n_tensor):
                target = join(z, m, 1 - c) * n_tensor + ((t - k) & (n_tensor - 1))
                perm.append((p * n_tensor + t, target))
        return lax.ppermute(value, ("dp", "tensor"), perm)

    def my_place():
        return split(lax.axis_index("dp"))

    def relative(p):
        z, m, c = split(p)
        my_z, my_m, my_c = my_place()
        return z ^ my_z, (m - my_m) & (inner - 1), c ^ my_c

    def owner(k, i, other):
        z, m, c = my_place()
        return join(z ^ k, (m + i) & (inner - 1), c ^ other)

    def first_row(j, r):
        start = ((lax.axis_index("tensor") + j) & (n_tensor - 1)) * r
        return pl.multiple_of(start, LANES)

    def turn(cot, by_planes):
        r = cot.shape[0]
        step = min(r, TILE)
        count = 4 if by_planes else 2
        lead = (2, inner) if by_planes else (inner, OUTER)

        def kernel(cot_ref, *refs):
            out_refs, (top_ref, wide_ref) = refs[:count], refs[count:]
            eye = identity(TILE)
            for start in range(0, D, TILE):
                size = min(TILE, D - start)
                wide_ref[start : start + size, :] = dot(
                    eye[:size, :size], cot_ref[:, start : start + size], NT
                )
            top = jnp.max(jnp.abs(wide_ref[...]).reshape(D // 8, 8, step), axis=0)
            top = jnp.broadcast_to(jnp.max(top), (8, LANES))

            @pl.when(pl.program_id(0) == 0)
            def _():
                top_ref[...] = top

            @pl.when(pl.program_id(0) > 0)
            def _():
                top_ref[...] = jnp.maximum(top_ref[...], top)

            for p in range(n_dp):
                k, i, other = relative(p)
                block = wide_ref[p * width : (p + 1) * width, :].astype(jnp.bfloat16)
                which, at = other, (i, k)
                if by_planes:
                    even = 1 - (k & 1)
                    which, at = 2 * even + other, ((k >> 1) ^ even, i)
                for n in range(count):

                    @pl.when(which == n)
                    def _(n=n, at=at, block=block):
                        out_refs[n][at] = block

        *outs, top = call(
            kernel,
            [array((*lead, width, r), jnp.bfloat16)] * count + [array((8, LANES), jnp.float32)],
            cot,
            grid=(r // step,),
            in_specs=[pl.BlockSpec((step, D), lambda s: (s, 0))],
            out_specs=[
                pl.BlockSpec((*lead, width, step), lambda s: (*(0 for _ in lead), 0, s))
            ] * count
            + [pl.BlockSpec((8, LANES), lambda s: (0, 0))],
            scratch_shapes=[pltpu.VMEM((D, step), jnp.float32)],
        )
        return outs, top

    def prepare_fake(act, scales, r):
        f = act.shape[0]

        def kernel(scale_ref, act_ref, top_ref, *out_refs):
            most = jnp.max(jnp.abs(act_ref[...].astype(jnp.float32)))
            top_ref[...] = jnp.full((8, LANES), most * scale_ref[1])
            for j, out_ref in enumerate(out_refs):
                part = act_ref[:, pl.ds(first_row(j, r), r)].astype(jnp.float32)
                out_ref[0] = (part * scale_ref[1]).astype(jnp.bfloat16)

        return call(
            kernel,
            [array((8, LANES), jnp.float32)] + [array((1, f, r), jnp.bfloat16)] * n_tensor,
            scales, act,
            in_specs=[SMEM, VMEM], out_specs=[VMEM] * (1 + n_tensor),
        )

    def prepare_student(act, top_s, top_f, top_act_f, scales, r):
        f = act.shape[0]

        def kernel(scale_ref, act_ref, top_s_ref, top_f_ref, top_act_f_ref, top_ref, out_ref):
            most = jnp.max(jnp.abs(act_ref[...].astype(jnp.float32)))
            most = jnp.full((8, LANES), most * scale_ref[0])
            rows = lax.broadcasted_iota(jnp.int32, (8, LANES), 0)
            tops = jnp.where(rows == 0, top_s_ref[...], most)
            tops = jnp.where(rows == 2, top_f_ref[...], tops)
            top_ref[...] = jnp.where(rows == 3, top_act_f_ref[...], tops)
            for j in range(n_tensor):
                part = act_ref[:, pl.ds(first_row(j, r), r)].astype(jnp.float32)
                out_ref[j] = (part * scale_ref[0]).astype(jnp.bfloat16)

        return call(
            kernel,
            [array((8, LANES), jnp.float32), array((n_tensor, f, r), jnp.bfloat16)],
            scales, act, top_s, top_f, top_act_f,
            in_specs=[SMEM] + [VMEM] * 4, out_specs=[VMEM] * 2,
        )

    def multiply(pieces, scaled, places):
        lead, r, f = pieces[0].shape[:-1], pieces[0].shape[-1], scaled[0].shape[1]
        pieces = [piece.reshape(-1, r) for piece in pieces]
        rows = pieces[0].shape[0]
        step = D // (2 * OUTER)
        count = len(pieces)

        def kernel(*refs):
            piece_refs, scaled_refs, out_ref = refs[:count], refs[count:-1], refs[-1]
            for start in range(0, rows, step):
                part = slice(start, start + step)
                total = None
                for piece_ref, (n, j) in zip(piece_refs, places):
                    term = dot(piece_ref[part], scaled_refs[n][j], NT)
                    total = term if total is None else total + term
                out_ref[part] = total

        out = call(
            kernel, array((rows, f), jnp.float32), *pieces, *scaled,
            in_specs=[VMEM] * (count + len(scaled)), out_specs=VMEM,
        )
        return out.reshape(*lead, f)

    def norms(total_s, total_f):
        def kernel(s_ref, f_ref, out_ref):
            sums = [jnp.sum(ref[...] * ref[...]) for ref in (s_ref, f_ref)]
            rows = lax.broadcasted_iota(jnp.int32, (8, LANES), 0)
            out_ref[...] = jnp.where(rows == 0, *sums)

        return call(
            kernel, array((8, LANES), jnp.float32), total_s, total_f,
            in_specs=[VMEM] * 2, out_specs=VMEM,
        )

    def update(squares, totals, states):
        shape = totals[0].shape

        def kernel(squares_ref, *refs):
            total_refs, state_refs, (own_ref, *out_refs) = refs[:2], refs[2:8], refs[8:]
            for net in range(2):
                new = adam_update(
                    total_refs[net][...],
                    squares_ref[net : net + 1, :1],
                    *(ref[...] for ref in state_refs[3 * net : 3 * net + 3]),
                )
                own_ref[net] = new[0].astype(jnp.bfloat16)
                for ref, value in zip(out_refs[3 * net :], new):
                    ref[...] = value

        own, *new = call(
            kernel,
            [array((2, *shape), jnp.bfloat16)] + [array(shape, jnp.float32)] * 6,
            squares, *totals, *states,
            in_specs=[VMEM] * 9,
            out_specs=[VMEM] * 7,
        )
        return own, new

    def back_part(whole, weight, pieces, scales, net, j, low, size, r, count):
        f = weight.shape[0]
        turned = len(pieces) > 1

        def kernel(scale_ref, weight_ref, *refs):
            piece_refs = refs[: len(pieces)]
            if turned:
                out_ref, done_ref, sem, wide_ref = refs[-4:]
                for k in range(OUTER):
                    for other in range(2):
                        for i in range(inner):
                            even = 1 - (k & 1)
                            block = piece_refs[2 * even + other][(k >> 1) ^ even, i]
                            block = block.astype(jnp.float32)
                            wide_ref[owner(k, i, other)] = block
                flat = wide_ref[...].reshape(D, size).astype(jnp.bfloat16)
                product = dot(weight_ref[...], flat, NN)
            else:
                out_ref, done_ref, sem = refs[-3:]
                product = dot(weight_ref[...], piece_refs[0][...], NT)
            done_ref[...] = (product * scale_ref[net]).astype(jnp.bfloat16)
            start = pl.multiple_of(first_row(j, r) + low, LANES)
            copy = pltpu.make_async_copy(done_ref, out_ref.at[:, pl.ds(start, size)], sem)
            copy.start()
            copy.wait()

        scratch = [pltpu.VMEM((f, size), jnp.bfloat16), pltpu.SemaphoreType.DMA]
        if turned:
            scratch.append(pltpu.VMEM((n_dp, width, size), jnp.float32))
        operands = [scales, weight, *pieces]
        in_specs = [SMEM] + [VMEM] * (len(operands) - 1)
        aliases = {}
        if whole is not None:
            aliases = {len(operands): 0}
            operands.append(whole)
            in_specs.append(ANY)
        return call(
            kernel, array((f, count), jnp.bfloat16), *operands,
            in_specs=in_specs, out_specs=ANY, scratch_shapes=scratch,
            input_output_aliases=aliases, mib=20,
        )

    def spread(stacks):
        count, _, _, f = stacks[0].shape
        tiles = [
            (net, start, min(TILE, f - start)) for net in range(2) for start in range(0, f, TILE)
        ]

        def kernel(*refs):
            stack_refs, out_refs, (wide_ref, done_ref, sem) = refs[:4], refs[4:6], refs[6:]
            eye = identity(TILE)
            copies = []
            for step, (net, start, size) in enumerate(tiles):
                for n, ref in enumerate(stack_refs):
                    for at in range(count):
                        k, i = divmod((n & 1) * count + at, inner)
                        block = ref[at, net, :, start : start + size].astype(jnp.float32)
                        wide_ref[owner(k, i, n >> 1), :, :size] = block
                flat = wide_ref[:, :, :size].reshape(D, size).astype(jnp.bfloat16)
                slot = step & 1
                if step >= 2:
                    copies[step - 2].wait()
                done_ref[slot, :size, :] = dot(eye[:size, :size], flat, NT).astype(jnp.bfloat16)
                copy = pltpu.make_async_copy(
                    done_ref.at[slot, pl.ds(0, size)],
                    out_refs[net].at[pl.ds(start, size)],
                    sem.at[slot],
                )
                copy.start()
                copies.append(copy)
            for copy in copies[-2:]:
                copy.wait()

        return call(
            kernel, [array((f, D), jnp.bfloat16)] * 2, *stacks,
            in_specs=[VMEM] * 4, out_specs=[ANY] * 2,
            scratch_shapes=[
                pltpu.VMEM((n_dp, width, TILE), jnp.float32),
                pltpu.VMEM((2, TILE, D), jnp.bfloat16),
                pltpu.SemaphoreType.DMA((2,)),
            ],
            mib=20,
        )

    def per_device(
        cot_student, cot_fake, act_student, act_fake, weight_student, weight_fake,
        master_student, first_student, second_student, master_fake, first_fake, second_fake,
        timesteps,
    ):
        f, count = act_student.shape
        r = cot_student.shape[0]
        assert timesteps.shape[2] == 1 and count == ROWS

        token = []

        def step(work, *inputs):
            if token:
                *inputs, _ = lax.optimization_barrier((*inputs, token[0]))
            out = work(*inputs)
            token[:] = jax.tree.leaves(out)[:1]
            return out

        def reduced(combine, value, got):
            return step(lambda *values: functools.reduce(combine, values), value, *got)

        def hops(value, combine, *axes):
            for axis in axes:
                distance = 1
                while distance < mesh.shape[axis]:
                    perm = [(p, p ^ distance) for p in range(mesh.shape[axis])]
                    got = lax.ppermute(value, axis, perm)
                    yield
                    value = step(combine, value, got)
                    distance *= 2
            yield value

        scales = step(
            lambda steps: 1.0 / (0.1 + steps.astype(jnp.float32) / 1000.0), timesteps[0, :, 0]
        )
        top_act, scaled_own, *sent = step(lambda act: prepare_fake(act, scales, r), act_fake)
        acts = [from_tensor(value, -j) for j, value in enumerate(sent, 1)]
        scaled_fake = [[scaled_own, to_core(scaled_own)]]
        fake_blocks, top_fake = step(lambda cot: turn(cot, False), cot_fake)
        mate_blocks = to_core(fake_blocks[1])
        planes, top_student = step(lambda cot: turn(cot, True), cot_student)

        same, diagonal = [], []

        def send_planes(g, own, other):
            same.append([from_tensor(own, j) for j in range(1, n_tensor)])
            diagonal.append([from_diagonal(other, j) for j in range(1, n_tensor)])

        tops, scaled_student = step(
            lambda *values: prepare_student(*values, scales, r),
            act_student, top_student, top_fake, top_act,
        )
        tops = hops(tops, jnp.maximum, "dp")
        next(tops)
        send_planes(0, planes[0], planes[1])
        parts_fake = []

        def multiply_fake(j):
            parts_fake.append(
                step(
                    lambda a, b, c, d: multiply([a, b], [c, d], [(0, 0), (1, 0)]),
                    fake_blocks[0], mate_blocks, *scaled_fake[j],
                )
            )

        multiply_fake(0)
        next(tops)
        next(tops)
        next(tops)
        acts = step(lambda *values: values, *acts)
        scaled_fake += [[act, to_core(act)] for act in acts]
        while (tops_own := next(tops)) is None:
            pass

        def factor(tops, net):
            bound = jnp.maximum(tops[2 * net, 0] * tops[2 * net + 1, 0], 1e-30)
            bound = bound * (1.01 * count * n_dp / HALF_LIMIT)
            return bound, 1.0 / bound

        factors = {"own": step(lambda tops: factor(tops, 1), tops_own)}

        def shrink(value, net):
            return (value * factors[net][1]).astype(jnp.float16)

        def widen(value, net):
            return value.astype(jnp.float32) * factors[net][0]

        def add_widened(total, values, net):
            for value in values:
                total = total + widen(value, net)
            return total

        fake_own, fake_got = {}, {}

        def which(j):
            return 1 if j else "own"

        def fake_middle(j):
            def work(both):
                sent = [shrink(both[i], which(j)) for i in range(1, inner)]
                return sent, both[0]

            sent, fake_own[j] = step(work, parts_fake[j])
            fake_got[j] = [to_middle(value, i) for i, value in enumerate(sent, 1)]

        def fake_near(j):
            def work(own, *got):
                own = add_widened(own, got, which(j))
                return shrink(own[1::2], which(j)), own[0::2]

            sent, fake_own[j] = step(work, fake_own[j], *fake_got[j])
            fake_got[j] = [to_plane(sent, 1)]

        def fake_far(j):
            def work(own, *got):
                own = add_widened(own, got, which(j))
                return shrink(own[1], which(j)), own[0]

            sent, fake_own[j] = step(work, fake_own[j], *fake_got[j])
            fake_got[j] = [to_plane(sent, 2)]

        def fake_total(j):
            return step(
                lambda own, *got: add_widened(own, got, which(j)), fake_own[j], *fake_got[j]
            )

        fake_middle(0)
        for j in range(1, n_tensor):
            multiply_fake(j)
        mate_student = to_core(scaled_student)
        mate_planes = [to_core(planes[1]), to_core(planes[3])]
        tops = hops(tops_own, jnp.maximum, "tensor")
        next(tops)
        mate_student, *mate_planes = step(lambda *values: values, mate_student, *mate_planes)

        def back(whole, net, pieces, j, low, size):
            weight = (weight_student, weight_fake)[net]
            has = [] if whole is None else [whole]

            def work(weight, *values):
                return back_part(
                    values[-1] if has else None, weight, values[: len(pieces)], scales,
                    net, j, low, size, r, count,
                )

            return step(work, weight, *pieces, *has)

        def multiply_student(g):
            pieces, places = [planes[2 * g], mate_planes[g]], [(0, 0), (1, 0)]
            for j in range(1, n_tensor):
                pieces += [same[g][j - 1], diagonal[g][j - 1]]
                places += [(0, j), (1, j)]
            return step(
                lambda *values: multiply(values[:-2], values[-2:], places),
                *pieces, scaled_student, mate_student,
            )

        back_student = back(None, 0, [cot_student], 0, 0, r)
        send_planes(1, *step(lambda a, b: (a, b), planes[2], planes[3]))
        back_fake = back(None, 1, [cot_fake], 0, 0, r)
        while (tops_all := next(tops)) is None:
            pass
        factors[0], factors[1] = step(lambda tops: (factor(tops, 0), factor(tops, 1)), tops_all)
        for j in range(1, n_tensor):
            fake_middle(j)
        both = multiply_student(0)

        def first_middle(both):
            return [shrink(both[:, i], 0) for i in range(1, inner)], both[:, 0]

        sent, own = step(first_middle, both)
        got = [to_middle(value, i) for i, value in enumerate(sent, 1)]
        for j in range(n_tensor):
            fake_near(j)

        def first_planes(own, *got):
            return shrink(add_widened(own, got, 0), 0)

        near = to_plane(step(first_planes, own, *got), 1)
        for j in range(n_tensor):
            fake_far(j)
        both = multiply_student(1)

        def second_middle(both):
            sent = [[shrink(both[n, i], 0) for i in range(1, inner)] for n in range(2)]
            return sent, both[0, 0], both[1, 0]

        sent, own_far, own = step(second_middle, both)
        got_far, got = (
            [to_middle(value, i) for i, value in enumerate(values, 1)] for values in sent
        )
        fake_mine = fake_total(0)
        fake_others = [fake_total(j) for j in range(1, n_tensor)]
        others_got = [from_tensor(value, j) for j, value in enumerate(fake_others, 1)]

        def far_plane(own, near, *got):
            return shrink(add_widened(own, (near[1], *got), 0), 0)

        far = to_plane(step(far_plane, own_far, near, *got_far), 2)
        total_student = step(
            lambda own, near, *got: add_widened(own, (near[0], *got), 0), own, near, *got
        )
        total_fake = reduced(jnp.add, fake_mine, others_got)
        total_student = step(
            lambda own, got: add_widened(own, (got,), 0), total_student, far
        )
        squares = step(norms, total_student, total_fake)
        squares = reduced(
            jnp.add, squares, [from_tensor(squares, j) for j in range(1, n_tensor)]
        )

        rows = step(lambda cot: cot, cot_fake)
        raw = [from_tensor(rows, j) for j in range(1, n_tensor)]

        got = [to_plane(squares, k) for k in range(1, OUTER)]
        squares = reduced(jnp.add, squares, got)
        got = [
            move_dp(squares, lambda z, m, c, i=i, o=o: (z, (m + i) & (inner - 1), c ^ o))
            for i in range(inner)
            for o in range(2)
            if i or o
        ]
        squares = reduced(jnp.add, squares, got)
        states = (
            master_student, first_student, second_student, master_fake, first_fake, second_fake,
        )
        own, updated = step(
            lambda squares, *values: update(squares, values[:2], values[2:]),
            squares, total_student, total_fake, *(state.T for state in states),
        )

        mine = {}

        def spread_middle(k, value):
            mine[k] = [value] + [to_middle(value, -i) for i in range(1, inner)]

        spread_middle(0, own)
        planes_got = {k: to_plane(own, k) for k in (1, 3, 2)}
        spread_middle(1, step(lambda value: value, planes_got[1]))
        spread_middle(3, step(lambda value: value, planes_got[3]))
        early = [value for k in (0, 1, 3) for value in mine[k]]
        early = step(lambda *values: values, *early)
        mine = {k: list(early[n * inner : (n + 1) * inner]) for n, k in enumerate((0, 1, 3))}
        spread_middle(2, step(lambda value: value, planes_got[2]))
        first_half = step(lambda *values: jnp.stack(values), *mine[0], *mine[1])
        theirs = [to_core(first_half)]
        hidden = step(lambda *values: values, *[value for group in diagonal for value in group])
        mate_others = [to_core(value) for value in hidden]
        mate_others = [mate_others[: n_tensor - 1], mate_others[n_tensor - 1 :]]
        for j in range(1, n_tensor):
            pieces = [
                piece for g in range(2) for piece in (same[g][j - 1], mate_others[g][j - 1])
            ]
            back_student = back(back_student, 0, pieces, j, 0, r)
        for j in range(1, n_tensor):
            back_fake = back(back_fake, 1, [raw[j - 1]], j, 0, r)
        second_half = step(lambda *values: jnp.stack(values), *mine[2], *mine[3])
        theirs.append(to_core(second_half))
        stacks = [first_half, second_half, *theirs]
        params = step(lambda *values: spread(values), *stacks)

        new_states = [value.T for value in updated]
        return (back_student, back_fake, *new_states, *params)

    placed = (
        P(("dp", "tensor"), None),
        P(("dp", "tensor"), None),
        P("tensor", "dp"),
        P("tensor", "dp"),
        P("tensor", None),
        P("tensor", None),
        P("tensor", "dp"),
        P("tensor", "dp"),
        P("tensor", "dp"),
        P("tensor", "dp"),
        P("tensor", "dp"),
        P("tensor", "dp"),
        P("dp", None, None),
    )
    return jax.shard_map(
        per_device,
        mesh=mesh,
        in_specs=placed,
        out_specs=(
            P("tensor", "dp"),
            P("tensor", "dp"),
            P("tensor", "dp"),
            P("tensor", "dp"),
            P("tensor", "dp"),
            P("tensor", "dp"),
            P("tensor", "dp"),
            P("tensor", "dp"),
            P("tensor", None),
            P("tensor", None),
        ),
        check_vma=False,
    )
```

```python
import functools

import jax
import jax.numpy as jnp
from jax import lax
from jax.experimental import pallas as pl
from jax.experimental.pallas import tpu as pltpu
from jax.sharding import PartitionSpec as P

D = 2432
F = 1216
ROWS = 1024


FIRST_CORRECTION = 0.9999734386011124
SECOND_CORRECTION = 0.0952078529183

OUTER = 4
HALF_LIMIT = 60000.0
TILE = 256
LANES = 128

NT = (((1,), (1,)), ((), ()))
NN = (((1,), (0,)), ((), ()))

SMEM = pl.BlockSpec(memory_space=pltpu.SMEM)
VMEM = pl.BlockSpec(memory_space=pltpu.VMEM)
ANY = pl.BlockSpec(memory_space=pl.ANY)


def adam_update(grad, squares, master, first, second):
    clip = jnp.minimum(1.0, jnp.sqrt(jnp.float32(D * F)) / jnp.sqrt(squares + 1e-06))
    clipped = grad * clip
    new_first = 0.9 * first + 0.1 * clipped
    new_second = 0.999 * second + 0.001 * clipped * clipped
    step_dir = new_first / FIRST_CORRECTION / (jnp.sqrt(new_second / SECOND_CORRECTION) + 1e-08)
    new_master = master * (1.0 - 0.01 * 0.01) - 0.01 * step_dir
    return (new_master, new_first, new_second)


def dot(a, b, dims):
    return lax.dot_general(a, b, dims, preferred_element_type=jnp.float32)


def identity(size):
    rows = lax.broadcasted_iota(jnp.int32, (size, size), 0)
    cols = lax.broadcasted_iota(jnp.int32, (size, size), 1)
    return jnp.where(rows == cols, 1.0, 0.0).astype(jnp.bfloat16)


def array(shape, dtype):
    return jax.ShapeDtypeStruct(shape, dtype)


def call(kernel, out_shape, *operands, mib=12, **kwargs):
    return pl.pallas_call(
        kernel,
        out_shape=out_shape,
        compiler_params=pltpu.CompilerParams(vmem_limit_bytes=mib * 1024 * 1024),
        cost_estimate=pl.CostEstimate(flops=0, bytes_accessed=0, transcendentals=0),
        **kwargs,
    )(*operands)


def solution(mesh):
    n_dp, n_tensor = mesh.shape["dp"], mesh.shape["tensor"]
    inner = n_dp // (2 * OUTER)
    width = D // n_dp

    def split(p):
        return (p >> inner.bit_length()) & (OUTER - 1), (p >> 1) & (inner - 1), p & 1

    def join(z, m, c):
        return (z * inner + m) * 2 + c

    def move_dp(value, where):
        perm = [(p, join(*where(*split(p)))) for p in range(n_dp)]
        return lax.ppermute(value, "dp", perm)

    def to_plane(value, k):
        return move_dp(value, lambda z, m, c: (z ^ k, m, c))

    def to_middle(value, k):
        return move_dp(value, lambda z, m, c: (z, (m + k) & (inner - 1), c))

    def to_core(value):
        return move_dp(value, lambda z, m, c: (z, m, 1 - c))

    def from_tensor(value, k):
        perm = [(s, (s - k) & (n_tensor - 1)) for s in range(n_tensor)]
        return lax.ppermute(value, "tensor", perm)

    def from_diagonal(value, k):
        perm = []
        for p in range(n_dp):
            z, m, c = split(p)
            for t in range(n_tensor):
                target = join(z, m, 1 - c) * n_tensor + ((t - k) & (n_tensor - 1))
                perm.append((p * n_tensor + t, target))
        return lax.ppermute(value, ("dp", "tensor"), perm)

    def my_place():
        return split(lax.axis_index("dp"))

    def relative(p):
        z, m, c = split(p)
        my_z, my_m, my_c = my_place()
        return z ^ my_z, (m - my_m) & (inner - 1), c ^ my_c

    def owner(k, i, other):
        z, m, c = my_place()
        return join(z ^ k, (m + i) & (inner - 1), c ^ other)

    def first_row(j, r):
        start = ((lax.axis_index("tensor") + j) & (n_tensor - 1)) * r
        return pl.multiple_of(start, LANES)

    def turn(cot, by_planes):
        r = cot.shape[0]
        step = min(r, TILE)
        count = 4 if by_planes else 2
        lead = (2, inner) if by_planes else (inner, OUTER)

        def kernel(cot_ref, *refs):
            out_refs, (top_ref, wide_ref) = refs[:count], refs[count:]
            eye = identity(TILE)
            for start in range(0, D, TILE):
                size = min(TILE, D - start)
                wide_ref[start : start + size, :] = dot(
                    eye[:size, :size], cot_ref[:, start : start + size], NT
                )
            top = jnp.max(jnp.abs(wide_ref[...]).reshape(D // 8, 8, step), axis=0)
            top = jnp.broadcast_to(jnp.max(top), (8, LANES))

            @pl.when(pl.program_id(0) == 0)
            def _():
                top_ref[...] = top

            @pl.when(pl.program_id(0) > 0)
            def _():
                top_ref[...] = jnp.maximum(top_ref[...], top)

            for p in range(n_dp):
                k, i, other = relative(p)
                block = wide_ref[p * width : (p + 1) * width, :].astype(jnp.bfloat16)
                which, at = other, (i, k)
                if by_planes:
                    even = 1 - (k & 1)
                    which, at = 2 * even + other, ((k >> 1) ^ even, i)
                for n in range(count):

                    @pl.when(which == n)
                    def _(n=n, at=at, block=block):
                        out_refs[n][at] = block

        *outs, top = call(
            kernel,
            [array((*lead, width, r), jnp.bfloat16)] * count + [array((8, LANES), jnp.float32)],
            cot,
            grid=(r // step,),
            in_specs=[pl.BlockSpec((step, D), lambda s: (s, 0))],
            out_specs=[
                pl.BlockSpec((*lead, width, step), lambda s: (*(0 for _ in lead), 0, s))
            ] * count
            + [pl.BlockSpec((8, LANES), lambda s: (0, 0))],
            scratch_shapes=[pltpu.VMEM((D, step), jnp.float32)],
        )
        return outs, top

    def prepare_fake(act, scales, r):
        f = act.shape[0]

        def kernel(scale_ref, act_ref, top_ref, *out_refs):
            most = jnp.max(jnp.abs(act_ref[...].astype(jnp.float32)))
            top_ref[...] = jnp.full((8, LANES), most * scale_ref[1])
            for j, out_ref in enumerate(out_refs):
                part = act_ref[:, pl.ds(first_row(j, r), r)].astype(jnp.float32)
                out_ref[0] = (part * scale_ref[1]).astype(jnp.bfloat16)

        return call(
            kernel,
            [array((8, LANES), jnp.float32)] + [array((1, f, r), jnp.bfloat16)] * n_tensor,
            scales, act,
            in_specs=[SMEM, VMEM], out_specs=[VMEM] * (1 + n_tensor),
        )

    def prepare_student(act, top_s, top_f, top_act_f, scales, r):
        f = act.shape[0]

        def kernel(scale_ref, act_ref, top_s_ref, top_f_ref, top_act_f_ref, top_ref, out_ref):
            most = jnp.max(jnp.abs(act_ref[...].astype(jnp.float32)))
            most = jnp.full((8, LANES), most * scale_ref[0])
            rows = lax.broadcasted_iota(jnp.int32, (8, LANES), 0)
            tops = jnp.where(rows == 0, top_s_ref[...], most)
            tops = jnp.where(rows == 2, top_f_ref[...], tops)
            top_ref[...] = jnp.where(rows == 3, top_act_f_ref[...], tops)
            for j in range(n_tensor):
                part = act_ref[:, pl.ds(first_row(j, r), r)].astype(jnp.float32)
                out_ref[j] = (part * scale_ref[0]).astype(jnp.bfloat16)

        return call(
            kernel,
            [array((8, LANES), jnp.float32), array((n_tensor, f, r), jnp.bfloat16)],
            scales, act, top_s, top_f, top_act_f,
            in_specs=[SMEM] + [VMEM] * 4, out_specs=[VMEM] * 2,
        )

    def multiply(pieces, scaled, places):
        lead, r, f = pieces[0].shape[:-1], pieces[0].shape[-1], scaled[0].shape[1]
        pieces = [piece.reshape(-1, r) for piece in pieces]
        rows = pieces[0].shape[0]
        step = D // (2 * OUTER)
        count = len(pieces)

        def kernel(*refs):
            piece_refs, scaled_refs, out_ref = refs[:count], refs[count:-1], refs[-1]
            for start in range(0, rows, step):
                part = slice(start, start + step)
                total = None
                for piece_ref, (n, j) in zip(piece_refs, places):
                    term = dot(piece_ref[part], scaled_refs[n][j], NT)
                    total = term if total is None else total + term
                out_ref[part] = total

        out = call(
            kernel, array((rows, f), jnp.float32), *pieces, *scaled,
            in_specs=[VMEM] * (count + len(scaled)), out_specs=VMEM,
        )
        return out.reshape(*lead, f)

    def norms(total_s, total_f):
        def kernel(s_ref, f_ref, out_ref):
            sums = [jnp.sum(ref[...] * ref[...]) for ref in (s_ref, f_ref)]
            rows = lax.broadcasted_iota(jnp.int32, (8, LANES), 0)
            out_ref[...] = jnp.where(rows == 0, *sums)

        return call(
            kernel, array((8, LANES), jnp.float32), total_s, total_f,
            in_specs=[VMEM] * 2, out_specs=VMEM,
        )

    def update(squares, totals, states):
        shape = totals[0].shape

        def kernel(squares_ref, *refs):
            total_refs, state_refs, (own_ref, *out_refs) = refs[:2], refs[2:8], refs[8:]
            for net in range(2):
                new = adam_update(
                    total_refs[net][...],
                    squares_ref[net : net + 1, :1],
                    *(ref[...] for ref in state_refs[3 * net : 3 * net + 3]),
                )
                own_ref[net] = new[0].astype(jnp.bfloat16)
                for ref, value in zip(out_refs[3 * net :], new):
                    ref[...] = value

        own, *new = call(
            kernel,
            [array((2, *shape), jnp.bfloat16)] + [array(shape, jnp.float32)] * 6,
            squares, *totals, *states,
            in_specs=[VMEM] * 9,
            out_specs=[VMEM] * 7,
        )
        return own, new

    def back_part(whole, weight, pieces, scales, net, j, low, size, r, count):
        f = weight.shape[0]
        turned = len(pieces) > 1

        def kernel(scale_ref, weight_ref, *refs):
            piece_refs = refs[: len(pieces)]
            if turned:
                out_ref, done_ref, sem, wide_ref = refs[-4:]
                for k in range(OUTER):
                    for other in range(2):
                        for i in range(inner):
                            even = 1 - (k & 1)
                            block = piece_refs[2 * even + other][(k >> 1) ^ even, i]
                            block = block.astype(jnp.float32)
                            wide_ref[owner(k, i, other)] = block
                flat = wide_ref[...].reshape(D, size).astype(jnp.bfloat16)
                product = dot(weight_ref[...], flat, NN)
            else:
                out_ref, done_ref, sem = refs[-3:]
                product = dot(weight_ref[...], piece_refs[0][...], NT)
            done_ref[...] = (product * scale_ref[net]).astype(jnp.bfloat16)
            start = pl.multiple_of(first_row(j, r) + low, LANES)
            copy = pltpu.make_async_copy(done_ref, out_ref.at[:, pl.ds(start, size)], sem)
            copy.start()
            copy.wait()

        scratch = [pltpu.VMEM((f, size), jnp.bfloat16), pltpu.SemaphoreType.DMA]
        if turned:
            scratch.append(pltpu.VMEM((n_dp, width, size), jnp.float32))
        operands = [scales, weight, *pieces]
        in_specs = [SMEM] + [VMEM] * (len(operands) - 1)
        aliases = {}
        if whole is not None:
            aliases = {len(operands): 0}
            operands.append(whole)
            in_specs.append(ANY)
        return call(
            kernel, array((f, count), jnp.bfloat16), *operands,
            in_specs=in_specs, out_specs=ANY, scratch_shapes=scratch,
            input_output_aliases=aliases, mib=20,
        )

    def spread(blocks, *arrays):
        f = arrays[0].shape[-1]
        tiles = [
            (net, start, min(TILE, f - start)) for net in range(2) for start in range(0, f, TILE)
        ]

        def kernel(*refs):
            array_refs, refs = refs[: len(arrays)], refs[len(arrays) :]
            out_refs, (wide_ref, done_ref, sem) = refs[:2], refs[2:]
            eye = identity(TILE)
            copies = []
            for step, (net, start, size) in enumerate(tiles):
                for (k, i, other), (n, at) in blocks.items():
                    ref = array_refs[n] if at is None else array_refs[n].at[at]
                    block = ref[net, :, start : start + size].astype(jnp.float32)
                    wide_ref[owner(k, i, other), :, :size] = block
                flat = wide_ref[:, :, :size].reshape(D, size).astype(jnp.bfloat16)
                slot = step & 1
                if step >= 2:
                    copies[step - 2].wait()
                done_ref[slot, :size, :] = dot(eye[:size, :size], flat, NT).astype(jnp.bfloat16)
                copy = pltpu.make_async_copy(
                    done_ref.at[slot, pl.ds(0, size)],
                    out_refs[net].at[pl.ds(start, size)],
                    sem.at[slot],
                )
                copy.start()
                copies.append(copy)
            for copy in copies[-2:]:
                copy.wait()

        return call(
            kernel, [array((f, D), jnp.bfloat16)] * 2, *arrays,
            in_specs=[VMEM] * len(arrays), out_specs=[ANY] * 2,
            scratch_shapes=[
                pltpu.VMEM((n_dp, width, TILE), jnp.float32),
                pltpu.VMEM((2, TILE, D), jnp.bfloat16),
                pltpu.SemaphoreType.DMA((2,)),
            ],
            mib=20,
        )

    def per_device(
        cot_student, cot_fake, act_student, act_fake, weight_student, weight_fake,
        master_student, first_student, second_student, master_fake, first_fake, second_fake,
        timesteps,
    ):
        f, count = act_student.shape
        r = cot_student.shape[0]
        assert timesteps.shape[2] == 1 and count == ROWS

        token = []

        def step(work, *inputs):
            if token:
                *inputs, _ = lax.optimization_barrier((*inputs, token[0]))
            out = work(*inputs)
            token[:] = jax.tree.leaves(out)[:1]
            return out

        def reduced(combine, value, got):
            return step(lambda *values: functools.reduce(combine, values), value, *got)

        def hops(value, combine, *axes):
            for axis in axes:
                distance = 1
                while distance < mesh.shape[axis]:
                    perm = [(p, p ^ distance) for p in range(mesh.shape[axis])]
                    got = lax.ppermute(value, axis, perm)
                    yield
                    value = step(combine, value, got)
                    distance *= 2
            yield value

        scales = step(
            lambda steps: 1.0 / (0.1 + steps.astype(jnp.float32) / 1000.0), timesteps[0, :, 0]
        )
        top_act, scaled_own, *sent = step(lambda act: prepare_fake(act, scales, r), act_fake)
        acts = [from_tensor(value, -j) for j, value in enumerate(sent, 1)]
        scaled_fake = [[scaled_own, to_core(scaled_own)]]
        fake_blocks, top_fake = step(lambda cot: turn(cot, False), cot_fake)
        mate_blocks = to_core(fake_blocks[1])
        planes, top_student = step(lambda cot: turn(cot, True), cot_student)

        same, diagonal = [], []

        def send_planes(g, own, other):
            same.append([from_tensor(own, j) for j in range(1, n_tensor)])
            diagonal.append([from_diagonal(other, j) for j in range(1, n_tensor)])

        tops, scaled_student = step(
            lambda *values: prepare_student(*values, scales, r),
            act_student, top_student, top_fake, top_act,
        )
        tops = hops(tops, jnp.maximum, "dp")
        next(tops)
        send_planes(0, planes[0], planes[1])
        parts_fake = []

        def multiply_fake(j):
            parts_fake.append(
                step(
                    lambda a, b, c, d: multiply([a, b], [c, d], [(0, 0), (1, 0)]),
                    fake_blocks[0], mate_blocks, *scaled_fake[j],
                )
            )

        multiply_fake(0)
        next(tops)
        next(tops)
        next(tops)
        acts = step(lambda *values: values, *acts)
        scaled_fake += [[act, to_core(act)] for act in acts]
        while (tops_own := next(tops)) is None:
            pass

        def factor(tops, net):
            bound = jnp.maximum(tops[2 * net, 0] * tops[2 * net + 1, 0], 1e-30)
            bound = bound * (1.01 * count * n_dp / HALF_LIMIT)
            return bound, 1.0 / bound

        factors = {"own": step(lambda tops: factor(tops, 1), tops_own)}

        def shrink(value, net):
            return (value * factors[net][1]).astype(jnp.float16)

        def widen(value, net):
            return value.astype(jnp.float32) * factors[net][0]

        def add_widened(total, values, net):
            for value in values:
                total = total + widen(value, net)
            return total

        fake_own, fake_got = {}, {}

        def which(j):
            return 1 if j else "own"

        def fake_middle(j):
            def work(both):
                sent = [shrink(both[i], which(j)) for i in range(1, inner)]
                return sent, both[0]

            sent, fake_own[j] = step(work, parts_fake[j])
            fake_got[j] = [to_middle(value, i) for i, value in enumerate(sent, 1)]

        def fake_near(j):
            def work(own, *got):
                own = add_widened(own, got, which(j))
                return shrink(own[1::2], which(j)), own[0::2]

            sent, fake_own[j] = step(work, fake_own[j], *fake_got[j])
            fake_got[j] = [to_plane(sent, 1)]

        def fake_far(j):
            def work(own, *got):
                own = add_widened(own, got, which(j))
                return shrink(own[1], which(j)), own[0]

            sent, fake_own[j] = step(work, fake_own[j], *fake_got[j])
            fake_got[j] = [to_plane(sent, 2)]

        def fake_total(j):
            return step(
                lambda own, *got: add_widened(own, got, which(j)), fake_own[j], *fake_got[j]
            )

        fake_middle(0)
        for j in range(1, n_tensor):
            multiply_fake(j)
        mate_student = to_core(scaled_student)
        mate_planes = [to_core(planes[1]), to_core(planes[3])]
        tops = hops(tops_own, jnp.maximum, "tensor")
        next(tops)
        mate_student, *mate_planes = step(lambda *values: values, mate_student, *mate_planes)

        def back(whole, net, pieces, j, low, size):
            weight = (weight_student, weight_fake)[net]
            has = [] if whole is None else [whole]

            def work(weight, *values):
                return back_part(
                    values[-1] if has else None, weight, values[: len(pieces)], scales,
                    net, j, low, size, r, count,
                )

            return step(work, weight, *pieces, *has)

        def multiply_student(g):
            pieces, places = [planes[2 * g], mate_planes[g]], [(0, 0), (1, 0)]
            for j in range(1, n_tensor):
                pieces += [same[g][j - 1], diagonal[g][j - 1]]
                places += [(0, j), (1, j)]
            return step(
                lambda *values: multiply(values[:-2], values[-2:], places),
                *pieces, scaled_student, mate_student,
            )

        back_student = back(None, 0, [cot_student], 0, 0, r)
        send_planes(1, *step(lambda a, b: (a, b), planes[2], planes[3]))
        back_fake = back(None, 1, [cot_fake], 0, 0, r)
        while (tops_all := next(tops)) is None:
            pass
        factors[0], factors[1] = step(lambda tops: (factor(tops, 0), factor(tops, 1)), tops_all)
        for j in range(1, n_tensor):
            fake_middle(j)
        both = multiply_student(0)

        def first_middle(both):
            return [shrink(both[:, i], 0) for i in range(1, inner)], both[:, 0]

        sent, own = step(first_middle, both)
        got = [to_middle(value, i) for i, value in enumerate(sent, 1)]
        for j in range(n_tensor):
            fake_near(j)

        def first_planes(own, *got):
            return shrink(add_widened(own, got, 0), 0)

        near = to_plane(step(first_planes, own, *got), 1)
        fake_far(0)
        both = multiply_student(1)

        def second_middle(both):
            sent = [[shrink(both[n, i], 0) for i in range(1, inner)] for n in range(2)]
            return sent, both[0, 0], both[1, 0]

        sent, own_far, own = step(second_middle, both)
        got_far, got = (
            [to_middle(value, i) for i, value in enumerate(values, 1)] for values in sent
        )
        for j in range(1, n_tensor):
            fake_far(j)
        fake_mine = fake_total(0)
        fake_others = [fake_total(j) for j in range(1, n_tensor)]
        others_got = [from_tensor(value, j) for j, value in enumerate(fake_others, 1)]

        def far_plane(own, near, *got):
            return shrink(add_widened(own, (near[1], *got), 0), 0)

        far = to_plane(step(far_plane, own_far, near, *got_far), 2)
        total_student = step(
            lambda own, near, *got: add_widened(own, (near[0], *got), 0), own, near, *got
        )
        total_fake = reduced(jnp.add, fake_mine, others_got)
        total_student = step(
            lambda own, got: add_widened(own, (got,), 0), total_student, far
        )
        squares = step(norms, total_student, total_fake)
        squares = reduced(
            jnp.add, squares, [from_tensor(squares, j) for j in range(1, n_tensor)]
        )

        rows = step(lambda cot: cot, cot_fake)
        raw = [from_tensor(rows, j) for j in range(1, n_tensor)]

        got = [to_plane(squares, k) for k in range(1, OUTER)]
        squares = reduced(jnp.add, squares, got)
        got = [
            move_dp(squares, lambda z, m, c, i=i, o=o: (z, (m + i) & (inner - 1), c ^ o))
            for i in range(inner)
            for o in range(2)
            if i or o
        ]
        squares = reduced(jnp.add, squares, got)
        states = (
            master_student, first_student, second_student, master_fake, first_fake, second_fake,
        )
        own, updated = step(
            lambda squares, *values: update(squares, values[:2], values[2:]),
            squares, total_student, total_fake, *(state.T for state in states),
        )

        mine = {}

        def spread_middle(k, value):
            mine[k] = [value] + [to_middle(value, -i) for i in range(1, inner)]

        spread_middle(0, own)
        far_got, near_got = to_plane(own, 2), to_plane(own, 1)
        spread_middle(1, step(lambda value: value, near_got))
        value = step(lambda value: value, far_got)
        spread_middle(2, value)
        passed_on = to_plane(value, 1)
        arrays = [step(lambda *values: jnp.stack(values), *mine[0], *mine[1])]
        arrays.append(to_core(arrays[0]))
        spread_middle(3, step(lambda value: value, passed_on))
        arrays.append(step(lambda *values: jnp.stack(values), *mine[2]))
        arrays.append(to_core(arrays[2]))
        mine[3] = step(lambda *values: values, *mine[3])
        raw = step(lambda *values: values, *raw)
        hidden = step(lambda *values: values, *[value for group in diagonal for value in group])
        mate_others = [to_core(value) for value in hidden]
        mate_others = [mate_others[: n_tensor - 1], mate_others[n_tensor - 1 :]]
        for j in range(1, n_tensor):
            pieces = [
                piece for g in range(2) for piece in (same[g][j - 1], mate_others[g][j - 1])
            ]
            back_student = back(back_student, 0, pieces, j, 0, r)
        for j in range(1, n_tensor):
            back_fake = back(back_fake, 1, [raw[j - 1]], j, 0, r)
        blocks = {}
        for other in range(2):
            for i in range(inner):
                for k in range(2):
                    blocks[k, i, other] = other, k * inner + i
                blocks[2, i, other] = 2 + other, i
        for i, value in enumerate(mine[3]):
            blocks[3, i, 0], blocks[3, i, 1] = (len(arrays), None), (len(arrays) + 1, None)
            arrays += [value, to_core(value)]
        params = step(lambda *values: spread(blocks, *values), *arrays)

        new_states = [value.T for value in updated]
        return (back_student, back_fake, *new_states, *params)

    placed = (
        P(("dp", "tensor"), None),
        P(("dp", "tensor"), None),
        P("tensor", "dp"),
        P("tensor", "dp"),
        P("tensor", None),
        P("tensor", None),
        P("tensor", "dp"),
        P("tensor", "dp"),
        P("tensor", "dp"),
        P("tensor", "dp"),
        P("tensor", "dp"),
        P("tensor", "dp"),
        P("dp", None, None),
    )
    return jax.shard_map(
        per_device,
        mesh=mesh,
        in_specs=placed,
        out_specs=(
            P("tensor", "dp"),
            P("tensor", "dp"),
            P("tensor", "dp"),
            P("tensor", "dp"),
            P("tensor", "dp"),
            P("tensor", "dp"),
            P("tensor", "dp"),
            P("tensor", "dp"),
            P("tensor", None),
            P("tensor", None),
        ),
        check_vma=False,
    )
```

```python
import functools

import jax
import jax.numpy as jnp
from jax import lax
from jax.experimental import pallas as pl
from jax.experimental.pallas import tpu as pltpu
from jax.sharding import PartitionSpec as P

D = 2432
F = 1216
ROWS = 1024


FIRST_CORRECTION = 0.9999734386011124
SECOND_CORRECTION = 0.0952078529183

OUTER = 4
HALF_LIMIT = 60000.0
TILE = 256
LANES = 128

NT = (((1,), (1,)), ((), ()))
NN = (((1,), (0,)), ((), ()))

SMEM = pl.BlockSpec(memory_space=pltpu.SMEM)
VMEM = pl.BlockSpec(memory_space=pltpu.VMEM)
ANY = pl.BlockSpec(memory_space=pl.ANY)


def adam_update(grad, squares, master, first, second):
    clip = jnp.minimum(1.0, jnp.sqrt(jnp.float32(D * F)) / jnp.sqrt(squares + 1e-06))
    clipped = grad * clip
    new_first = 0.9 * first + 0.1 * clipped
    new_second = 0.999 * second + 0.001 * clipped * clipped
    step_dir = new_first / FIRST_CORRECTION / (jnp.sqrt(new_second / SECOND_CORRECTION) + 1e-08)
    new_master = master * (1.0 - 0.01 * 0.01) - 0.01 * step_dir
    return (new_master, new_first, new_second)


def dot(a, b, dims):
    return lax.dot_general(a, b, dims, preferred_element_type=jnp.float32)


def identity(size):
    rows = lax.broadcasted_iota(jnp.int32, (size, size), 0)
    cols = lax.broadcasted_iota(jnp.int32, (size, size), 1)
    return jnp.where(rows == cols, 1.0, 0.0).astype(jnp.bfloat16)


def array(shape, dtype):
    return jax.ShapeDtypeStruct(shape, dtype)


def call(kernel, out_shape, *operands, mib=12, **kwargs):
    return pl.pallas_call(
        kernel,
        out_shape=out_shape,
        compiler_params=pltpu.CompilerParams(vmem_limit_bytes=mib * 1024 * 1024),
        cost_estimate=pl.CostEstimate(flops=0, bytes_accessed=0, transcendentals=0),
        **kwargs,
    )(*operands)


def solution(mesh):
    n_dp, n_tensor = mesh.shape["dp"], mesh.shape["tensor"]
    inner = n_dp // (2 * OUTER)
    width = D // n_dp

    def split(p):
        return (p >> inner.bit_length()) & (OUTER - 1), (p >> 1) & (inner - 1), p & 1

    def join(z, m, c):
        return (z * inner + m) * 2 + c

    def move_dp(value, where):
        perm = [(p, join(*where(*split(p)))) for p in range(n_dp)]
        return lax.ppermute(value, "dp", perm)

    def to_plane(value, k):
        return move_dp(value, lambda z, m, c: (z ^ k, m, c))

    def to_middle(value, k):
        return move_dp(value, lambda z, m, c: (z, (m + k) & (inner - 1), c))

    def to_core(value):
        return move_dp(value, lambda z, m, c: (z, m, 1 - c))

    def from_tensor(value, k):
        perm = [(s, (s - k) & (n_tensor - 1)) for s in range(n_tensor)]
        return lax.ppermute(value, "tensor", perm)

    def from_diagonal(value, k):
        perm = []
        for p in range(n_dp):
            z, m, c = split(p)
            for t in range(n_tensor):
                target = join(z, m, 1 - c) * n_tensor + ((t - k) & (n_tensor - 1))
                perm.append((p * n_tensor + t, target))
        return lax.ppermute(value, ("dp", "tensor"), perm)

    def my_place():
        return split(lax.axis_index("dp"))

    def relative(p):
        z, m, c = split(p)
        my_z, my_m, my_c = my_place()
        return z ^ my_z, (m - my_m) & (inner - 1), c ^ my_c

    def owner(k, i, other):
        z, m, c = my_place()
        return join(z ^ k, (m + i) & (inner - 1), c ^ other)

    def first_row(j, r):
        start = ((lax.axis_index("tensor") + j) & (n_tensor - 1)) * r
        return pl.multiple_of(start, LANES)

    def turn(cot, by_planes):
        r = cot.shape[0]
        step = min(r, TILE)
        count = 4 if by_planes else 2
        lead = (2, inner) if by_planes else (inner, OUTER)

        def kernel(cot_ref, *refs):
            out_refs, (top_ref, wide_ref) = refs[:count], refs[count:]
            eye = identity(TILE)
            for start in range(0, D, TILE):
                size = min(TILE, D - start)
                wide_ref[start : start + size, :] = dot(
                    eye[:size, :size], cot_ref[:, start : start + size], NT
                )
            top = jnp.max(jnp.abs(wide_ref[...]).reshape(D // 8, 8, step), axis=0)
            top = jnp.broadcast_to(jnp.max(top), (8, LANES))

            @pl.when(pl.program_id(0) == 0)
            def _():
                top_ref[...] = top

            @pl.when(pl.program_id(0) > 0)
            def _():
                top_ref[...] = jnp.maximum(top_ref[...], top)

            for p in range(n_dp):
                k, i, other = relative(p)
                block = wide_ref[p * width : (p + 1) * width, :].astype(jnp.bfloat16)
                which, at = other, (i, k)
                if by_planes:
                    even = 1 - (k & 1)
                    which, at = 2 * even + other, ((k >> 1) ^ even, i)
                for n in range(count):

                    @pl.when(which == n)
                    def _(n=n, at=at, block=block):
                        out_refs[n][at] = block

        *outs, top = call(
            kernel,
            [array((*lead, width, r), jnp.bfloat16)] * count + [array((8, LANES), jnp.float32)],
            cot,
            grid=(r // step,),
            in_specs=[pl.BlockSpec((step, D), lambda s: (s, 0))],
            out_specs=[
                pl.BlockSpec((*lead, width, step), lambda s: (*(0 for _ in lead), 0, s))
            ] * count
            + [pl.BlockSpec((8, LANES), lambda s: (0, 0))],
            scratch_shapes=[pltpu.VMEM((D, step), jnp.float32)],
        )
        return outs, top

    def prepare_fake(act, scales, r):
        f = act.shape[0]

        def kernel(scale_ref, act_ref, top_ref, *out_refs):
            most = jnp.max(jnp.abs(act_ref[...].astype(jnp.float32)))
            top_ref[...] = jnp.full((8, LANES), most * scale_ref[1])
            for j, out_ref in enumerate(out_refs):
                part = act_ref[:, pl.ds(first_row(j, r), r)].astype(jnp.float32)
                out_ref[0] = (part * scale_ref[1]).astype(jnp.bfloat16)

        return call(
            kernel,
            [array((8, LANES), jnp.float32)] + [array((1, f, r), jnp.bfloat16)] * n_tensor,
            scales, act,
            in_specs=[SMEM, VMEM], out_specs=[VMEM] * (1 + n_tensor),
        )

    def prepare_student(act, top_s, top_f, top_act_f, scales, r):
        f = act.shape[0]

        def kernel(scale_ref, act_ref, top_s_ref, top_f_ref, top_act_f_ref, top_ref, out_ref):
            most = jnp.max(jnp.abs(act_ref[...].astype(jnp.float32)))
            most = jnp.full((8, LANES), most * scale_ref[0])
            rows = lax.broadcasted_iota(jnp.int32, (8, LANES), 0)
            tops = jnp.where(rows == 0, top_s_ref[...], most)
            tops = jnp.where(rows == 2, top_f_ref[...], tops)
            top_ref[...] = jnp.where(rows == 3, top_act_f_ref[...], tops)
            for j in range(n_tensor):
                part = act_ref[:, pl.ds(first_row(j, r), r)].astype(jnp.float32)
                out_ref[j] = (part * scale_ref[0]).astype(jnp.bfloat16)

        return call(
            kernel,
            [array((8, LANES), jnp.float32), array((n_tensor, f, r), jnp.bfloat16)],
            scales, act, top_s, top_f, top_act_f,
            in_specs=[SMEM] + [VMEM] * 4, out_specs=[VMEM] * 2,
        )

    def multiply(pieces, scaled, places):
        lead, r, f = pieces[0].shape[:-1], pieces[0].shape[-1], scaled[0].shape[1]
        pieces = [piece.reshape(-1, r) for piece in pieces]
        rows = pieces[0].shape[0]
        step = D // (2 * OUTER)
        count = len(pieces)

        def kernel(*refs):
            piece_refs, scaled_refs, out_ref = refs[:count], refs[count:-1], refs[-1]
            for start in range(0, rows, step):
                part = slice(start, start + step)
                total = None
                for piece_ref, (n, j) in zip(piece_refs, places):
                    term = dot(piece_ref[part], scaled_refs[n][j], NT)
                    total = term if total is None else total + term
                out_ref[part] = total

        out = call(
            kernel, array((rows, f), jnp.float32), *pieces, *scaled,
            in_specs=[VMEM] * (count + len(scaled)), out_specs=VMEM,
        )
        return out.reshape(*lead, f)

    def norms(total_s, total_f):
        def kernel(s_ref, f_ref, out_ref):
            sums = [jnp.sum(ref[...] * ref[...]) for ref in (s_ref, f_ref)]
            rows = lax.broadcasted_iota(jnp.int32, (8, LANES), 0)
            out_ref[...] = jnp.where(rows == 0, *sums)

        return call(
            kernel, array((8, LANES), jnp.float32), total_s, total_f,
            in_specs=[VMEM] * 2, out_specs=VMEM,
        )

    def update(squares, totals, states):
        shape = totals[0].shape

        def kernel(squares_ref, *refs):
            total_refs, state_refs, (own_ref, *out_refs) = refs[:2], refs[2:8], refs[8:]
            for net in range(2):
                new = adam_update(
                    total_refs[net][...],
                    squares_ref[net : net + 1, :1],
                    *(ref[...] for ref in state_refs[3 * net : 3 * net + 3]),
                )
                own_ref[net] = new[0].astype(jnp.bfloat16)
                for ref, value in zip(out_refs[3 * net :], new):
                    ref[...] = value

        own, *new = call(
            kernel,
            [array((2, *shape), jnp.bfloat16)] + [array(shape, jnp.float32)] * 6,
            squares, *totals, *states,
            in_specs=[VMEM] * 9,
            out_specs=[VMEM] * 7,
        )
        return own, new

    def back_part(whole, weight, pieces, scales, net, j, low, size, r, count):
        f = weight.shape[0]
        turned = len(pieces) > 1

        def kernel(scale_ref, weight_ref, *refs):
            piece_refs = refs[: len(pieces)]
            if turned:
                out_ref, done_ref, sem, wide_ref = refs[-4:]
                for k in range(OUTER):
                    for other in range(2):
                        for i in range(inner):
                            even = 1 - (k & 1)
                            block = piece_refs[2 * even + other][(k >> 1) ^ even, i]
                            block = block.astype(jnp.float32)
                            wide_ref[owner(k, i, other)] = block
                flat = wide_ref[...].reshape(D, size).astype(jnp.bfloat16)
                product = dot(weight_ref[...], flat, NN)
            else:
                out_ref, done_ref, sem = refs[-3:]
                product = dot(weight_ref[...], piece_refs[0][...], NT)
            done_ref[...] = (product * scale_ref[net]).astype(jnp.bfloat16)
            start = pl.multiple_of(first_row(j, r) + low, LANES)
            copy = pltpu.make_async_copy(done_ref, out_ref.at[:, pl.ds(start, size)], sem)
            copy.start()
            copy.wait()

        scratch = [pltpu.VMEM((f, size), jnp.bfloat16), pltpu.SemaphoreType.DMA]
        if turned:
            scratch.append(pltpu.VMEM((n_dp, width, size), jnp.float32))
        operands = [scales, weight, *pieces]
        in_specs = [SMEM] + [VMEM] * (len(operands) - 1)
        aliases = {}
        if whole is not None:
            aliases = {len(operands): 0}
            operands.append(whole)
            in_specs.append(ANY)
        return call(
            kernel, array((f, count), jnp.bfloat16), *operands,
            in_specs=in_specs, out_specs=ANY, scratch_shapes=scratch,
            input_output_aliases=aliases, mib=20,
        )

    def spread(blocks, *arrays):
        f = arrays[0].shape[-1]
        tiles = [
            (net, start, min(TILE, f - start)) for net in range(2) for start in range(0, f, TILE)
        ]

        def kernel(*refs):
            array_refs, refs = refs[: len(arrays)], refs[len(arrays) :]
            out_refs, (wide_ref, done_ref, sem) = refs[:2], refs[2:]
            eye = identity(TILE)
            copies = []
            for step, (net, start, size) in enumerate(tiles):
                for (k, i, other), (n, at) in blocks.items():
                    ref = array_refs[n] if at is None else array_refs[n].at[at]
                    block = ref[net, :, start : start + size].astype(jnp.float32)
                    wide_ref[owner(k, i, other), :, :size] = block
                flat = wide_ref[:, :, :size].reshape(D, size).astype(jnp.bfloat16)
                slot = step & 1
                if step >= 2:
                    copies[step - 2].wait()
                done_ref[slot, :size, :] = dot(eye[:size, :size], flat, NT).astype(jnp.bfloat16)
                copy = pltpu.make_async_copy(
                    done_ref.at[slot, pl.ds(0, size)],
                    out_refs[net].at[pl.ds(start, size)],
                    sem.at[slot],
                )
                copy.start()
                copies.append(copy)
            for copy in copies[-2:]:
                copy.wait()

        return call(
            kernel, [array((f, D), jnp.bfloat16)] * 2, *arrays,
            in_specs=[VMEM] * len(arrays), out_specs=[ANY] * 2,
            scratch_shapes=[
                pltpu.VMEM((n_dp, width, TILE), jnp.float32),
                pltpu.VMEM((2, TILE, D), jnp.bfloat16),
                pltpu.SemaphoreType.DMA((2,)),
            ],
            mib=20,
        )

    def per_device(
        cot_student, cot_fake, act_student, act_fake, weight_student, weight_fake,
        master_student, first_student, second_student, master_fake, first_fake, second_fake,
        timesteps,
    ):
        f, count = act_student.shape
        r = cot_student.shape[0]
        assert timesteps.shape[2] == 1 and count == ROWS

        token = []

        def step(work, *inputs):
            if token:
                *inputs, _ = lax.optimization_barrier((*inputs, token[0]))
            out = work(*inputs)
            token[:] = jax.tree.leaves(out)[:1]
            return out

        def reduced(combine, value, got):
            return step(lambda *values: functools.reduce(combine, values), value, *got)

        def hops(value, combine, *axes):
            for axis in axes:
                distance = 1
                while distance < mesh.shape[axis]:
                    perm = [(p, p ^ distance) for p in range(mesh.shape[axis])]
                    got = lax.ppermute(value, axis, perm)
                    yield
                    value = step(combine, value, got)
                    distance *= 2
            yield value

        scales = step(
            lambda steps: 1.0 / (0.1 + steps.astype(jnp.float32) / 1000.0), timesteps[0, :, 0]
        )
        top_act, scaled_own, *sent = step(lambda act: prepare_fake(act, scales, r), act_fake)
        acts = [from_tensor(value, -j) for j, value in enumerate(sent, 1)]
        scaled_fake = [[scaled_own, to_core(scaled_own)]]
        fake_blocks, top_fake = step(lambda cot: turn(cot, False), cot_fake)
        mate_blocks = to_core(fake_blocks[1])
        planes, top_student = step(lambda cot: turn(cot, True), cot_student)

        same, diagonal = [], []

        def send_planes(g, own, other):
            same.append([from_tensor(own, j) for j in range(1, n_tensor)])
            diagonal.append([from_diagonal(other, j) for j in range(1, n_tensor)])

        tops, scaled_student = step(
            lambda *values: prepare_student(*values, scales, r),
            act_student, top_student, top_fake, top_act,
        )
        tops = hops(tops, jnp.maximum, "dp")
        next(tops)
        send_planes(0, planes[0], planes[1])
        parts_fake = []

        def multiply_fake(j):
            parts_fake.append(
                step(
                    lambda a, b, c, d: multiply([a, b], [c, d], [(0, 0), (1, 0)]),
                    fake_blocks[0], mate_blocks, *scaled_fake[j],
                )
            )

        multiply_fake(0)
        next(tops)
        next(tops)
        next(tops)
        acts = step(lambda *values: values, *acts)
        scaled_fake += [[act, to_core(act)] for act in acts]
        while (tops_own := next(tops)) is None:
            pass

        def factor(tops, net):
            bound = jnp.maximum(tops[2 * net, 0] * tops[2 * net + 1, 0], 1e-30)
            bound = bound * (1.01 * count * n_dp / HALF_LIMIT)
            return bound, 1.0 / bound

        factors = {"own": step(lambda tops: factor(tops, 1), tops_own)}

        def shrink(value, net):
            return (value * factors[net][1]).astype(jnp.float16)

        def widen(value, net):
            return value.astype(jnp.float32) * factors[net][0]

        def add_widened(total, values, net):
            for value in values:
                total = total + widen(value, net)
            return total

        fake_own, fake_got = {}, {}

        def which(j):
            return 1 if j else "own"

        def fake_middle(j):
            def work(both):
                sent = [shrink(both[i], which(j)) for i in range(1, inner)]
                return sent, both[0]

            sent, fake_own[j] = step(work, parts_fake[j])
            fake_got[j] = [to_middle(value, i) for i, value in enumerate(sent, 1)]

        def fake_near(j):
            def work(own, *got):
                own = add_widened(own, got, which(j))
                return shrink(own[1::2], which(j)), own[0::2]

            sent, fake_own[j] = step(work, fake_own[j], *fake_got[j])
            fake_got[j] = [to_plane(sent, 1)]

        def fake_far(j):
            def work(own, *got):
                own = add_widened(own, got, which(j))
                return shrink(own[1], which(j)), own[0]

            sent, fake_own[j] = step(work, fake_own[j], *fake_got[j])
            fake_got[j] = [to_plane(sent, 2)]

        def fake_total(j):
            return step(
                lambda own, *got: add_widened(own, got, which(j)), fake_own[j], *fake_got[j]
            )

        fake_middle(0)
        for j in range(1, n_tensor):
            multiply_fake(j)
        mate_student = to_core(scaled_student)
        mate_planes = [to_core(planes[1]), to_core(planes[3])]
        tops = hops(tops_own, jnp.maximum, "tensor")
        next(tops)
        mate_student, *mate_planes = step(lambda *values: values, mate_student, *mate_planes)

        def back(whole, net, pieces, j, low, size):
            weight = (weight_student, weight_fake)[net]
            has = [] if whole is None else [whole]

            def work(weight, *values):
                return back_part(
                    values[-1] if has else None, weight, values[: len(pieces)], scales,
                    net, j, low, size, r, count,
                )

            return step(work, weight, *pieces, *has)

        def multiply_student(g):
            pieces, places = [planes[2 * g], mate_planes[g]], [(0, 0), (1, 0)]
            for j in range(1, n_tensor):
                pieces += [same[g][j - 1], diagonal[g][j - 1]]
                places += [(0, j), (1, j)]
            return step(
                lambda *values: multiply(values[:-2], values[-2:], places),
                *pieces, scaled_student, mate_student,
            )

        back_student = back(None, 0, [cot_student], 0, 0, r)
        send_planes(1, *step(lambda a, b: (a, b), planes[2], planes[3]))
        back_fake = back(None, 1, [cot_fake], 0, 0, r)
        while (tops_all := next(tops)) is None:
            pass
        factors[0], factors[1] = step(lambda tops: (factor(tops, 0), factor(tops, 1)), tops_all)
        for j in range(1, n_tensor):
            fake_middle(j)
        both = multiply_student(0)

        def first_middle(both):
            return [shrink(both[:, i], 0) for i in range(1, inner)], both[:, 0]

        sent, own = step(first_middle, both)
        got = [to_middle(value, i) for i, value in enumerate(sent, 1)]
        for j in range(n_tensor):
            fake_near(j)

        def first_planes(own, *got):
            return shrink(add_widened(own, got, 0), 0)

        near = to_plane(step(first_planes, own, *got), 1)
        fake_far(0)
        both = multiply_student(1)

        def second_middle(both):
            sent = [[shrink(both[n, i], 0) for i in range(1, inner)] for n in range(2)]
            return sent, both[0, 0], both[1, 0]

        sent, own_far, own = step(second_middle, both)
        got_far, got = (
            [to_middle(value, i) for i, value in enumerate(values, 1)] for values in sent
        )
        for j in range(1, n_tensor):
            fake_far(j)
        fake_mine = fake_total(0)
        fake_others = [fake_total(j) for j in range(1, n_tensor)]
        others_got = [from_tensor(value, j) for j, value in enumerate(fake_others, 1)]

        def far_plane(own, near, *got):
            return shrink(add_widened(own, (near[1], *got), 0), 0)

        far = to_plane(step(far_plane, own_far, near, *got_far), 2)
        total_student = step(
            lambda own, near, *got: add_widened(own, (near[0], *got), 0), own, near, *got
        )
        total_fake = reduced(jnp.add, fake_mine, others_got)
        total_student = step(
            lambda own, got: add_widened(own, (got,), 0), total_student, far
        )
        squares = step(norms, total_student, total_fake)
        squares = reduced(
            jnp.add, squares, [from_tensor(squares, j) for j in range(1, n_tensor)]
        )

        rows = step(lambda cot: cot, cot_fake)
        raw = [from_tensor(rows, j) for j in range(1, n_tensor)]

        got = [to_plane(squares, k) for k in range(1, OUTER)]
        squares = reduced(jnp.add, squares, got)
        got = [
            move_dp(squares, lambda z, m, c, i=i, o=o: (z, (m + i) & (inner - 1), c ^ o))
            for i in range(inner)
            for o in range(2)
            if i or o
        ]
        squares = reduced(jnp.add, squares, got)
        states = (
            master_student, first_student, second_student, master_fake, first_fake, second_fake,
        )
        own, updated = step(
            lambda squares, *values: update(squares, values[:2], values[2:]),
            squares, total_student, total_fake, *(state.T for state in states),
        )

        mine = {}

        def spread_middle(k, value):
            mine[k] = [value] + [to_middle(value, -i) for i in range(1, inner)]

        spread_middle(0, own)
        far_got, near_got = to_plane(own, 2), to_plane(own, 1)
        spread_middle(1, step(lambda value: value, near_got))
        value = step(lambda value: value, far_got)
        spread_middle(2, value)
        passed_on = to_plane(value, 1)
        arrays = [step(lambda *values: jnp.stack(values), *mine[0], *mine[1])]
        arrays.append(to_core(arrays[0]))
        spread_middle(3, step(lambda value: value, passed_on))
        arrays.append(step(lambda *values: jnp.stack(values), *mine[2]))
        arrays.append(to_core(arrays[2]))
        hidden = step(lambda *values: values, *[value for group in diagonal for value in group])
        mate_others = [to_core(value) for value in hidden]
        mate_others = [mate_others[: n_tensor - 1], mate_others[n_tensor - 1 :]]
        for j in range(1, n_tensor):
            pieces = [
                piece for g in range(2) for piece in (same[g][j - 1], mate_others[g][j - 1])
            ]
            back_student = back(back_student, 0, pieces, j, 0, r)
        for j in range(1, n_tensor):
            back_fake = back(back_fake, 1, [raw[j - 1]], j, 0, r)
        mine[3] = step(lambda *values: values, *mine[3])
        blocks = {}
        for other in range(2):
            for i in range(inner):
                for k in range(2):
                    blocks[k, i, other] = other, k * inner + i
                blocks[2, i, other] = 2 + other, i
        for i, value in enumerate(mine[3]):
            blocks[3, i, 0], blocks[3, i, 1] = (len(arrays), None), (len(arrays) + 1, None)
            arrays += [value, to_core(value)]
        params = step(lambda *values: spread(blocks, *values), *arrays)

        new_states = [value.T for value in updated]
        return (back_student, back_fake, *new_states, *params)

    placed = (
        P(("dp", "tensor"), None),
        P(("dp", "tensor"), None),
        P("tensor", "dp"),
        P("tensor", "dp"),
        P("tensor", None),
        P("tensor", None),
        P("tensor", "dp"),
        P("tensor", "dp"),
        P("tensor", "dp"),
        P("tensor", "dp"),
        P("tensor", "dp"),
        P("tensor", "dp"),
        P("dp", None, None),
    )
    return jax.shard_map(
        per_device,
        mesh=mesh,
        in_specs=placed,
        out_specs=(
            P("tensor", "dp"),
            P("tensor", "dp"),
            P("tensor", "dp"),
            P("tensor", "dp"),
            P("tensor", "dp"),
            P("tensor", "dp"),
            P("tensor", "dp"),
            P("tensor", "dp"),
            P("tensor", None),
            P("tensor", None),
        ),
        check_vma=False,
    )
```

```python
import functools

import jax
import jax.numpy as jnp
from jax import lax
from jax.experimental import pallas as pl
from jax.experimental.pallas import tpu as pltpu
from jax.sharding import PartitionSpec as P

D = 2432
F = 1216
ROWS = 1024


FIRST_CORRECTION = 0.9999734386011124
SECOND_CORRECTION = 0.0952078529183

OUTER = 4
HALF_LIMIT = 60000.0
TILE = 256
LANES = 128

NT = (((1,), (1,)), ((), ()))
NN = (((1,), (0,)), ((), ()))

SMEM = pl.BlockSpec(memory_space=pltpu.SMEM)
VMEM = pl.BlockSpec(memory_space=pltpu.VMEM)
ANY = pl.BlockSpec(memory_space=pl.ANY)


def adam_update(grad, squares, master, first, second):
    clip = jnp.minimum(1.0, jnp.sqrt(jnp.float32(D * F)) / jnp.sqrt(squares + 1e-06))
    clipped = grad * clip
    new_first = 0.9 * first + 0.1 * clipped
    new_second = 0.999 * second + 0.001 * clipped * clipped
    step_dir = new_first / FIRST_CORRECTION / (jnp.sqrt(new_second / SECOND_CORRECTION) + 1e-08)
    new_master = master * (1.0 - 0.01 * 0.01) - 0.01 * step_dir
    return (new_master, new_first, new_second)


def dot(a, b, dims):
    return lax.dot_general(a, b, dims, preferred_element_type=jnp.float32)


def identity(size):
    rows = lax.broadcasted_iota(jnp.int32, (size, size), 0)
    cols = lax.broadcasted_iota(jnp.int32, (size, size), 1)
    return jnp.where(rows == cols, 1.0, 0.0).astype(jnp.bfloat16)


def array(shape, dtype):
    return jax.ShapeDtypeStruct(shape, dtype)


def call(kernel, out_shape, *operands, mib=12, **kwargs):
    return pl.pallas_call(
        kernel,
        out_shape=out_shape,
        compiler_params=pltpu.CompilerParams(vmem_limit_bytes=mib * 1024 * 1024),
        cost_estimate=pl.CostEstimate(flops=0, bytes_accessed=0, transcendentals=0),
        **kwargs,
    )(*operands)


def solution(mesh):
    n_dp, n_tensor = mesh.shape["dp"], mesh.shape["tensor"]
    inner = n_dp // (2 * OUTER)
    width = D // n_dp

    def split(p):
        return (p >> inner.bit_length()) & (OUTER - 1), (p >> 1) & (inner - 1), p & 1

    def join(z, m, c):
        return (z * inner + m) * 2 + c

    def move_dp(value, where):
        perm = [(p, join(*where(*split(p)))) for p in range(n_dp)]
        return lax.ppermute(value, "dp", perm)

    def to_plane(value, k):
        return move_dp(value, lambda z, m, c: (z ^ k, m, c))

    def to_middle(value, k):
        return move_dp(value, lambda z, m, c: (z, (m + k) & (inner - 1), c))

    def to_core(value):
        return move_dp(value, lambda z, m, c: (z, m, 1 - c))

    def from_tensor(value, k):
        perm = [(s, (s - k) & (n_tensor - 1)) for s in range(n_tensor)]
        return lax.ppermute(value, "tensor", perm)

    def from_diagonal(value, k):
        perm = []
        for p in range(n_dp):
            z, m, c = split(p)
            for t in range(n_tensor):
                target = join(z, m, 1 - c) * n_tensor + ((t - k) & (n_tensor - 1))
                perm.append((p * n_tensor + t, target))
        return lax.ppermute(value, ("dp", "tensor"), perm)

    def my_place():
        return split(lax.axis_index("dp"))

    def relative(p):
        z, m, c = split(p)
        my_z, my_m, my_c = my_place()
        return z ^ my_z, (m - my_m) & (inner - 1), c ^ my_c

    def owner(k, i, other):
        z, m, c = my_place()
        return join(z ^ k, (m + i) & (inner - 1), c ^ other)

    def first_row(j, r):
        start = ((lax.axis_index("tensor") + j) & (n_tensor - 1)) * r
        return pl.multiple_of(start, LANES)

    def turn(cot, by_planes):
        r = cot.shape[0]
        step = min(r, TILE)
        count = 4 if by_planes else 2
        lead = (2, inner) if by_planes else (inner, OUTER)

        def kernel(cot_ref, *refs):
            out_refs, (top_ref, wide_ref) = refs[:count], refs[count:]
            eye = identity(TILE)
            for start in range(0, D, TILE):
                size = min(TILE, D - start)
                wide_ref[start : start + size, :] = dot(
                    eye[:size, :size], cot_ref[:, start : start + size], NT
                )
            top = jnp.max(jnp.abs(wide_ref[...]).reshape(D // 8, 8, step), axis=0)
            top = jnp.broadcast_to(jnp.max(top), (8, LANES))

            @pl.when(pl.program_id(0) == 0)
            def _():
                top_ref[...] = top

            @pl.when(pl.program_id(0) > 0)
            def _():
                top_ref[...] = jnp.maximum(top_ref[...], top)

            for p in range(n_dp):
                k, i, other = relative(p)
                block = wide_ref[p * width : (p + 1) * width, :].astype(jnp.bfloat16)
                which, at = other, (i, k)
                if by_planes:
                    even = 1 - (k & 1)
                    which, at = 2 * even + other, ((k >> 1) ^ even, i)
                for n in range(count):

                    @pl.when(which == n)
                    def _(n=n, at=at, block=block):
                        out_refs[n][at] = block

        *outs, top = call(
            kernel,
            [array((*lead, width, r), jnp.bfloat16)] * count + [array((8, LANES), jnp.float32)],
            cot,
            grid=(r // step,),
            in_specs=[pl.BlockSpec((step, D), lambda s: (s, 0))],
            out_specs=[
                pl.BlockSpec((*lead, width, step), lambda s: (*(0 for _ in lead), 0, s))
            ] * count
            + [pl.BlockSpec((8, LANES), lambda s: (0, 0))],
            scratch_shapes=[pltpu.VMEM((D, step), jnp.float32)],
        )
        return outs, top

    def prepare_fake(act, scales, r):
        f = act.shape[0]

        def kernel(scale_ref, act_ref, top_ref, *out_refs):
            most = jnp.max(jnp.abs(act_ref[...].astype(jnp.float32)))
            top_ref[...] = jnp.full((8, LANES), most * scale_ref[1])
            for j, out_ref in enumerate(out_refs):
                part = act_ref[:, pl.ds(first_row(j, r), r)].astype(jnp.float32)
                out_ref[0] = (part * scale_ref[1]).astype(jnp.bfloat16)

        return call(
            kernel,
            [array((8, LANES), jnp.float32)] + [array((1, f, r), jnp.bfloat16)] * n_tensor,
            scales, act,
            in_specs=[SMEM, VMEM], out_specs=[VMEM] * (1 + n_tensor),
        )

    def prepare_student(act, top_s, top_f, top_act_f, scales, r):
        f = act.shape[0]

        def kernel(scale_ref, act_ref, top_s_ref, top_f_ref, top_act_f_ref, top_ref, out_ref):
            most = jnp.max(jnp.abs(act_ref[...].astype(jnp.float32)))
            most = jnp.full((8, LANES), most * scale_ref[0])
            rows = lax.broadcasted_iota(jnp.int32, (8, LANES), 0)
            tops = jnp.where(rows == 0, top_s_ref[...], most)
            tops = jnp.where(rows == 2, top_f_ref[...], tops)
            top_ref[...] = jnp.where(rows == 3, top_act_f_ref[...], tops)
            for j in range(n_tensor):
                part = act_ref[:, pl.ds(first_row(j, r), r)].astype(jnp.float32)
                out_ref[j] = (part * scale_ref[0]).astype(jnp.bfloat16)

        return call(
            kernel,
            [array((8, LANES), jnp.float32), array((n_tensor, f, r), jnp.bfloat16)],
            scales, act, top_s, top_f, top_act_f,
            in_specs=[SMEM] + [VMEM] * 4, out_specs=[VMEM] * 2,
        )

    def multiply(pieces, scaled, places):
        lead, r, f = pieces[0].shape[:-1], pieces[0].shape[-1], scaled[0].shape[1]
        pieces = [piece.reshape(-1, r) for piece in pieces]
        rows = pieces[0].shape[0]
        step = D // (2 * OUTER)
        count = len(pieces)

        def kernel(*refs):
            piece_refs, scaled_refs, out_ref = refs[:count], refs[count:-1], refs[-1]
            for start in range(0, rows, step):
                part = slice(start, start + step)
                total = None
                for piece_ref, (n, j) in zip(piece_refs, places):
                    term = dot(piece_ref[part], scaled_refs[n][j], NT)
                    total = term if total is None else total + term
                out_ref[part] = total

        out = call(
            kernel, array((rows, f), jnp.float32), *pieces, *scaled,
            in_specs=[VMEM] * (count + len(scaled)), out_specs=VMEM,
        )
        return out.reshape(*lead, f)

    def norms(total_s, total_f):
        def kernel(s_ref, f_ref, out_ref):
            sums = [jnp.sum(ref[...] * ref[...]) for ref in (s_ref, f_ref)]
            rows = lax.broadcasted_iota(jnp.int32, (8, LANES), 0)
            out_ref[...] = jnp.where(rows == 0, *sums)

        return call(
            kernel, array((8, LANES), jnp.float32), total_s, total_f,
            in_specs=[VMEM] * 2, out_specs=VMEM,
        )

    def update(squares, totals, states):
        shape = totals[0].shape

        def kernel(squares_ref, *refs):
            total_refs, state_refs, (own_ref, *out_refs) = refs[:2], refs[2:8], refs[8:]
            for net in range(2):
                new = adam_update(
                    total_refs[net][...],
                    squares_ref[net : net + 1, :1],
                    *(ref[...] for ref in state_refs[3 * net : 3 * net + 3]),
                )
                own_ref[net] = new[0].astype(jnp.bfloat16)
                for ref, value in zip(out_refs[3 * net :], new):
                    ref[...] = value

        own, *new = call(
            kernel,
            [array((2, *shape), jnp.bfloat16)] + [array(shape, jnp.float32)] * 6,
            squares, *totals, *states,
            in_specs=[VMEM] * 9,
            out_specs=[VMEM] * 7,
        )
        return own, new

    def back_part(whole, weight, pieces, scales, net, j, low, size, r, count):
        f = weight.shape[0]
        turned = len(pieces) > 1

        def kernel(scale_ref, weight_ref, *refs):
            piece_refs = refs[: len(pieces)]
            if turned:
                out_ref, done_ref, sem, wide_ref = refs[-4:]
                for k in range(OUTER):
                    for other in range(2):
                        for i in range(inner):
                            even = 1 - (k & 1)
                            block = piece_refs[2 * even + other][(k >> 1) ^ even, i]
                            block = block.astype(jnp.float32)
                            wide_ref[owner(k, i, other)] = block
                flat = wide_ref[...].reshape(D, size).astype(jnp.bfloat16)
                product = dot(weight_ref[...], flat, NN)
            else:
                out_ref, done_ref, sem = refs[-3:]
                product = dot(weight_ref[...], piece_refs[0][...], NT)
            done_ref[...] = (product * scale_ref[net]).astype(jnp.bfloat16)
            start = pl.multiple_of(first_row(j, r) + low, LANES)
            copy = pltpu.make_async_copy(done_ref, out_ref.at[:, pl.ds(start, size)], sem)
            copy.start()
            copy.wait()

        scratch = [pltpu.VMEM((f, size), jnp.bfloat16), pltpu.SemaphoreType.DMA]
        if turned:
            scratch.append(pltpu.VMEM((n_dp, width, size), jnp.float32))
        operands = [scales, weight, *pieces]
        in_specs = [SMEM] + [VMEM] * (len(operands) - 1)
        aliases = {}
        if whole is not None:
            aliases = {len(operands): 0}
            operands.append(whole)
            in_specs.append(ANY)
        return call(
            kernel, array((f, count), jnp.bfloat16), *operands,
            in_specs=in_specs, out_specs=ANY, scratch_shapes=scratch,
            input_output_aliases=aliases, mib=20,
        )

    def spread(blocks, *arrays):
        f = arrays[0].shape[-1]
        tiles = [
            (net, start, min(TILE, f - start)) for net in range(2) for start in range(0, f, TILE)
        ]

        def kernel(*refs):
            array_refs, refs = refs[: len(arrays)], refs[len(arrays) :]
            out_refs, (wide_ref, done_ref, sem) = refs[:2], refs[2:]
            eye = identity(TILE)
            copies = []
            for step, (net, start, size) in enumerate(tiles):
                for (k, i, other), (n, at) in blocks.items():
                    ref = array_refs[n] if at is None else array_refs[n].at[at]
                    block = ref[net, :, start : start + size].astype(jnp.float32)
                    wide_ref[owner(k, i, other), :, :size] = block
                flat = wide_ref[:, :, :size].reshape(D, size).astype(jnp.bfloat16)
                slot = step & 1
                if step >= 2:
                    copies[step - 2].wait()
                done_ref[slot, :size, :] = dot(eye[:size, :size], flat, NT).astype(jnp.bfloat16)
                copy = pltpu.make_async_copy(
                    done_ref.at[slot, pl.ds(0, size)],
                    out_refs[net].at[pl.ds(start, size)],
                    sem.at[slot],
                )
                copy.start()
                copies.append(copy)
            for copy in copies[-2:]:
                copy.wait()

        return call(
            kernel, [array((f, D), jnp.bfloat16)] * 2, *arrays,
            in_specs=[VMEM] * len(arrays), out_specs=[ANY] * 2,
            scratch_shapes=[
                pltpu.VMEM((n_dp, width, TILE), jnp.float32),
                pltpu.VMEM((2, TILE, D), jnp.bfloat16),
                pltpu.SemaphoreType.DMA((2,)),
            ],
            mib=20,
        )

    def per_device(
        cot_student, cot_fake, act_student, act_fake, weight_student, weight_fake,
        master_student, first_student, second_student, master_fake, first_fake, second_fake,
        timesteps,
    ):
        f, count = act_student.shape
        r = cot_student.shape[0]
        assert timesteps.shape[2] == 1 and count == ROWS

        token = []

        def step(work, *inputs):
            if token:
                *inputs, _ = lax.optimization_barrier((*inputs, token[0]))
            out = work(*inputs)
            token[:] = jax.tree.leaves(out)[:1]
            return out

        def reduced(combine, value, got):
            return step(lambda *values: functools.reduce(combine, values), value, *got)

        def hops(value, combine, *axes):
            for axis in axes:
                distance = 1
                while distance < mesh.shape[axis]:
                    perm = [(p, p ^ distance) for p in range(mesh.shape[axis])]
                    got = lax.ppermute(value, axis, perm)
                    yield
                    value = step(combine, value, got)
                    distance *= 2
            yield value

        scales = step(
            lambda steps: 1.0 / (0.1 + steps.astype(jnp.float32) / 1000.0), timesteps[0, :, 0]
        )
        top_act, scaled_own, *sent = step(lambda act: prepare_fake(act, scales, r), act_fake)
        acts = [from_tensor(value, -j) for j, value in enumerate(sent, 1)]
        scaled_fake = [[scaled_own, to_core(scaled_own)]]
        fake_blocks, top_fake = step(lambda cot: turn(cot, False), cot_fake)
        mate_blocks = to_core(fake_blocks[1])
        planes, top_student = step(lambda cot: turn(cot, True), cot_student)

        same, diagonal = [], []

        def send_planes(g, own, other):
            same.append([from_tensor(own, j) for j in range(1, n_tensor)])
            diagonal.append([from_diagonal(other, j) for j in range(1, n_tensor)])

        tops, scaled_student = step(
            lambda *values: prepare_student(*values, scales, r),
            act_student, top_student, top_fake, top_act,
        )
        tops = hops(tops, jnp.maximum, "dp")
        next(tops)
        send_planes(0, planes[0], planes[1])
        parts_fake = []

        def multiply_fake(j):
            parts_fake.append(
                step(
                    lambda a, b, c, d: multiply([a, b], [c, d], [(0, 0), (1, 0)]),
                    fake_blocks[0], mate_blocks, *scaled_fake[j],
                )
            )

        multiply_fake(0)
        next(tops)
        next(tops)
        next(tops)
        acts = step(lambda *values: values, *acts)
        scaled_fake += [[act, to_core(act)] for act in acts]
        while (tops_own := next(tops)) is None:
            pass

        def factor(tops, net):
            bound = jnp.maximum(tops[2 * net, 0] * tops[2 * net + 1, 0], 1e-30)
            bound = bound * (1.01 * count * n_dp / HALF_LIMIT)
            return bound, 1.0 / bound

        factors = {"own": step(lambda tops: factor(tops, 1), tops_own)}

        def shrink(value, net):
            return (value * factors[net][1]).astype(jnp.float16)

        def widen(value, net):
            return value.astype(jnp.float32) * factors[net][0]

        def add_widened(total, values, net):
            for value in values:
                total = total + widen(value, net)
            return total

        fake_own, fake_got = {}, {}

        def which(j):
            return 1 if j else "own"

        def fake_middle(j):
            def work(both):
                sent = [shrink(both[i], which(j)) for i in range(1, inner)]
                return sent, both[0]

            sent, fake_own[j] = step(work, parts_fake[j])
            fake_got[j] = [to_middle(value, i) for i, value in enumerate(sent, 1)]

        def fake_near(j):
            def work(own, *got):
                own = add_widened(own, got, which(j))
                return shrink(own[1::2], which(j)), own[0::2]

            sent, fake_own[j] = step(work, fake_own[j], *fake_got[j])
            fake_got[j] = [to_plane(sent, 1)]

        def fake_far(j):
            def work(own, *got):
                own = add_widened(own, got, which(j))
                return shrink(own[1], which(j)), own[0]

            sent, fake_own[j] = step(work, fake_own[j], *fake_got[j])
            fake_got[j] = [to_plane(sent, 2)]

        def fake_total(j):
            return step(
                lambda own, *got: add_widened(own, got, which(j)), fake_own[j], *fake_got[j]
            )

        fake_middle(0)
        for j in range(1, n_tensor):
            multiply_fake(j)
        mate_student = to_core(scaled_student)
        mate_planes = [to_core(planes[1]), to_core(planes[3])]
        tops = hops(tops_own, jnp.maximum, "tensor")
        next(tops)
        mate_student, *mate_planes = step(lambda *values: values, mate_student, *mate_planes)

        def back(whole, net, pieces, j, low, size):
            weight = (weight_student, weight_fake)[net]
            has = [] if whole is None else [whole]

            def work(weight, *values):
                return back_part(
                    values[-1] if has else None, weight, values[: len(pieces)], scales,
                    net, j, low, size, r, count,
                )

            return step(work, weight, *pieces, *has)

        def multiply_student(g):
            pieces, places = [planes[2 * g], mate_planes[g]], [(0, 0), (1, 0)]
            for j in range(1, n_tensor):
                pieces += [same[g][j - 1], diagonal[g][j - 1]]
                places += [(0, j), (1, j)]
            return step(
                lambda *values: multiply(values[:-2], values[-2:], places),
                *pieces, scaled_student, mate_student,
            )

        back_student = back(None, 0, [cot_student], 0, 0, r)
        send_planes(1, *step(lambda a, b: (a, b), planes[2], planes[3]))
        back_fake = back(None, 1, [cot_fake], 0, 0, r)
        while (tops_all := next(tops)) is None:
            pass
        factors[0], factors[1] = step(lambda tops: (factor(tops, 0), factor(tops, 1)), tops_all)
        for j in range(1, n_tensor):
            fake_middle(j)
        both = multiply_student(0)

        def first_middle(both):
            return [shrink(both[:, i], 0) for i in range(1, inner)], both[:, 0]

        sent, own = step(first_middle, both)
        got = [to_middle(value, i) for i, value in enumerate(sent, 1)]
        for j in range(n_tensor):
            fake_near(j)

        def first_planes(own, *got):
            return shrink(add_widened(own, got, 0), 0)

        near = to_plane(step(first_planes, own, *got), 1)
        fake_far(0)
        both = multiply_student(1)

        def second_middle(both):
            sent = [[shrink(both[n, i], 0) for i in range(1, inner)] for n in range(2)]
            return sent, both[0, 0], both[1, 0]

        sent, own_far, own = step(second_middle, both)
        got_far, got = (
            [to_middle(value, i) for i, value in enumerate(values, 1)] for values in sent
        )
        for j in range(1, n_tensor):
            fake_far(j)

        def far_plane(own, near, *got):
            return shrink(add_widened(own, (near[1], *got), 0), 0)

        far = to_plane(step(far_plane, own_far, near, *got_far), 2)
        fake_others = [fake_total(j) for j in range(1, n_tensor)]
        others_got = [from_tensor(value, j) for j, value in enumerate(fake_others, 1)]
        fake_mine = fake_total(0)
        total_student = step(
            lambda own, near, *got: add_widened(own, (near[0], *got), 0), own, near, *got
        )
        total_fake = reduced(jnp.add, fake_mine, others_got)
        total_student = step(
            lambda own, got: add_widened(own, (got,), 0), total_student, far
        )
        squares = step(norms, total_student, total_fake)
        squares = reduced(
            jnp.add, squares, [from_tensor(squares, j) for j in range(1, n_tensor)]
        )

        rows = step(lambda cot: cot, cot_fake)
        raw = [from_tensor(rows, j) for j in range(1, n_tensor)]

        got = [to_plane(squares, k) for k in range(1, OUTER)]
        squares = reduced(jnp.add, squares, got)
        got = [
            move_dp(squares, lambda z, m, c, i=i, o=o: (z, (m + i) & (inner - 1), c ^ o))
            for i in range(inner)
            for o in range(2)
            if i or o
        ]
        squares = reduced(jnp.add, squares, got)
        states = (
            master_student, first_student, second_student, master_fake, first_fake, second_fake,
        )
        own, updated = step(
            lambda squares, *values: update(squares, values[:2], values[2:]),
            squares, total_student, total_fake, *(state.T for state in states),
        )

        mine = {}

        def spread_middle(k, value):
            mine[k] = [value] + [to_middle(value, -i) for i in range(1, inner)]

        spread_middle(0, own)
        far_got, near_got = to_plane(own, 2), to_plane(own, 1)
        spread_middle(1, step(lambda value: value, near_got))
        value = step(lambda value: value, far_got)
        spread_middle(2, value)
        passed_on = to_plane(value, 1)
        arrays = [step(lambda *values: jnp.stack(values), *mine[0], *mine[1])]
        arrays.append(to_core(arrays[0]))
        spread_middle(3, step(lambda value: value, passed_on))
        arrays.append(step(lambda *values: jnp.stack(values), *mine[2]))
        arrays.append(to_core(arrays[2]))
        hidden = step(lambda *values: values, *[value for group in diagonal for value in group])
        mate_others = [to_core(value) for value in hidden]
        mate_others = [mate_others[: n_tensor - 1], mate_others[n_tensor - 1 :]]
        for j in range(1, n_tensor):
            pieces = [
                piece for g in range(2) for piece in (same[g][j - 1], mate_others[g][j - 1])
            ]
            back_student = back(back_student, 0, pieces, j, 0, r)
        for j in range(1, n_tensor):
            back_fake = back(back_fake, 1, [raw[j - 1]], j, 0, r)
        mine[3] = step(lambda *values: values, *mine[3])
        blocks = {}
        for other in range(2):
            for i in range(inner):
                for k in range(2):
                    blocks[k, i, other] = other, k * inner + i
                blocks[2, i, other] = 2 + other, i
        for i, value in enumerate(mine[3]):
            blocks[3, i, 0], blocks[3, i, 1] = (len(arrays), None), (len(arrays) + 1, None)
            arrays += [value, to_core(value)]
        params = step(lambda *values: spread(blocks, *values), *arrays)

        new_states = [value.T for value in updated]
        return (back_student, back_fake, *new_states, *params)

    placed = (
        P(("dp", "tensor"), None),
        P(("dp", "tensor"), None),
        P("tensor", "dp"),
        P("tensor", "dp"),
        P("tensor", None),
        P("tensor", None),
        P("tensor", "dp"),
        P("tensor", "dp"),
        P("tensor", "dp"),
        P("tensor", "dp"),
        P("tensor", "dp"),
        P("tensor", "dp"),
        P("dp", None, None),
    )
    return jax.shard_map(
        per_device,
        mesh=mesh,
        in_specs=placed,
        out_specs=(
            P("tensor", "dp"),
            P("tensor", "dp"),
            P("tensor", "dp"),
            P("tensor", "dp"),
            P("tensor", "dp"),
            P("tensor", "dp"),
            P("tensor", "dp"),
            P("tensor", "dp"),
            P("tensor", None),
            P("tensor", None),
        ),
        check_vma=False,
    )
```

```python
import functools

import jax
import jax.numpy as jnp
from jax import lax
from jax.experimental import pallas as pl
from jax.experimental.pallas import tpu as pltpu
from jax.sharding import PartitionSpec as P

D = 2432
F = 1216
ROWS = 1024


FIRST_CORRECTION = 0.9999734386011124
SECOND_CORRECTION = 0.0952078529183

OUTER = 4
HALF_LIMIT = 60000.0
TILE = 256
LANES = 128

NT = (((1,), (1,)), ((), ()))
NN = (((1,), (0,)), ((), ()))

SMEM = pl.BlockSpec(memory_space=pltpu.SMEM)
VMEM = pl.BlockSpec(memory_space=pltpu.VMEM)
ANY = pl.BlockSpec(memory_space=pl.ANY)


def adam_update(grad, squares, master, first, second):
    clip = jnp.minimum(1.0, jnp.sqrt(jnp.float32(D * F)) / jnp.sqrt(squares + 1e-06))
    clipped = grad * clip
    new_first = 0.9 * first + 0.1 * clipped
    new_second = 0.999 * second + 0.001 * clipped * clipped
    step_dir = new_first / FIRST_CORRECTION / (jnp.sqrt(new_second / SECOND_CORRECTION) + 1e-08)
    new_master = master * (1.0 - 0.01 * 0.01) - 0.01 * step_dir
    return (new_master, new_first, new_second)


def dot(a, b, dims):
    return lax.dot_general(a, b, dims, preferred_element_type=jnp.float32)


def identity(size):
    rows = lax.broadcasted_iota(jnp.int32, (size, size), 0)
    cols = lax.broadcasted_iota(jnp.int32, (size, size), 1)
    return jnp.where(rows == cols, 1.0, 0.0).astype(jnp.bfloat16)


def array(shape, dtype):
    return jax.ShapeDtypeStruct(shape, dtype)


def call(kernel, out_shape, *operands, mib=12, **kwargs):
    return pl.pallas_call(
        kernel,
        out_shape=out_shape,
        compiler_params=pltpu.CompilerParams(vmem_limit_bytes=mib * 1024 * 1024),
        cost_estimate=pl.CostEstimate(flops=0, bytes_accessed=0, transcendentals=0),
        **kwargs,
    )(*operands)


def solution(mesh):
    n_dp, n_tensor = mesh.shape["dp"], mesh.shape["tensor"]
    inner = n_dp // (2 * OUTER)
    width = D // n_dp

    def split(p):
        return (p >> inner.bit_length()) & (OUTER - 1), (p >> 1) & (inner - 1), p & 1

    def join(z, m, c):
        return (z * inner + m) * 2 + c

    def move_dp(value, where):
        perm = [(p, join(*where(*split(p)))) for p in range(n_dp)]
        return lax.ppermute(value, "dp", perm)

    def to_plane(value, k):
        return move_dp(value, lambda z, m, c: (z ^ k, m, c))

    def to_middle(value, k):
        return move_dp(value, lambda z, m, c: (z, (m + k) & (inner - 1), c))

    def to_core(value):
        return move_dp(value, lambda z, m, c: (z, m, 1 - c))

    def from_tensor(value, k):
        perm = [(s, (s - k) & (n_tensor - 1)) for s in range(n_tensor)]
        return lax.ppermute(value, "tensor", perm)

    def from_diagonal(value, k):
        perm = []
        for p in range(n_dp):
            z, m, c = split(p)
            for t in range(n_tensor):
                target = join(z, m, 1 - c) * n_tensor + ((t - k) & (n_tensor - 1))
                perm.append((p * n_tensor + t, target))
        return lax.ppermute(value, ("dp", "tensor"), perm)

    def my_place():
        return split(lax.axis_index("dp"))

    def relative(p):
        z, m, c = split(p)
        my_z, my_m, my_c = my_place()
        return z ^ my_z, (m - my_m) & (inner - 1), c ^ my_c

    def owner(k, i, other):
        z, m, c = my_place()
        return join(z ^ k, (m + i) & (inner - 1), c ^ other)

    def first_row(j, r):
        start = ((lax.axis_index("tensor") + j) & (n_tensor - 1)) * r
        return pl.multiple_of(start, LANES)

    def turn(cot, by_planes):
        r = cot.shape[0]
        step = min(r, TILE)
        count = 4 if by_planes else 2
        lead = (2, inner) if by_planes else (inner, OUTER)

        def kernel(cot_ref, *refs):
            out_refs, (top_ref, wide_ref) = refs[:count], refs[count:]
            eye = identity(TILE)
            for start in range(0, D, TILE):
                size = min(TILE, D - start)
                wide_ref[start : start + size, :] = dot(
                    eye[:size, :size], cot_ref[:, start : start + size], NT
                )
            top = jnp.max(jnp.abs(wide_ref[...]).reshape(D // 8, 8, step), axis=0)
            top = jnp.broadcast_to(jnp.max(top), (8, LANES))

            @pl.when(pl.program_id(0) == 0)
            def _():
                top_ref[...] = top

            @pl.when(pl.program_id(0) > 0)
            def _():
                top_ref[...] = jnp.maximum(top_ref[...], top)

            for p in range(n_dp):
                k, i, other = relative(p)
                block = wide_ref[p * width : (p + 1) * width, :].astype(jnp.bfloat16)
                which, at = other, (i, k)
                if by_planes:
                    even = 1 - (k & 1)
                    which, at = 2 * even + other, ((k >> 1) ^ even, i)
                for n in range(count):

                    @pl.when(which == n)
                    def _(n=n, at=at, block=block):
                        out_refs[n][at] = block

        *outs, top = call(
            kernel,
            [array((*lead, width, r), jnp.bfloat16)] * count + [array((8, LANES), jnp.float32)],
            cot,
            grid=(r // step,),
            in_specs=[pl.BlockSpec((step, D), lambda s: (s, 0))],
            out_specs=[
                pl.BlockSpec((*lead, width, step), lambda s: (*(0 for _ in lead), 0, s))
            ] * count
            + [pl.BlockSpec((8, LANES), lambda s: (0, 0))],
            scratch_shapes=[pltpu.VMEM((D, step), jnp.float32)],
        )
        return outs, top

    def prepare_fake(act, scales, r):
        f = act.shape[0]

        def kernel(scale_ref, act_ref, top_ref, *out_refs):
            most = jnp.max(jnp.abs(act_ref[...].astype(jnp.float32)))
            top_ref[...] = jnp.full((8, LANES), most * scale_ref[1])
            for j, out_ref in enumerate(out_refs):
                part = act_ref[:, pl.ds(first_row(j, r), r)].astype(jnp.float32)
                out_ref[0] = (part * scale_ref[1]).astype(jnp.bfloat16)

        return call(
            kernel,
            [array((8, LANES), jnp.float32)] + [array((1, f, r), jnp.bfloat16)] * n_tensor,
            scales, act,
            in_specs=[SMEM, VMEM], out_specs=[VMEM] * (1 + n_tensor),
        )

    def prepare_student(act, top_s, top_f, top_act_f, scales, r):
        f = act.shape[0]

        def kernel(scale_ref, act_ref, top_s_ref, top_f_ref, top_act_f_ref, top_ref, out_ref):
            most = jnp.max(jnp.abs(act_ref[...].astype(jnp.float32)))
            most = jnp.full((8, LANES), most * scale_ref[0])
            rows = lax.broadcasted_iota(jnp.int32, (8, LANES), 0)
            tops = jnp.where(rows == 0, top_s_ref[...], most)
            tops = jnp.where(rows == 2, top_f_ref[...], tops)
            top_ref[...] = jnp.where(rows == 3, top_act_f_ref[...], tops)
            for j in range(n_tensor):
                part = act_ref[:, pl.ds(first_row(j, r), r)].astype(jnp.float32)
                out_ref[j] = (part * scale_ref[0]).astype(jnp.bfloat16)

        return call(
            kernel,
            [array((8, LANES), jnp.float32), array((n_tensor, f, r), jnp.bfloat16)],
            scales, act, top_s, top_f, top_act_f,
            in_specs=[SMEM] + [VMEM] * 4, out_specs=[VMEM] * 2,
        )

    def multiply(pieces, scaled, places):
        lead, r, f = pieces[0].shape[:-1], pieces[0].shape[-1], scaled[0].shape[1]
        pieces = [piece.reshape(-1, r) for piece in pieces]
        rows = pieces[0].shape[0]
        step = D // (2 * OUTER)
        count = len(pieces)

        def kernel(*refs):
            piece_refs, scaled_refs, out_ref = refs[:count], refs[count:-1], refs[-1]
            for start in range(0, rows, step):
                part = slice(start, start + step)
                total = None
                for piece_ref, (n, j) in zip(piece_refs, places):
                    term = dot(piece_ref[part], scaled_refs[n][j], NT)
                    total = term if total is None else total + term
                out_ref[part] = total

        out = call(
            kernel, array((rows, f), jnp.float32), *pieces, *scaled,
            in_specs=[VMEM] * (count + len(scaled)), out_specs=VMEM,
        )
        return out.reshape(*lead, f)

    def norms(total_s, total_f):
        def kernel(s_ref, f_ref, out_ref):
            sums = [jnp.sum(ref[...] * ref[...]) for ref in (s_ref, f_ref)]
            rows = lax.broadcasted_iota(jnp.int32, (8, LANES), 0)
            out_ref[...] = jnp.where(rows == 0, *sums)

        return call(
            kernel, array((8, LANES), jnp.float32), total_s, total_f,
            in_specs=[VMEM] * 2, out_specs=VMEM,
        )

    def update(squares, totals, states):
        shape = totals[0].shape

        def kernel(squares_ref, *refs):
            total_refs, state_refs, (own_ref, *out_refs) = refs[:2], refs[2:8], refs[8:]
            for net in range(2):
                new = adam_update(
                    total_refs[net][...],
                    squares_ref[net : net + 1, :1],
                    *(ref[...] for ref in state_refs[3 * net : 3 * net + 3]),
                )
                own_ref[net] = new[0].astype(jnp.bfloat16)
                for ref, value in zip(out_refs[3 * net :], new):
                    ref[...] = value

        own, *new = call(
            kernel,
            [array((2, *shape), jnp.bfloat16)] + [array(shape, jnp.float32)] * 6,
            squares, *totals, *states,
            in_specs=[VMEM] * 9,
            out_specs=[VMEM] * 7,
        )
        return own, new

    def back_part(whole, weight, pieces, scales, net, j, low, size, r, count):
        f = weight.shape[0]
        turned = len(pieces) > 1

        def kernel(scale_ref, weight_ref, *refs):
            piece_refs = refs[: len(pieces)]
            if turned:
                out_ref, done_ref, sem, wide_ref = refs[-4:]
                for k in range(OUTER):
                    for other in range(2):
                        for i in range(inner):
                            even = 1 - (k & 1)
                            block = piece_refs[2 * even + other][(k >> 1) ^ even, i]
                            block = block.astype(jnp.float32)
                            wide_ref[owner(k, i, other)] = block
                flat = wide_ref[...].reshape(D, size).astype(jnp.bfloat16)
                product = dot(weight_ref[...], flat, NN)
            else:
                out_ref, done_ref, sem = refs[-3:]
                product = dot(weight_ref[...], piece_refs[0][...], NT)
            done_ref[...] = (product * scale_ref[net]).astype(jnp.bfloat16)
            start = pl.multiple_of(first_row(j, r) + low, LANES)
            copy = pltpu.make_async_copy(done_ref, out_ref.at[:, pl.ds(start, size)], sem)
            copy.start()
            copy.wait()

        scratch = [pltpu.VMEM((f, size), jnp.bfloat16), pltpu.SemaphoreType.DMA]
        if turned:
            scratch.append(pltpu.VMEM((n_dp, width, size), jnp.float32))
        operands = [scales, weight, *pieces]
        in_specs = [SMEM] + [VMEM] * (len(operands) - 1)
        aliases = {}
        if whole is not None:
            aliases = {len(operands): 0}
            operands.append(whole)
            in_specs.append(ANY)
        return call(
            kernel, array((f, count), jnp.bfloat16), *operands,
            in_specs=in_specs, out_specs=ANY, scratch_shapes=scratch,
            input_output_aliases=aliases, mib=16,
        )

    def spread(blocks, *arrays):
        f = arrays[0].shape[-1]
        tiles = [
            (net, start, min(TILE, f - start)) for net in range(2) for start in range(0, f, TILE)
        ]

        def kernel(*refs):
            array_refs, refs = refs[: len(arrays)], refs[len(arrays) :]
            out_refs, (wide_ref, done_ref, sem) = refs[:2], refs[2:]
            eye = identity(TILE)
            copies = []
            for step, (net, start, size) in enumerate(tiles):
                for (k, i, other), (n, at) in blocks.items():
                    ref = array_refs[n] if at is None else array_refs[n].at[at]
                    block = ref[net, :, start : start + size].astype(jnp.float32)
                    wide_ref[owner(k, i, other), :, :size] = block
                flat = wide_ref[:, :, :size].reshape(D, size).astype(jnp.bfloat16)
                slot = step & 1
                if step >= 2:
                    copies[step - 2].wait()
                done_ref[slot, :size, :] = dot(eye[:size, :size], flat, NT).astype(jnp.bfloat16)
                copy = pltpu.make_async_copy(
                    done_ref.at[slot, pl.ds(0, size)],
                    out_refs[net].at[pl.ds(start, size)],
                    sem.at[slot],
                )
                copy.start()
                copies.append(copy)
            for copy in copies[-2:]:
                copy.wait()

        return call(
            kernel, [array((f, D), jnp.bfloat16)] * 2, *arrays,
            in_specs=[VMEM] * len(arrays), out_specs=[ANY] * 2,
            scratch_shapes=[
                pltpu.VMEM((n_dp, width, TILE), jnp.float32),
                pltpu.VMEM((2, TILE, D), jnp.bfloat16),
                pltpu.SemaphoreType.DMA((2,)),
            ],
            mib=16,
        )

    def per_device(
        cot_student, cot_fake, act_student, act_fake, weight_student, weight_fake,
        master_student, first_student, second_student, master_fake, first_fake, second_fake,
        timesteps,
    ):
        f, count = act_student.shape
        r = cot_student.shape[0]
        assert timesteps.shape[2] == 1 and count == ROWS

        token = []

        def step(work, *inputs):
            if token:
                *inputs, _ = lax.optimization_barrier((*inputs, token[0]))
            out = work(*inputs)
            token[:] = jax.tree.leaves(out)[:1]
            return out

        def reduced(combine, value, got):
            return step(lambda *values: functools.reduce(combine, values), value, *got)

        def hops(value, combine, *axes):
            for axis in axes:
                distance = 1
                while distance < mesh.shape[axis]:
                    perm = [(p, p ^ distance) for p in range(mesh.shape[axis])]
                    got = lax.ppermute(value, axis, perm)
                    yield
                    value = step(combine, value, got)
                    distance *= 2
            yield value

        scales = step(
            lambda steps: 1.0 / (0.1 + steps.astype(jnp.float32) / 1000.0), timesteps[0, :, 0]
        )
        top_act, scaled_own, *sent = step(lambda act: prepare_fake(act, scales, r), act_fake)
        acts = [from_tensor(value, -j) for j, value in enumerate(sent, 1)]
        scaled_fake = [[scaled_own, to_core(scaled_own)]]
        fake_blocks, top_fake = step(lambda cot: turn(cot, False), cot_fake)
        mate_blocks = to_core(fake_blocks[1])
        planes, top_student = step(lambda cot: turn(cot, True), cot_student)

        same, diagonal = [], []

        def send_planes(g, own, other):
            same.append([from_tensor(own, j) for j in range(1, n_tensor)])
            diagonal.append([from_diagonal(other, j) for j in range(1, n_tensor)])

        tops, scaled_student = step(
            lambda *values: prepare_student(*values, scales, r),
            act_student, top_student, top_fake, top_act,
        )
        tops = hops(tops, jnp.maximum, "dp")
        next(tops)
        send_planes(0, planes[0], planes[1])
        parts_fake = []

        def multiply_fake(j):
            parts_fake.append(
                step(
                    lambda a, b, c, d: multiply([a, b], [c, d], [(0, 0), (1, 0)]),
                    fake_blocks[0], mate_blocks, *scaled_fake[j],
                )
            )

        multiply_fake(0)
        next(tops)
        next(tops)
        next(tops)
        acts = step(lambda *values: values, *acts)
        scaled_fake += [[act, to_core(act)] for act in acts]
        while (tops_own := next(tops)) is None:
            pass

        def factor(tops, net):
            bound = jnp.maximum(tops[2 * net, 0] * tops[2 * net + 1, 0], 1e-30)
            bound = bound * (1.01 * count * n_dp / HALF_LIMIT)
            return bound, 1.0 / bound

        factors = {"own": step(lambda tops: factor(tops, 1), tops_own)}

        def shrink(value, net):
            return (value * factors[net][1]).astype(jnp.float16)

        def widen(value, net):
            return value.astype(jnp.float32) * factors[net][0]

        def add_widened(total, values, net):
            for value in values:
                total = total + widen(value, net)
            return total

        fake_own, fake_got = {}, {}

        def which(j):
            return 1 if j else "own"

        def fake_middle(j):
            def work(both):
                sent = [shrink(both[i], which(j)) for i in range(1, inner)]
                return sent, both[0]

            sent, fake_own[j] = step(work, parts_fake[j])
            fake_got[j] = [to_middle(value, i) for i, value in enumerate(sent, 1)]

        def fake_near(j):
            def work(own, *got):
                own = add_widened(own, got, which(j))
                return shrink(own[1::2], which(j)), own[0::2]

            sent, fake_own[j] = step(work, fake_own[j], *fake_got[j])
            fake_got[j] = [to_plane(sent, 1)]

        def fake_far(j):
            def work(own, *got):
                own = add_widened(own, got, which(j))
                return shrink(own[1], which(j)), own[0]

            sent, fake_own[j] = step(work, fake_own[j], *fake_got[j])
            fake_got[j] = [to_plane(sent, 2)]

        def fake_total(j):
            return step(
                lambda own, *got: add_widened(own, got, which(j)), fake_own[j], *fake_got[j]
            )

        fake_middle(0)
        for j in range(1, n_tensor):
            multiply_fake(j)
        mate_student = to_core(scaled_student)
        mate_planes = [to_core(planes[1]), to_core(planes[3])]
        tops = hops(tops_own, jnp.maximum, "tensor")
        next(tops)
        mate_student, *mate_planes = step(lambda *values: values, mate_student, *mate_planes)

        def back(whole, net, pieces, j, low, size):
            weight = (weight_student, weight_fake)[net]
            has = [] if whole is None else [whole]

            def work(weight, *values):
                return back_part(
                    values[-1] if has else None, weight, values[: len(pieces)], scales,
                    net, j, low, size, r, count,
                )

            return step(work, weight, *pieces, *has)

        def multiply_student(g):
            pieces, places = [planes[2 * g], mate_planes[g]], [(0, 0), (1, 0)]
            for j in range(1, n_tensor):
                pieces += [same[g][j - 1], diagonal[g][j - 1]]
                places += [(0, j), (1, j)]
            return step(
                lambda *values: multiply(values[:-2], values[-2:], places),
                *pieces, scaled_student, mate_student,
            )

        back_student = back(None, 0, [cot_student], 0, 0, r)
        send_planes(1, *step(lambda a, b: (a, b), planes[2], planes[3]))
        back_fake = back(None, 1, [cot_fake], 0, 0, r)
        while (tops_all := next(tops)) is None:
            pass
        factors[0], factors[1] = step(lambda tops: (factor(tops, 0), factor(tops, 1)), tops_all)
        for j in range(1, n_tensor):
            fake_middle(j)
        both = multiply_student(0)

        def first_middle(both):
            return [shrink(both[:, i], 0) for i in range(1, inner)], both[:, 0]

        sent, own = step(first_middle, both)
        got = [to_middle(value, i) for i, value in enumerate(sent, 1)]
        for j in range(n_tensor):
            fake_near(j)

        def first_planes(own, *got):
            return shrink(add_widened(own, got, 0), 0)

        near = to_plane(step(first_planes, own, *got), 1)
        fake_far(0)
        both = multiply_student(1)

        def second_middle(both):
            sent = [[shrink(both[n, i], 0) for i in range(1, inner)] for n in range(2)]
            return sent, both[0, 0], both[1, 0]

        sent, own_far, own = step(second_middle, both)
        got_far, got = (
            [to_middle(value, i) for i, value in enumerate(values, 1)] for values in sent
        )
        for j in range(1, n_tensor):
            fake_far(j)
        fake_mine = fake_total(0)
        fake_others = [fake_total(j) for j in range(1, n_tensor)]
        others_got = [from_tensor(value, j) for j, value in enumerate(fake_others, 1)]

        def far_plane(own, near, *got):
            return shrink(add_widened(own, (near[1], *got), 0), 0)

        far = to_plane(step(far_plane, own_far, near, *got_far), 2)
        total_student = step(
            lambda own, near, *got: add_widened(own, (near[0], *got), 0), own, near, *got
        )
        total_fake = reduced(jnp.add, fake_mine, others_got)
        total_student = step(
            lambda own, got: add_widened(own, (got,), 0), total_student, far
        )
        squares = step(norms, total_student, total_fake)
        squares = reduced(
            jnp.add, squares, [from_tensor(squares, j) for j in range(1, n_tensor)]
        )

        rows = step(lambda cot: cot, cot_fake)
        raw = [from_tensor(rows, j) for j in range(1, n_tensor)]

        got = [to_plane(squares, k) for k in range(1, OUTER)]
        squares = reduced(jnp.add, squares, got)
        got = [
            move_dp(squares, lambda z, m, c, i=i, o=o: (z, (m + i) & (inner - 1), c ^ o))
            for i in range(inner)
            for o in range(2)
            if i or o
        ]
        squares = reduced(jnp.add, squares, got)
        states = (
            master_student, first_student, second_student, master_fake, first_fake, second_fake,
        )
        own, updated = step(
            lambda squares, *values: update(squares, values[:2], values[2:]),
            squares, total_student, total_fake, *(state.T for state in states),
        )

        mine = {}

        def spread_middle(k, value):
            mine[k] = [value] + [to_middle(value, -i) for i in range(1, inner)]

        spread_middle(0, own)
        far_got, near_got = to_plane(own, 2), to_plane(own, 1)
        spread_middle(1, step(lambda value: value, near_got))
        value = step(lambda value: value, far_got)
        spread_middle(2, value)
        passed_on = to_plane(value, 1)
        arrays = [step(lambda *values: jnp.stack(values), *mine[0], *mine[1])]
        arrays.append(to_core(arrays[0]))
        spread_middle(3, step(lambda value: value, passed_on))
        arrays.append(step(lambda *values: jnp.stack(values), *mine[2]))
        arrays.append(to_core(arrays[2]))
        hidden = step(lambda *values: values, *[value for group in diagonal for value in group])
        mate_others = [to_core(value) for value in hidden]
        mate_others = [mate_others[: n_tensor - 1], mate_others[n_tensor - 1 :]]
        for j in range(1, n_tensor):
            pieces = [
                piece for g in range(2) for piece in (same[g][j - 1], mate_others[g][j - 1])
            ]
            back_student = back(back_student, 0, pieces, j, 0, r)
        for j in range(1, n_tensor):
            back_fake = back(back_fake, 1, [raw[j - 1]], j, 0, r)
        mine[3] = step(lambda *values: values, *mine[3])
        blocks = {}
        for other in range(2):
            for i in range(inner):
                for k in range(2):
                    blocks[k, i, other] = other, k * inner + i
                blocks[2, i, other] = 2 + other, i
        for i, value in enumerate(mine[3]):
            blocks[3, i, 0], blocks[3, i, 1] = (len(arrays), None), (len(arrays) + 1, None)
            arrays += [value, to_core(value)]
        params = step(lambda *values: spread(blocks, *values), *arrays)

        new_states = [value.T for value in updated]
        return (back_student, back_fake, *new_states, *params)

    placed = (
        P(("dp", "tensor"), None),
        P(("dp", "tensor"), None),
        P("tensor", "dp"),
        P("tensor", "dp"),
        P("tensor", None),
        P("tensor", None),
        P("tensor", "dp"),
        P("tensor", "dp"),
        P("tensor", "dp"),
        P("tensor", "dp"),
        P("tensor", "dp"),
        P("tensor", "dp"),
        P("dp", None, None),
    )
    return jax.shard_map(
        per_device,
        mesh=mesh,
        in_specs=placed,
        out_specs=(
            P("tensor", "dp"),
            P("tensor", "dp"),
            P("tensor", "dp"),
            P("tensor", "dp"),
            P("tensor", "dp"),
            P("tensor", "dp"),
            P("tensor", "dp"),
            P("tensor", "dp"),
            P("tensor", None),
            P("tensor", None),
        ),
        check_vma=False,
    )
```
